32 devices in a mesh: dp: 8 (over z, y), rep: 4 (over x, core).
Axes of the slice: x: 2, y: 2, z: 4, core: 2. Of those that a mesh axis runs over, the one named last changes fastest.
Arguments:
- hop_features: float32 [4, 100, 49152], P(None, None, ('dp', 'rep')), may hold values from -50 to 50
- branch_weight: float32 [4, 100, 512], replicated, may hold values from -0.625 to 0.625
- branch_gain: float32 [2048], replicated, may hold values from 0.5 to 1.5
- branch_bias: float32 [2048], replicated, may hold values from -1.5 to 1.5
- first_slope: float32 [2048], replicated, may hold values from 0.05 to 0.45
- second_slope: float32 [2048], replicated, may hold values from 0.05 to 0.45
- mid_weight: float32 [2048, 512], replicated, may hold values from -0.125 to 0.125
- mid_gain: float32 [512], replicated, may hold values from 0.5 to 1.5
- mid_bias: float32 [512], replicated, may hold values from -1.5 to 1.5
- mid_slope: float32 [512], replicated, may hold values from 0.05 to 0.45
- out_weight: float32 [512, 47], replicated, may hold values from -0.375 to 0.375
- out_bias: float32 [47], replicated, may hold values from -2.5 to 2.5
- labels: int32 [49152], P(('dp', 'rep')), may hold values from 0 to 46
- valid_mask: int32 [49152], P(('dp', 'rep')), may hold values from 0 to 1
Outputs:
- logits: float32 [47, 49152], P(None, ('dp', 'rep'))
- mean_loss: float32 [], replicated
- feature_grad: float32 [4, 100, 49152], P(None, None, ('dp', 'rep'))
- branch_weight_grad: float32 [4, 100, 512], replicated
- branch_gain_grad: float32 [2048], replicated
- branch_bias_grad: float32 [2048], replicated
- first_slope_grad: float32 [2048], replicated
- second_slope_grad: float32 [2048], replicated
- mid_weight_grad: float32 [2048, 512], replicated
- mid_gain_grad: float32 [512], replicated
- mid_bias_grad: float32 [512], replicated
- mid_slope_grad: float32 [512], replicated
- out_weight_grad: float32 [512, 47], replicated
- out_bias_grad: float32 [47], replicated
The draws below stay inside these ranges and needn't reach their ends.
All inputs are finite; a program needn't handle non-finite values.
Results may differ from the reference program's by a relative error of at most 0.0003.
Values sent between devices are 32-bit elements; how exact they have to be, the bound alone decides.
No kernel may reach another device: no remote copies, remote signals or barrier semaphores. Data moves between devices by JAX's collectives and lax.ppermute only.
A program may use at most 128 MiB of HBM per device.

```python
import jax
import jax.numpy as jnp
from jax import lax

HOPS = 4
FEAT = 100
HID = 512
MIDW = 512
CLASSES = 47
NODE_DEV = 1536
CAT = 2048
NODES = 49152


def draw_hop_features(key, part):
    key = jax.random.fold_in(key, 11)
    subkeys = jax.random.split(key, 3)
    blocks = NODES // NODE_DEV
    node_scale = jnp.exp(jax.random.uniform(subkeys[0], (NODES,), minval=0.0, maxval=2.3)) / 3.0
    offsets = jnp.clip(0.5 * jax.random.normal(subkeys[1], (HOPS, FEAT, blocks)), -2.5, 2.5)
    offset_full = jnp.repeat(offsets, NODE_DEV, axis=2)
    noise_part = jnp.clip(jax.random.normal(subkeys[2], (HOPS, FEAT, NODES)), -5.0, 5.0)
    return (node_scale * (noise_part + offset_full)).astype(jnp.float32)


def draw_valid_mask(key, part):
    key = jax.random.fold_in(key, 23)
    blocks = NODES // NODE_DEV
    last_block = max(blocks - 1, 1)
    block_index = jnp.arange(NODES, dtype=jnp.int32) // NODE_DEV
    drawn = jax.random.randint(key, (NODES,), 0, 3 * last_block)
    return (drawn < last_block + 2 * block_index).astype(jnp.int32)


def place_ends(values, rng, least, top_value):
    longest = values.shape.index(max(values.shape))
    spots = []
    for shift in (0, 1):
        where = [jax.random.randint(jax.random.fold_in(rng, axis), (), 0, length) for axis, length in enumerate(values.shape)]
        where[longest] = (where[longest] + shift) % values.shape[longest]
        spots.append(tuple(where))
    return values.at[spots[0]].set(least).at[spots[1]].set(top_value)


def scatter_about(key, extent, scale, reach, kind=jnp.bfloat16):
    return jnp.clip(scale * jax.random.normal(key, extent, jnp.float32), -reach, reach).astype(kind)


def setup_inputs(seed: int = 0) -> dict:
    splits = jax.random.split(jax.random.key(seed), 15)
    return {
        "hop_features": draw_hop_features(jax.random.fold_in(splits[14], 71), 0),
        "branch_weight": scatter_about(splits[1], (HOPS, FEAT, HID), FEAT ** -0.5, 0.625, jnp.float32),
        "branch_gain": jnp.clip(1.0 + 0.1 * jax.random.normal(splits[2], (CAT,), jnp.float32), 0.5, 1.5),
        "branch_bias": scatter_about(splits[3], (CAT,), 0.3, 1.5, jnp.float32),
        "first_slope": jnp.clip(jax.random.uniform(splits[4], (CAT,), jnp.float32, 0.05, 0.45), 0.05, 0.45),
        "second_slope": jnp.clip(jax.random.uniform(splits[5], (CAT,), jnp.float32, 0.05, 0.45), 0.05, 0.45),
        "mid_weight": scatter_about(splits[6], (CAT, MIDW), CAT ** -0.5, 0.125, jnp.float32),
        "mid_gain": jnp.clip(1.0 + 0.1 * jax.random.normal(splits[7], (MIDW,), jnp.float32), 0.5, 1.5),
        "mid_bias": scatter_about(splits[8], (MIDW,), 0.3, 1.5, jnp.float32),
        "mid_slope": jnp.clip(jax.random.uniform(splits[9], (MIDW,), jnp.float32, 0.05, 0.45), 0.05, 0.45),
        "out_weight": scatter_about(splits[10], (MIDW, CLASSES), (MIDW // 2) ** -0.5, 0.375, jnp.float32),
        "out_bias": scatter_about(splits[11], (CLASSES,), 0.5, 2.5, jnp.float32),
        "labels": place_ends(jax.random.randint(splits[12], (NODES,), 0, CLASSES), jax.random.fold_in(splits[12], 1), 0, CLASSES - 1).astype(jnp.int32),
        "valid_mask": draw_valid_mask(jax.random.fold_in(splits[14], 71), 0),
    }


epsilon = 1e-05
precise = lax.Precision.HIGHEST

@jax.custom_vjp
def low(v):
    return lax.optimization_barrier(v.astype(jnp.bfloat16)).astype(jnp.float32)

@jax.custom_vjp
def low_back(v):
    return v

def low_keep(v):
    return (low(v), None)

def low_pass(kept, grad):
    return (grad,)

def back_keep(v):
    return (v, None)

def back_low(kept, grad):
    return (low(grad),)
low.defvjp(low_keep, low_pass)
low_back.defvjp(back_keep, back_low)

def smooth_prelu(values, slopes):
    return slopes * values + (1.0 - slopes) * jax.nn.silu(values)

def batch_norm(inputs, node_weight, counted, gains, biases):
    average = lax.optimization_barrier(jnp.sum(node_weight * inputs, axis=0)) / counted
    center = inputs - average
    variance = lax.optimization_barrier(jnp.sum(node_weight * center * center, axis=0)) / counted
    return gains * center * lax.rsqrt(variance + epsilon) + biases

def reference(hop_features, branch_weight, branch_gain, branch_bias, first_slope, second_slope, mid_weight, mid_gain, mid_bias, mid_slope, out_weight, out_bias, labels, valid_mask):
    keep_float = valid_mask.astype(jnp.float32)
    counted = jnp.sum(keep_float)
    node_weight = keep_float[:, None]
    onehot = (jnp.arange(out_weight.shape[1], dtype=jnp.int32)[:, None] == labels[None, :]).astype(jnp.float32)
    target_mask = onehot * keep_float[None, :]
    node_total = hop_features.shape[2]

    def forward(features, weights_branch, gains_branch, biases_branch, slopes_first, slopes_second, weights_mid, gains_mid, biases_mid, slopes_mid, weights_out, biases_out):
        first_pre = jnp.einsum('hfn,hfc->nhc', features, weights_branch, precision=precise).reshape(node_total, -1)
        first_out = batch_norm(first_pre, node_weight, counted, gains_branch, biases_branch)
        second_act = smooth_prelu(smooth_prelu(first_out, slopes_first), slopes_second)
        mid_pre = jnp.dot(second_act, weights_mid, precision=precise, preferred_element_type=jnp.float32)
        mid_act = smooth_prelu(batch_norm(mid_pre, node_weight, counted, gains_mid, biases_mid), slopes_mid)
        scores = lax.dot_general(weights_out, mid_act, (((0,), (1,)), ((), ())), precision=precise) + biases_out[:, None]
        log_probs = jax.nn.log_softmax(scores, axis=0)
        return (-jnp.sum(target_mask * log_probs), scores)
    total, backward, logits = jax.vjp(forward, hop_features, branch_weight, branch_gain, branch_bias, first_slope, second_slope, mid_weight, mid_gain, mid_bias, mid_slope, out_weight, out_bias, has_aux=True)
    grads = backward(jnp.ones_like(total))
    return (logits, total / counted, grads[0], grads[1], grads[2], grads[3], grads[4], grads[5], grads[6], grads[7], grads[8], grads[9], grads[10], grads[11])
```

```python
import math

import jax
import jax.numpy as jnp
from jax import lax
from jax.sharding import PartitionSpec as P

epsilon = 1e-05
precise = lax.Precision.HIGH
axes = ("dp", "rep")


def gather_all(row, devices):
    return lax.all_to_all(
        jnp.broadcast_to(row[None], (devices,) + row.shape), axes, 0, 0, tiled=True
    )


def exchange(values, bit, devices):
    return lax.ppermute(values, axes, [(i, i ^ (1 << bit)) for i in range(devices)])


def big_sum(values, devices):
    bits = int(math.log2(devices))
    me = lax.axis_index(axes)
    rows = values.shape[0]
    for bit in range(bits):
        half = values.shape[0] // 2
        mine = (me >> bit) & 1
        keep = lax.dynamic_slice_in_dim(values, mine * half, half)
        send = lax.dynamic_slice_in_dim(values, (1 - mine) * half, half)
        values = keep + exchange(send, bit, devices)
    for bit in reversed(range(bits)):
        mine = (me >> bit) & 1
        other = exchange(values, bit, devices)
        values = jnp.where(
            mine == 0, jnp.concatenate([values, other]), jnp.concatenate([other, values])
        )
    return values


def smooth_prelu(values, slopes):
    return slopes * values + (1.0 - slopes) * jax.nn.silu(values)


def prelu_slope(values, slopes):
    sigmoid_values = jax.nn.sigmoid(values)
    return slopes + (1.0 - slopes) * sigmoid_values * (1.0 + values * (1.0 - sigmoid_values))


def moments(inputs, node_weight, local_count, devices):
    safe = jnp.maximum(local_count, 1.0)
    local_mean = jnp.sum(node_weight * inputs, axis=0) / safe
    center = inputs - local_mean
    local_square = jnp.sum(node_weight * center * center, axis=0)
    row = jnp.concatenate([local_mean, local_square, jnp.full((128,), local_count)])
    gathered = gather_all(row, devices)
    width = inputs.shape[1]
    means, squares, counts = (
        gathered[:, :width],
        gathered[:, width : 2 * width],
        gathered[:, 2 * width : 2 * width + 1],
    )
    counted = jnp.sum(counts)
    average = jnp.sum(counts * means, axis=0) / counted
    variance = jnp.sum(squares + counts * jnp.square(means - average), axis=0) / counted
    return (average, lax.rsqrt(variance + epsilon), counted)


def norm_back(upstream, normed, inverse, gains, node_weight, counted, devices):
    width = upstream.shape[1]
    row = jnp.concatenate([jnp.sum(upstream, axis=0), jnp.sum(upstream * normed, axis=0)])
    total = jnp.sum(gather_all(row, devices), axis=0)
    bias_grad, gain_grad = (total[:width], total[width:])
    inner = upstream - bias_grad / counted - normed * (gain_grad / counted)
    return (node_weight * (gains * inverse) * inner, gain_grad, bias_grad)


def on_device(
    devices,
    hop_features,
    branch_weight,
    branch_gain,
    branch_bias,
    first_slope,
    second_slope,
    mid_weight,
    mid_gain,
    mid_bias,
    mid_slope,
    out_weight,
    out_bias,
    labels,
    valid_mask,
):
    node_rows = hop_features.shape[2]
    keep_float = valid_mask.astype(jnp.float32)
    node_weight = keep_float[:, None]
    local_count = jnp.sum(keep_float)
    first_pre = jnp.einsum("hfn,hfc->nhc", hop_features, branch_weight, precision=precise).reshape(
        node_rows, -1
    )
    first_mean, first_inverse, counted = moments(first_pre, node_weight, local_count, devices)
    first_normed = (first_pre - first_mean) * first_inverse
    first_out = branch_gain * first_normed + branch_bias
    first_act = smooth_prelu(first_out, first_slope)
    second_act = smooth_prelu(first_act, second_slope)
    mid_pre = jnp.dot(second_act, mid_weight, precision=precise, preferred_element_type=jnp.float32)
    mid_mean, mid_inverse, _ = moments(mid_pre, node_weight, local_count, devices)
    mid_normed = (mid_pre - mid_mean) * mid_inverse
    mid_out = mid_gain * mid_normed + mid_bias
    mid_act = smooth_prelu(mid_out, mid_slope)
    logits = (
        lax.dot_general(out_weight, mid_act, (((0,), (1,)), ((), ())), precision=precise)
        + out_bias[:, None]
    )
    log_probs = jax.nn.log_softmax(logits, axis=0)
    onehot = (jnp.arange(logits.shape[0], dtype=jnp.int32)[:, None] == labels[None, :]).astype(
        jnp.float32
    )
    target_mask = onehot * keep_float[None, :]
    local_loss = -jnp.sum(target_mask * log_probs)
    logit_grad = keep_float[None, :] * jnp.exp(log_probs) - target_mask
    out_weight_grad = lax.dot_general(
        mid_act, logit_grad, (((0,), (1,)), ((), ())), precision=precise
    )
    out_bias_grad = jnp.sum(logit_grad, axis=1)
    mid_act_grad = lax.dot_general(
        logit_grad, out_weight, (((0,), (1,)), ((), ())), precision=precise
    )
    mid_slope_grad = jnp.sum(mid_act_grad * (mid_out - jax.nn.silu(mid_out)), axis=0)
    mid_out_grad = mid_act_grad * prelu_slope(mid_out, mid_slope)
    mid_pre_grad, mid_gain_grad, mid_bias_grad = norm_back(
        mid_out_grad, mid_normed, mid_inverse, mid_gain, node_weight, counted, devices
    )
    mid_weight_grad = lax.dot_general(
        second_act, mid_pre_grad, (((0,), (0,)), ((), ())), precision=precise
    )
    second_act_grad = lax.dot_general(
        mid_pre_grad, mid_weight, (((1,), (1,)), ((), ())), precision=precise
    )
    second_slope_grad = jnp.sum(second_act_grad * (first_act - jax.nn.silu(first_act)), axis=0)
    first_act_grad = second_act_grad * prelu_slope(first_act, second_slope)
    first_slope_grad = jnp.sum(first_act_grad * (first_out - jax.nn.silu(first_out)), axis=0)
    first_out_grad = first_act_grad * prelu_slope(first_out, first_slope)
    first_pre_grad, branch_gain_grad, branch_bias_grad = norm_back(
        first_out_grad, first_normed, first_inverse, branch_gain, node_weight, counted, devices
    )
    split_grad = first_pre_grad.reshape(node_rows, branch_weight.shape[0], -1)
    branch_weight_grad = jnp.einsum("hfn,nhc->hfc", hop_features, split_grad, precision=precise)
    feature_grad = jnp.einsum("hfc,nhc->hfn", branch_weight, split_grad, precision=precise)
    mid_weight_grad = big_sum(mid_weight_grad, devices)
    pieces = (
        branch_weight_grad,
        out_weight_grad,
        first_slope_grad,
        second_slope_grad,
        mid_slope_grad,
        out_bias_grad,
        local_loss,
    )
    flat = jnp.concatenate([piece.reshape(-1) for piece in pieces])
    unit = 1024 * devices
    total = -(-flat.shape[0] // unit) * unit
    flat = big_sum(jnp.pad(flat, (0, total - flat.shape[0])).reshape(-1, 128), devices).reshape(-1)
    summed = []
    start = 0
    for piece in pieces:
        summed.append(flat[start : start + piece.size].reshape(piece.shape))
        start += piece.size
    (
        branch_weight_grad,
        out_weight_grad,
        first_slope_grad,
        second_slope_grad,
        mid_slope_grad,
        out_bias_grad,
        local_loss,
    ) = summed
    mean_loss = local_loss / counted
    return (
        logits,
        mean_loss,
        feature_grad,
        branch_weight_grad,
        branch_gain_grad,
        branch_bias_grad,
        first_slope_grad,
        second_slope_grad,
        mid_weight_grad,
        mid_gain_grad,
        mid_bias_grad,
        mid_slope_grad,
        out_weight_grad,
        out_bias_grad,
    )


def solution(mesh):
    devices = mesh.shape["dp"] * mesh.shape["rep"]

    def body(*arrays):
        return on_device(devices, *arrays)

    nodes = P(("dp", "rep"))
    return jax.shard_map(
        body,
        mesh=mesh,
        in_specs=(P(None, None, ("dp", "rep")),) + (P(),) * 11 + (nodes, nodes),
        out_specs=(P(None, ("dp", "rep")), P(), P(None, None, ("dp", "rep"))) + (P(),) * 11,
        check_vma=False,
    )
```

```python
import functools

import jax
import jax.numpy as jnp
from jax import lax
from jax.experimental import pallas as pl
from jax.experimental.pallas import tpu as pltpu
from jax.sharding import PartitionSpec as P

epsilon = 1e-05
axes = ("dp", "rep")
exact = lax.Precision.HIGHEST
f32 = jnp.float32
bf16 = jnp.bfloat16
LANES = 128
CHUNK = 256
PIECES = 16
HOP_ROWS = 104
HEAD_ROWS = 56
CLASS_ROWS = 48
VMEM_LIMIT = 56 * 1024 * 1024


def dot(left, right, precision=None):
    return lax.dot_general(
        left, right, (((1,), (0,)), ((), ())), precision=precision, preferred_element_type=f32
    )


def dot_nt(left, right, precision=None):
    return lax.dot_general(
        left, right, (((1,), (1,)), ((), ())), precision=precision, preferred_element_type=f32
    )


def split(values):
    high = values.astype(bf16)
    return high, (values - high.astype(f32)).astype(bf16)


def as_column(row):
    return jnp.broadcast_to(row, (LANES, row.shape[1])).T


def wide(column, width):
    return jnp.concatenate([column] * (width // LANES), axis=1)


def fold(values):
    total = values[:, :LANES]
    for start in range(LANES, values.shape[1], LANES):
        total = total + values[:, start : start + LANES]
    return total


def total_row(partial):
    return jnp.sum(partial.T, axis=0, keepdims=True)


def pad_rows(values, rows):
    return jnp.concatenate(
        [values, jnp.zeros((rows - values.shape[0], values.shape[1]), values.dtype)], axis=0
    )


def weave(products, slabs):
    done = 0
    for j, product in enumerate(products):
        until = (j + 1) * len(slabs) // len(products)
        for slab in slabs[done:until]:
            slab()
        done = until
        product()


def cost(flops=0, bytes_accessed=0):
    return pl.CostEstimate(flops=flops, bytes_accessed=bytes_accessed, transcendentals=0)


def call(kernel, **options):
    return pl.pallas_call(
        kernel, compiler_params=pltpu.CompilerParams(vmem_limit_bytes=VMEM_LIMIT), **options
    )


def whole(*shape):
    return pl.BlockSpec(shape, lambda *_: (0,) * len(shape))


anywhere = pl.BlockSpec(memory_space=pl.ANY)


def stats_kernel(
    x_hbm, w_hbm, mask_ref,
    pay_ref, gram_ref, xcat_ref, w_ref,
    x_scr, row_ref, x_sem, w_sem,
):
    hops = w_ref.shape[0]
    feats = x_hbm.shape[0]
    x_in = [pltpu.make_async_copy(x_hbm.at[:, h, :], x_scr.at[h], x_sem.at[h]) for h in range(hops)]
    w_in = [pltpu.make_async_copy(w_hbm.at[:, h, :], w_ref.at[h], w_sem.at[h]) for h in range(hops)]
    for h in range(hops):
        x_in[h].start()
        w_in[h].start()
    keep = mask_ref[...].astype(f32)
    count = jnp.sum(keep, axis=1, keepdims=True)
    safe = jnp.maximum(count, 1.0)
    row_ref[...] = jnp.zeros_like(row_ref)
    for h in range(hops):
        x_in[h].wait()
        x = x_scr[h]
        mean = jnp.sum(x * keep, axis=1, keepdims=True) / safe
        high, low = split(pad_rows(x - mean, LANES))
        xcat_ref[h, :LANES, :] = high
        xcat_ref[h, LANES:, :] = low
        real = jnp.concatenate([high, low], axis=0) * keep.astype(bf16)
        gram = dot_nt(real, real)
        gram = (gram[:LANES, :LANES] + gram[LANES:, LANES:]) + (
            gram[:LANES, LANES:] + gram[LANES:, :LANES]
        )
        gram_ref[h] = gram
        w_in[h].wait()
        w = pad_rows(w_ref[h], LANES)
        square = jnp.sum(dot(gram, w, exact) * w, axis=0, keepdims=True)
        tiles = w.shape[1] // LANES
        for i in range(tiles):
            row_ref[h * 5 + i : h * 5 + i + 1, :] = square[:, i * LANES : (i + 1) * LANES]
        mean = pad_rows(jnp.broadcast_to(mean, (feats, LANES)), LANES).T
        row_ref[h * 5 + 4 : h * 5 + 5, :] = mean[:1]
        row_ref[h * 5 + 4 : h * 5 + 5, LANES - 1 :] = count
    pay_ref[...] = jnp.broadcast_to(row_ref[...][None], pay_ref.shape)


def real_nodes(pay_ref):
    return pay_ref[:, 4, LANES - 1 :]


def feature_shift(pay_ref, h):
    means = pay_ref[:, h * 5 + 4, :]
    counts = means[:, LANES - 1 :]
    total = jnp.sum(counts, axis=0, keepdims=True)
    return means - jnp.sum(counts * means, axis=0, keepdims=True) / total


def prepare_kernel(
    xcat_ref, w_ref, w2_ref, slope1_ref, slope2_ref, pre_ref, w2cat_ref, col_ref
):
    w = pad_rows(w_ref[0], LANES).T
    width = w.shape[0]
    high, low = split(w)
    wcat = jnp.concatenate(
        [jnp.concatenate([high, high], axis=1), jnp.concatenate([low, low], axis=1)], axis=0
    )
    nodes = xcat_ref.shape[2]
    for start in range(0, nodes, 2 * CHUNK):
        product = dot(wcat, xcat_ref[0, :, start : start + 2 * CHUNK])
        pre_ref[:, start : start + 2 * CHUNK] = product[:width] + product[width:]
    high, low = split(w2_ref[...].T)
    mid = low.shape[0]
    w2cat_ref[0, :, :width] = high
    w2cat_ref[0, :, width : 2 * width] = high
    w2cat_ref[0, :, 2 * width :] = low
    slope1, slope2 = as_column(slope1_ref[0]), as_column(slope2_ref[0])
    col_ref[0, 0] = 0.5 + 0.5 * slope1
    col_ref[0, 1] = 0.5 - 0.5 * slope1
    col_ref[0, 2] = 1.0 + slope2
    col_ref[0, 3] = 1.0 - slope2


def forward_kernel(
    code_ref, pay_ref, w_ref, gain_ref, bias_ref, pre_ref, col_ref, w2cat_ref, mask_ref,
    act_ref, mid_ref, stat_ref, inv_ref, norm_ref,
    acat_ref, shift_ref, row_ref,
):
    step = pl.program_id(0)
    hops = pl.num_programs(0) - 1
    width, nodes = pre_ref.shape

    def norm(h):
        means = pay_ref[:, pl.ds(h * 5 + 4, 1), :][:, 0, :]
        counts = means[:, LANES - 1 :]
        total = jnp.sum(counts, axis=0, keepdims=True)
        means = means - jnp.sum(counts * means, axis=0, keepdims=True) / total
        shift = dot(means, pad_rows(w_ref[0], LANES), exact)
        shift_ref[...] = shift
        squares = jnp.concatenate(
            [pay_ref[:, pl.ds(h * 5 + i, 1), :][:, 0, :] for i in range(width // LANES)], axis=1
        )
        square = jnp.sum(squares + counts * shift * shift, axis=0, keepdims=True)
        inverse = lax.rsqrt(square / total + epsilon)
        inv_ref[0] = inverse
        scale = 0.5 * gain_ref[0] * inverse
        norm_ref[0, 0] = as_column(scale)
        norm_ref[0, 1] = as_column(shift_ref[pl.ds(code_ref[0], 1), :] * scale + 0.5 * bias_ref[0])

    def slabs(place):
        rows = 16

        def slab(r):
            rs = slice(r, r + rows)
            scale, shift = wide(norm_ref[0, 0, rs], nodes), wide(norm_ref[0, 1, rs], nodes)
            p1, q1, p2, q2 = (wide(col_ref[0, i, rs], nodes) for i in range(4))
            half = pre_ref[rs, :] * scale + shift
            half = half * (p1 + q1 * jnp.tanh(half))
            act = half * (p2 + q2 * jnp.tanh(half))
            high, low = split(act)
            act_ref[0, rs, :] = high
            act_ref[1, rs, :] = low
            acat_ref[place, rs, :] = high
            acat_ref[place, slice(width + r, width + r + rows), :] = low

        return [functools.partial(slab, r) for r in range(0, width, rows)]

    def products(place, first):
        def product(start):
            cols = slice(start, start + CHUNK)
            high, low = acat_ref[place, :width, cols], acat_ref[place, width:, cols]
            value = dot(w2cat_ref[0], jnp.concatenate([high, low, high], axis=0))
            mid_ref[:, cols] = value if first else mid_ref[:, cols] + value

        return [functools.partial(product, start) for start in range(0, nodes, CHUNK)]

    @pl.when(step < hops)
    def _():
        norm(step)

    for h in range(5):

        @pl.when(step == h)
        def _():
            if h == 0:
                weave([lambda: None], slabs(0))
            elif h < 4:
                weave(products((h - 1) % 2, h == 1), slabs(h % 2))
            else:
                weave(products((h - 1) % 2, False), [])

    @pl.when(step == hops)
    def _():
        keep = mask_ref[...].astype(f32)
        count = jnp.maximum(jnp.sum(keep, axis=1, keepdims=True), 1.0)
        mid = mid_ref[...]
        average = total_row(fold(mid * keep)) / count
        off = mid - wide(as_column(average), nodes)
        square = total_row(fold(off * off * keep))
        put_rows(row_ref, average, square)
        stat_ref[...] = jnp.broadcast_to(row_ref[...][None], stat_ref.shape)


def put_rows(row_ref, *rows):
    at = 0
    for row in rows:
        for start in range(0, row.shape[1], LANES):
            row_ref[at : at + 1, :] = row[:, start : start + LANES]
            at += 1


def rows_of(ref, first, count):
    return jnp.concatenate([ref[:, i, :] for i in range(first, first + count)], axis=1)


def head_kernel(
    pay_ref, stat_ref, mid_ref, gain_ref, bias_ref, slope_ref, ow_ref, ob_ref, label_ref, mask_ref,
    logit_ref, up_ref, norm_ref, inv_ref, sums_ref, misc_ref,
    ow_scr, ob_scr, row_ref, half_ref, tan_ref, acat_ref, col_ref, back_ref, acc_ref, misc_scr,
):
    width, nodes = mid_ref.shape
    classes = ow_ref.shape[0]
    tiles = width // LANES
    counts = real_nodes(pay_ref)
    total = jnp.sum(counts, axis=0, keepdims=True)
    means = rows_of(stat_ref, 0, tiles)
    average = jnp.sum(counts * means, axis=0, keepdims=True) / total
    off = means - average
    square = jnp.sum(rows_of(stat_ref, tiles, tiles) + counts * off * off, axis=0, keepdims=True)
    inverse = lax.rsqrt(square / total + epsilon)
    inv_ref[...] = inverse
    col_ref[0] = as_column(average)
    col_ref[1] = as_column(inverse)
    col_ref[2] = 0.5 * as_column(gain_ref[...])
    col_ref[3] = 0.5 * as_column(bias_ref[...])
    slope = as_column(slope_ref[...])
    col_ref[4] = 0.5 + 0.5 * slope
    col_ref[5] = 0.5 - 0.5 * slope
    ow_scr[...] = jnp.zeros_like(ow_scr)
    ow_scr[:classes, :] = ow_ref[...]
    ow_t = split(ow_scr[:CLASS_ROWS, :])
    ow = split(ow_scr[...].T)
    ob_scr[...] = jnp.zeros_like(ob_scr)
    ob_scr[:, :classes] = ob_ref[...]
    ob_col = wide(as_column(ob_scr[...])[:CLASS_ROWS], nodes)
    rows = 16
    for r in range(0, width, rows):
        rs = slice(r, r + rows)
        mean, inv, gain, bias, p, q = (wide(col_ref[i, rs], nodes) for i in range(6))
        normed = (mid_ref[rs, :] - mean) * inv
        norm_ref[rs, :] = normed
        half = normed * gain + bias
        tangent = jnp.tanh(half)
        half_ref[rs, :] = half
        tan_ref[rs, :] = tangent
        high, low = split(2.0 * half * (p + q * tangent))
        acat_ref[rs, :] = high
        acat_ref[slice(width + r, width + r + rows), :] = low
    high, low = acat_ref[:width, :], acat_ref[width:, :]
    logits = dot(jnp.concatenate([ow_t[0], ow_t[0]], axis=1), acat_ref[...]) + dot(ow_t[1], high)
    logits = logits + ob_col
    logit_ref[...] = logits[:classes]
    keep = mask_ref[...].astype(f32)
    place = lax.broadcasted_iota(jnp.int32, (CLASS_ROWS, nodes), 0)
    logits = jnp.where(place < classes, logits, -3.0e38)
    shifted = logits - jnp.max(logits, axis=0, keepdims=True)
    weights = jnp.exp(shifted)
    norm = jnp.sum(weights, axis=0, keepdims=True)
    onehot = place == label_ref[...]
    picked = jnp.sum(jnp.where(onehot, shifted, 0.0), axis=0, keepdims=True)
    loss = jnp.sum(fold(keep * (jnp.log(norm) - picked)), axis=1, keepdims=True)
    grad = keep * (weights * (1.0 / norm) - jnp.where(onehot, 1.0, 0.0))
    grad_sum = fold(grad)
    grad_high, grad_low = split(pad_rows(grad, LANES))
    gcat = jnp.concatenate([grad_high, grad_low, grad_high], axis=0)
    owcat = jnp.concatenate([ow[0], ow[0], ow[1]], axis=1)

    def back(start):
        back_ref[:, start : start + CHUNK] = dot(owcat, gcat[:, start : start + CHUNK])

    for start in range(0, nodes, CHUNK):
        back(start)
    both = jnp.concatenate([grad_high, grad_low], axis=0)

    def weight_grad():
        value = dot_nt(both, high)
        value = value[:CLASS_ROWS] + value[LANES : LANES + CLASS_ROWS]
        misc_scr[:CLASS_ROWS, :] = value + dot_nt(grad_high[:CLASS_ROWS], low)

    def slab(r):
        rs = slice(r, r + rows)
        p, q = wide(col_ref[4, rs], nodes), wide(col_ref[5, rs], nodes)
        half, tangent, act_grad = half_ref[rs, :], tan_ref[rs, :], back_ref[rs, :]
        away = half * (1.0 - tangent)
        acc_ref[0, rs] = fold(act_grad * away)
        up = act_grad * (p + q * (tangent + away * (1.0 + tangent)))
        up_ref[rs, :] = up
        acc_ref[1, rs] = fold(up)
        acc_ref[2, rs] = fold(up * norm_ref[rs, :])

    slabs = [functools.partial(slab, r) for r in range(0, width, rows)]
    for one in slabs[:8]:
        one()
    weight_grad()
    for one in slabs[8:]:
        one()
    put_rows(row_ref, total_row(acc_ref[1]), total_row(acc_ref[2]))
    sums_ref[...] = jnp.broadcast_to(row_ref[...][None], sums_ref.shape)
    misc_scr[CLASS_ROWS:, :] = jnp.zeros((HEAD_ROWS - CLASS_ROWS, width), f32)
    misc_scr[CLASS_ROWS : CLASS_ROWS + 1, :] = total_row(acc_ref[0])
    misc_scr[CLASS_ROWS + 1 : CLASS_ROWS + 2, :LANES] = total_row(pad_rows(grad_sum, LANES))
    misc_scr[CLASS_ROWS + 2 : CLASS_ROWS + 3, :1] = loss
    for t in range(tiles):
        misc_ref[t] = misc_scr[:, t * LANES : (t + 1) * LANES]


def mid_grad_kernel(
    code_ref, pay_ref, sums_ref, inv_ref, gain_ref, up_ref, norm_ref, mask_ref, act_ref,
    out_ref, gcat_ref, bg_ref,
):
    step = pl.program_id(0)
    width, nodes = up_ref.shape
    tiles = width // LANES

    @pl.when(step == 0)
    def _():
        total = jnp.sum(real_nodes(pay_ref), axis=0, keepdims=True)
        bias_sum = jnp.sum(rows_of(sums_ref, 0, tiles), axis=0, keepdims=True)
        gain_sum = jnp.sum(rows_of(sums_ref, tiles, tiles), axis=0, keepdims=True)
        bg_ref[0:1, :] = bias_sum
        bg_ref[1:2, :] = gain_sum
        scale = as_column(gain_ref[...] * inv_ref[...])
        bias_col = as_column(bias_sum / total)
        gain_col = as_column(gain_sum / total)
        keep = mask_ref[...].astype(f32)
        rows = 16
        for r in range(0, width, rows):
            rs = slice(r, r + rows)
            bias, gain = wide(bias_col[rs], nodes), wide(gain_col[rs], nodes)
            grad = up_ref[rs, :] - bias - norm_ref[rs, :] * gain
            high, low = split(keep * (wide(scale[rs], nodes) * grad))
            gcat_ref[rs, :] = high
            gcat_ref[width + r : width + r + rows, :] = low
            gcat_ref[2 * width + r : 2 * width + r + rows, :] = high

    scatter(out_ref, code_ref[step], mid_product(act_ref, gcat_ref))


def mid_product(act_ref, gcat_ref):
    mid = gcat_ref.shape[0] // 3
    high, low = gcat_ref[:mid, :], gcat_ref[mid : 2 * mid, :]
    return dot_nt(act_ref[0], high) + dot_nt(act_ref[0], low) + dot_nt(act_ref[1], high)


def scatter(out_ref, code, values):
    rows = values.shape[0] // PIECES
    for i in range(PIECES):
        place = pl.multiple_of((i ^ (code & (PIECES - 1))) * rows, rows)
        out_ref[0, pl.ds(place, rows), :] = values[i * rows : (i + 1) * rows]


def mid_grad_rest_kernel(code_ref, act_ref, gcat_ref, out_ref):
    scatter(out_ref, code_ref[pl.program_id(0)], mid_product(act_ref, gcat_ref))


def backward_kernel(
    h, code_ref, pay_ref, inv_ref, gain_ref, bias_ref, w_ref, gram_ref, misc_ref,
    gcat_hbm, w2_hbm, pre_hbm, norm_hbm, col_hbm, xcat_hbm, *refs,
):
    (
        feat_hbm, pack_hbm,
        gcat, w2, pre, norm, col, xcat, down, ucat, acc, prod, rows_scr, pack, feat,
        in_sem, g_sem, z_sem, out_sem,
    ) = refs[-19:]
    width, nodes = pre.shape
    feats = w_ref.shape[1]
    mid = w2.shape[1]
    tiles = mid // LANES
    chunks = [slice(start, start + CHUNK) for start in range(0, nodes, CHUNK)]
    own = slice(h * width, (h + 1) * width)
    early = [
        pltpu.make_async_copy(w2_hbm.at[own, :], w2, in_sem.at[0]),
    ]
    late = [
        pltpu.make_async_copy(norm_hbm.at[h], norm, in_sem.at[1]),
        pltpu.make_async_copy(col_hbm.at[h], col, in_sem.at[2]),
        pltpu.make_async_copy(xcat_hbm.at[h], xcat, in_sem.at[3]),
    ]
    g_in = [
        pltpu.make_async_copy(gcat_hbm.at[:, c], gcat.at[:, c], g_sem.at[j])
        for j, c in enumerate(chunks)
    ]
    z_in = [
        pltpu.make_async_copy(pre_hbm.at[own, c], pre.at[:, c], z_sem.at[j])
        for j, c in enumerate(chunks)
    ]
    early[0].start()
    g_in[0].start()
    g_in[1].start()
    late[0].start()
    late[1].start()
    z_in[0].start()
    for j in range(2, len(chunks)):
        g_in[j].start()
        z_in[j - 1].start()
    z_in[-1].start()
    late[2].start()
    gain, bias, inverse = gain_ref[0], bias_ref[0], inv_ref[0]
    w = pad_rows(w_ref[0], LANES)
    whigh, wlow = split(w * (gain * inverse))
    wcat = jnp.concatenate([whigh, whigh, wlow], axis=1)
    acc[...] = jnp.zeros_like(acc)
    early[0].wait()
    high, low = split(0.5 * w2[...])
    w2cat = jnp.concatenate([high, high, low], axis=1)

    def down_product(j):
        g_in[j].wait()
        down[:, chunks[j]] = dot(w2cat, gcat[:, chunks[j]])

    def slab(j, r, rows):
        rs, cs = slice(r, r + rows), chunks[j]
        scale, shift = wide(norm[0, rs], CHUNK), wide(norm[1, rs], CHUNK)
        p1, q1, p2, q2 = (wide(col[i, rs], CHUNK) for i in range(4))
        half1 = pre[rs, cs] * scale + shift
        grad2 = down[rs, cs]
        tan1 = jnp.tanh(half1)
        half2 = half1 * (p1 + q1 * tan1)
        tan2 = jnp.tanh(half2)
        away2 = half2 * (1.0 - tan2)
        acc[0, rs] += fold(grad2 * away2)
        grad1 = grad2 * (p2 + q2 * (tan2 + away2 * (1.0 + tan2)))
        away1 = half1 * (1.0 - tan1)
        acc[1, rs] += fold(grad1 * away1)
        grad = grad1 * (p1 + q1 * (tan1 + away1 * (1.0 + tan1)))
        acc[2, rs] += fold(grad)
        acc[3, rs] += fold(grad * half1)
        high, low = split(grad)
        ucat[rs, cs] = high
        ucat[width + r : width + r + rows, cs] = low

    def feature_product(j):
        cs = chunks[j]
        high, low = ucat[:width, cs], ucat[width:, cs]
        feat[:, cs] = dot(wcat, jnp.concatenate([high, low, high], axis=0))[:feats]

    def weight_product(part):
        size = nodes // 2
        cs = slice(part * size, (part + 1) * size)
        value = dot_nt(xcat[:, cs], ucat[:width, cs])
        value = value[:LANES] + value[LANES:] + dot_nt(xcat[:LANES, cs], ucat[width:, cs])
        prod[...] = value if part == 0 else prod[...] + value

    rows = 64
    count = len(chunks)
    down_product(0)
    for copy in late:
        copy.wait()
    for j in range(count):
        products = []
        if j + 1 < count:
            products.append(functools.partial(down_product, j + 1))
        if j >= 1:
            products.append(functools.partial(feature_product, j - 1))
        if j == count // 2:
            products.append(functools.partial(weight_product, 0))
        z_in[j].wait()
        weave(products, [functools.partial(slab, j, r, rows) for r in range(0, width, rows)])
    feature_product(count - 1)
    feat_out = pltpu.make_async_copy(feat, feat_hbm.at[h], out_sem.at[4])
    feat_out.start()
    weight_product(1)
    bias_sum = total_row(acc[2])
    shift = feature_shift(pay_ref, h)
    counts = real_nodes(pay_ref)
    rows_scr[: shift.shape[0], :] = shift
    rows_scr[shift.shape[0] :, :] = jnp.broadcast_to(counts, shift.shape)
    me = code_ref[0]
    own_shift = rows_scr[pl.ds(me, 1), :]
    own_count = rows_scr[pl.ds(shift.shape[0] + me, 1), :]
    column = as_column(own_shift)
    prod[...] = prod[...] + wide(column, mid) * bias_sum
    prod[feats : feats + 1, :] = total_row(acc[1])
    prod[feats + 1 : feats + 2, :] = 2.0 * total_row(acc[0])
    prod[feats + 2 : feats + 3, :] = bias_sum
    prod[feats + 3 : feats + 4, :] = (2.0 * total_row(acc[3]) - bias * bias_sum) / gain
    pack[:, :HOP_ROWS, :] = jnp.stack(
        [prod[:HOP_ROWS, t * LANES : (t + 1) * LANES] for t in range(tiles)]
    )
    pack[0, HOP_ROWS:, :] = (gram_ref[0] + column * (own_shift * own_count))[:HOP_ROWS]
    flip = code_ref[1] * (tiles // 2)
    outs = [feat_out]
    for t in range(tiles):
        outs.append(
            pltpu.make_async_copy(
                pack.at[t, pl.ds(0, HOP_ROWS)],
                pack_hbm.at[t ^ flip, pl.ds(h * HOP_ROWS, HOP_ROWS)],
                out_sem.at[t],
            )
        )
    at = tiles * HOP_ROWS
    outs.append(
        pltpu.make_async_copy(
            pack.at[0, pl.ds(HOP_ROWS, HOP_ROWS)],
            pack_hbm.at[h ^ flip, pl.ds(at + HEAD_ROWS, HOP_ROWS)],
            out_sem.at[5],
        )
    )
    if h == 0:
        for t in range(tiles):
            outs.append(
                pltpu.make_async_copy(
                    misc_ref.at[t], pack_hbm.at[t ^ flip, pl.ds(at, HEAD_ROWS)], out_sem.at[6 + t]
                )
            )
    for copy in outs[1:]:
        copy.start()
    for copy in outs:
        copy.wait()


def finish_kernel(
    code_ref, pay_ref, inv_ref, mine_ref, other_ref, feat_ref, xcat_ref, w_ref, gain_ref, mask_ref, bg_ref,
    fgrad_hbm, wgrad_hbm, gain_out, bias_out, slope1_out, slope2_out, mgain_out, mbias_out, mslope_out,
    owg_out, obg_out, loss_out,
    sum_ref, rows_scr, fgrad, wgrad, sem,
):
    hops, feats, width = w_ref.shape
    tiles = mine_ref.shape[0] * 2
    half = tiles // 2
    flip = code_ref[1]

    @pl.when(flip == 0)
    def _():
        for t in range(half):
            sum_ref[:, t * LANES : (t + 1) * LANES] = mine_ref[t]
            sum_ref[:, (half + t) * LANES : (half + t + 1) * LANES] = other_ref[t]

    @pl.when(flip != 0)
    def _():
        for t in range(half):
            sum_ref[:, t * LANES : (t + 1) * LANES] = other_ref[t]
            sum_ref[:, (half + t) * LANES : (half + t + 1) * LANES] = mine_ref[t]

    counts = real_nodes(pay_ref)
    total = jnp.sum(counts, axis=0, keepdims=True)
    keep = mask_ref[...].astype(f32)
    at = hops * HOP_ROWS
    copies = []
    for h in range(hops):
        base = h * HOP_ROWS
        w = pad_rows(w_ref[h], LANES)
        inverse = inv_ref[h]
        scale = gain_ref[h] * inverse
        slope1_out[h] = sum_ref[base + feats : base + feats + 1, :]
        slope2_out[h] = sum_ref[base + feats + 1 : base + feats + 2, :]
        bias_sum = sum_ref[base + feats + 2 : base + feats + 3, :]
        gain_sum = sum_ref[base + feats + 3 : base + feats + 4, :]
        bias_out[h] = bias_sum
        gain_out[h] = gain_sum
        gram = sum_ref[at + HEAD_ROWS : at + HEAD_ROWS + HOP_ROWS, h * LANES : (h + 1) * LANES]
        inner = dot(gram, w, exact)[:feats] * (inverse * gain_sum / total)
        wgrad[h] = scale * (sum_ref[base : base + feats, :] - inner)
        copies.append(pltpu.make_async_copy(wgrad.at[h], wgrad_hbm.at[:, h, :], sem.at[0, h]))
        copies[-1].start()
        shift = feature_shift(pay_ref, h)
        rows_scr[...] = shift
        own_shift = rows_scr[pl.ds(code_ref[0], 1), :]
        mix = dot_nt(w * (scale * inverse * gain_sum / total), w, exact)
        lane = lax.broadcasted_iota(jnp.int32, (1, LANES), 1)
        off = jnp.sum(w * (scale * bias_sum / total), axis=1, keepdims=True)
        off = off + jnp.sum(mix * jnp.where(lane < feats, own_shift, 0.0), axis=1, keepdims=True)
        high, low = split(mix)
        mixed = dot(jnp.concatenate([high, high], axis=1), xcat_ref[h]) + dot(low, xcat_ref[h, :LANES])
        fgrad[h] = keep * (feat_ref[h] - (mixed + off)[:feats])
        copies.append(pltpu.make_async_copy(fgrad.at[h], fgrad_hbm.at[:, h, :], sem.at[1, h]))
        copies[-1].start()
    owg_out[...] = sum_ref[at : at + owg_out.shape[0], :]
    mslope_out[...] = sum_ref[at + CLASS_ROWS : at + CLASS_ROWS + 1, :]
    obg_out[...] = sum_ref[at + CLASS_ROWS + 1 : at + CLASS_ROWS + 2, : obg_out.shape[1]]
    loss_out[...] = sum_ref[at + CLASS_ROWS + 2 : at + CLASS_ROWS + 3, :1] / total
    mbias_out[...] = bg_ref[0:1, :]
    mgain_out[...] = bg_ref[1:2, :]
    for copy in copies:
        copy.wait()


def place_kernel(code_ref, in_ref, *refs):
    out_ref = refs[-1]
    rows = in_ref.shape[1] // PIECES
    code = code_ref[pl.program_id(0)] & (PIECES - 1)
    for i in range(PIECES):
        place = pl.multiple_of((i ^ code) * rows, rows)
        out_ref[i * rows : (i + 1) * rows, :] = in_ref[0, pl.ds(place, rows), :]


def exchange(values, bit, devices):
    return lax.ppermute(values, axes, [(i, i ^ (1 << bit)) for i in range(devices)])


def code_of(me, order):
    code = 0
    for bit in order:
        code = code * 2 + ((me >> bit) & 1)
    return code


def after(values, *others):
    return lax.optimization_barrier((values, *others))[0]


def on_device(
    devices,
    hop_features,
    branch_weight,
    branch_gain,
    branch_bias,
    first_slope,
    second_slope,
    mid_weight,
    mid_gain,
    mid_bias,
    mid_slope,
    out_weight,
    out_bias,
    labels,
    valid_mask,
):
    hops, feats, nodes = hop_features.shape
    width = branch_weight.shape[2]
    mid = mid_weight.shape[1]
    classes = out_weight.shape[1]
    tiles = mid // LANES
    bits = devices.bit_length() - 1
    me = lax.axis_index(axes).astype(jnp.int32)
    rest = tuple(range(5, bits))
    codes = jnp.stack([code_of(me, (0, 1, 2, 3, 4)), code_of(me, (0, 2, 1, 3, 4))])
    place_code = jnp.stack([me, me & 1])
    shape = jax.ShapeDtypeStruct
    mask = valid_mask.reshape(1, nodes)
    label = labels.reshape(1, nodes)
    by_hop = lambda v: v.reshape(hops, 1, width)
    gain, bias, slope1, slope2 = map(by_hop, (branch_gain, branch_bias, first_slope, second_slope))
    row = lambda v: v.reshape(1, -1)
    gather = functools.partial(
        lax.all_to_all, axis_name=axes, split_axis=0, concat_axis=0, tiled=True
    )
    dma = pltpu.SemaphoreType.DMA

    pay, gram, xcat, w = call(
        stats_kernel,
        in_specs=[anywhere, anywhere, whole(1, nodes)],
        out_shape=(
            shape((devices, 24, LANES), f32), shape((hops, LANES, LANES), f32),
            shape((hops, 2 * LANES, nodes), bf16), shape((hops, feats, width), f32),
        ),
        scratch_shapes=[
            pltpu.VMEM((hops, feats, nodes), f32), pltpu.VMEM((24, LANES), f32),
            dma((hops,)), dma((hops,)),
        ],
        name="first_stats",
    )(jnp.transpose(hop_features, (1, 0, 2)), jnp.transpose(branch_weight, (1, 0, 2)), mask)
    pay = gather(pay)

    hop_row = pl.BlockSpec((1, 1, width), lambda h, *_: (h, 0, 0))
    hop_w = pl.BlockSpec((1, feats, width), lambda h, *_: (h, 0, 0))
    pre, w2cat, col = call(
        prepare_kernel,
        grid=(hops,),
        in_specs=[
            pl.BlockSpec((1, 2 * LANES, nodes), lambda h: (h, 0, 0)), hop_w,
            pl.BlockSpec((width, mid), lambda h: (h, 0)), hop_row, hop_row,
        ],
        out_specs=[
            pl.BlockSpec((width, nodes), lambda h: (h, 0)),
            pl.BlockSpec((1, mid, 3 * width), lambda h: (h, 0, 0)),
            pl.BlockSpec((1, 4, width, LANES), lambda h: (h, 0, 0, 0)),
        ],
        out_shape=(
            shape((hops * width, nodes), f32), shape((hops, mid, 3 * width), bf16),
            shape((hops, 4, width, LANES), f32),
        ),
        cost_estimate=cost(4 * 2 * 4 * hops * LANES * width * nodes, 40_000_000),
        name="prepare",
    )(xcat, w, mid_weight, slope1, slope2)

    pay_spec = whole(devices, 24, LANES)
    now = lambda s: jnp.minimum(s, hops - 1)
    before = lambda s: jnp.maximum(s - 1, 0)
    act, mid_pre, stat, first_inv, norm = call(
        forward_kernel,
        grid_spec=pltpu.PrefetchScalarGridSpec(
            num_scalar_prefetch=1,
            grid=(hops + 1,),
            in_specs=[
                pay_spec,
                pl.BlockSpec((1, feats, width), lambda s, *_: (now(s), 0, 0)),
                pl.BlockSpec((1, 1, width), lambda s, *_: (now(s), 0, 0)),
                pl.BlockSpec((1, 1, width), lambda s, *_: (now(s), 0, 0)),
                pl.BlockSpec((width, nodes), lambda s, *_: (now(s), 0)),
                pl.BlockSpec((1, 4, width, LANES), lambda s, *_: (now(s), 0, 0, 0)),
                pl.BlockSpec((1, mid, 3 * width), lambda s, *_: (before(s), 0, 0)),
                whole(1, nodes),
            ],
            out_specs=[
                pl.BlockSpec((2, width, nodes), lambda s, *_: (0, now(s), 0)),
                whole(mid, nodes), whole(devices, 8, LANES),
                pl.BlockSpec((1, 1, width), lambda s, *_: (now(s), 0, 0)),
                pl.BlockSpec((1, 2, width, LANES), lambda s, *_: (now(s), 0, 0, 0)),
            ],
            scratch_shapes=[
                pltpu.VMEM((2, 2 * width, nodes), bf16), pltpu.VMEM((devices, width), f32),
                pltpu.VMEM((8, LANES), f32),
            ],
        ),
        out_shape=(
            shape((2, hops * width, nodes), bf16), shape((mid, nodes), f32),
            shape((devices, 8, LANES), f32), shape((hops, 1, width), f32),
            shape((hops, 2, width, LANES), f32),
        ),
        name="forward",
    )(place_code, pay, w, gain, bias, pre, col, w2cat, mask)
    stat = gather(stat)

    logits, up, normed, mid_inv, sums, misc = call(
        head_kernel,
        out_shape=(
            shape((classes, nodes), f32), shape((mid, nodes), f32), shape((mid, nodes), f32),
            shape((1, mid), f32), shape((devices, 8, LANES), f32),
            shape((tiles, HEAD_ROWS, LANES), f32),
        ),
        scratch_shapes=[
            pltpu.VMEM((LANES, mid), f32), pltpu.VMEM((1, LANES), f32), pltpu.VMEM((8, LANES), f32),
            pltpu.VMEM((mid, nodes), f32), pltpu.VMEM((mid, nodes), f32),
            pltpu.VMEM((2 * mid, nodes), bf16), pltpu.VMEM((6, mid, LANES), f32),
            pltpu.VMEM((mid, nodes), f32), pltpu.VMEM((3, mid, LANES), f32),
            pltpu.VMEM((HEAD_ROWS, mid), f32),
        ],
        name="head",
    )(pay, stat, mid_pre, row(mid_gain), row(mid_bias), row(mid_slope), out_weight.T, row(out_bias), label, mask)
    sums = gather(sums)

    def rows_for(half_sel):
        return pl.BlockSpec(
            (2, width, nodes), lambda s, code: (0, s * 2 + (half_sel ^ (code[s] >> 4)), 0)
        )

    full = whole(mid, nodes)
    piece = pl.BlockSpec((1, width, mid), lambda s, code: (s, 0, 0))
    product_cost = cost(2 * 3 * 2 * width * mid * nodes, 20_000_000)
    send, gcat, mid_bg = call(
        mid_grad_kernel,
        grid_spec=pltpu.PrefetchScalarGridSpec(
            num_scalar_prefetch=1,
            grid=(2,),
            in_specs=[
                pay_spec, whole(devices, 8, LANES), whole(1, mid), whole(1, mid), full, full,
                whole(1, nodes), rows_for(1),
            ],
            out_specs=[piece, whole(3 * mid, nodes), whole(2, mid)],
        ),
        out_shape=(
            shape((2, width, mid), f32), shape((3 * mid, nodes), bf16), shape((2, mid), f32),
        ),
        cost_estimate=product_cost,
        name="mid_grad_send",
    )(codes, pay, sums, mid_inv, row(mid_gain), up, normed, mask, act)
    came = exchange(send, 0, devices)
    kept = call(
        mid_grad_rest_kernel,
        grid_spec=pltpu.PrefetchScalarGridSpec(
            num_scalar_prefetch=1,
            grid=(2,),
            in_specs=[rows_for(0), whole(3 * mid, nodes)],
            out_specs=piece,
        ),
        out_shape=shape((2, width, mid), f32),
        cost_estimate=product_cost,
        name="mid_grad_keep",
    )(codes, act, gcat)

    pack_rows = hops * HOP_ROWS + HEAD_ROWS + HOP_ROWS

    def backward(h, feat_pack, gcat):
        base = () if feat_pack is None else feat_pack
        one = lambda *dims: pl.BlockSpec(dims, lambda *_: (h,) + (0,) * (len(dims) - 1))
        inputs = (
            place_code, pay, first_inv, gain, bias, w, gram, misc, gcat, mid_weight, pre, norm, col, xcat,
        )
        return call(
            functools.partial(backward_kernel, h),
            grid_spec=pltpu.PrefetchScalarGridSpec(
                num_scalar_prefetch=1,
                grid=(1,),
                in_specs=[
                    pay_spec, one(1, 1, width), one(1, 1, width), one(1, 1, width), one(1, feats, width),
                    one(1, LANES, LANES), whole(tiles, HEAD_ROWS, LANES),
                ] + [anywhere] * (6 + len(base)),
                out_specs=[anywhere, anywhere],
                scratch_shapes=[
                    pltpu.VMEM((3 * mid, nodes), bf16), pltpu.VMEM((width, mid), f32),
                    pltpu.VMEM((width, nodes), f32), pltpu.VMEM((2, width, LANES), f32),
                    pltpu.VMEM((4, width, LANES), f32), pltpu.VMEM((2 * LANES, nodes), bf16),
                    pltpu.VMEM((width, nodes), f32), pltpu.VMEM((2 * width, nodes), bf16),
                    pltpu.VMEM((4, width, LANES), f32), pltpu.VMEM((LANES, mid), f32),
                    pltpu.VMEM((2 * devices, LANES), f32),
                    pltpu.VMEM((tiles, 2 * HOP_ROWS, LANES), f32), pltpu.VMEM((feats, nodes), f32),
                    dma((4,)), dma((nodes // CHUNK,)), dma((nodes // CHUNK,)), dma((10,)),
                ],
            ),
            out_shape=(
                shape((hops, feats, nodes), f32), shape((tiles, pack_rows, LANES), f32),
            ),
            input_output_aliases={len(inputs): 0, len(inputs) + 1: 1} if base else {},
            cost_estimate=cost(2 * 4 * width * mid * nodes, 12_000_000),
            name="backward",
        )(*inputs, *base)

    a, b = kept[0] + came[0], kept[1] + came[1]
    grads = gcat
    state = None
    step = 0
    for bit_a, bit_b in ((1, 2), (2, 1)):
        size = a.shape[0] // 2
        send_a, send_b = a[size:], b[size:]
        grads = after(grads, send_a, send_b)
        ra = exchange(send_a, bit_a, devices)
        rb = exchange(send_b, bit_b, devices)
        state = backward(step, state, grads)
        step += 1
        ra, rb = after(ra, state[1]), after(rb, state[1])
        a, b = a[:size] + ra, b[:size] + rb
    part = a.shape[0] // 4
    both = jnp.stack([a.reshape(4, part, mid), b.reshape(4, part, mid)], axis=1)
    for bit in (3, 4):
        size = both.shape[0] // 2
        send_z = both[size:]
        grads = after(grads, send_z)
        rz = exchange(send_z, bit, devices)
        state = backward(step, state, grads)
        step += 1
        rz = after(rz, state[1])
        both = both[:size] + rz
    for bit in rest:
        both = both + exchange(both, bit, devices)
    feat, pack = state

    half = tiles // 2
    blocks = devices // 2
    groups = [[i for i in range(devices) if i % 2 == c] for c in (0, 1)]
    spread = functools.partial(
        lax.all_to_all, axis_name=axes, split_axis=0, concat_axis=0, axis_index_groups=groups, tiled=True
    )
    pack = pack[:half] + exchange(pack[half:], 0, devices)
    pack = spread(pack.reshape(blocks, -1, LANES)).sum(axis=0)
    pack = spread(jnp.broadcast_to(pack[None], (blocks,) + pack.shape))
    pack = pack.reshape(half, pack_rows, LANES)
    pack_other = exchange(pack, 0, devices)

    both = jnp.concatenate([both, exchange(both, 4, devices)])
    both = jnp.concatenate([both, exchange(both, 3, devices)])
    a, b = both[:, 0].reshape(-1, mid), both[:, 1].reshape(-1, mid)
    for bit_a, bit_b in ((2, 1), (1, 2)):
        ra = exchange(a, bit_a, devices)
        rb = exchange(b, bit_b, devices)
        a, b = jnp.concatenate([a, ra]), jnp.concatenate([b, rb])
    mine = jnp.stack([a, b])
    other = exchange(mine, 0, devices)

    def place(half_sel, values, *base):
        return call(
            place_kernel,
            grid_spec=pltpu.PrefetchScalarGridSpec(
                num_scalar_prefetch=1,
                grid=(2,),
                in_specs=[piece] + [anywhere] * len(base),
                out_specs=pl.BlockSpec(
                    (width, mid), lambda s, code: (s * 2 + (half_sel ^ (code[s] >> 4)), 0)
                ),
            ),
            out_shape=shape(mid_weight.shape, f32),
            input_output_aliases={2: 0} if base else {},
            cost_estimate=cost(0, 8_000_000),
            name="place",
        )(codes, values, *base)

    mid_weight_grad = place(1, other, place(0, mine))

    rows_out = [shape((hops, 1, width), f32)] * 4
    rows_mid = [shape((1, mid), f32)] * 3
    (
        feature_grad, branch_weight_grad, branch_gain_grad, branch_bias_grad, first_slope_grad,
        second_slope_grad, mid_gain_grad, mid_bias_grad, mid_slope_grad, out_weight_grad,
        out_bias_grad, mean_loss,
    ) = call(
        finish_kernel,
        grid_spec=pltpu.PrefetchScalarGridSpec(
            num_scalar_prefetch=1,
            grid=(1,),
            in_specs=[
                pay_spec, whole(hops, 1, width), whole(half, pack_rows, LANES), whole(half, pack_rows, LANES),
                whole(hops, feats, nodes), whole(hops, 2 * LANES, nodes), whole(hops, feats, width),
                whole(hops, 1, width), whole(1, nodes), whole(2, mid),
            ],
            out_specs=[anywhere, anywhere] + [whole(hops, 1, width)] * 4 + [whole(1, mid)] * 3 + [
                whole(classes, mid), whole(1, classes), whole(1, 1),
            ],
            scratch_shapes=[
                pltpu.VMEM((pack_rows, mid), f32), pltpu.VMEM((devices, LANES), f32),
                pltpu.VMEM((hops, feats, nodes), f32), pltpu.VMEM((hops, feats, width), f32),
                dma((2, hops)),
            ],
        ),
        out_shape=(
            shape((feats, hops, nodes), f32), shape((feats, hops, width), f32), *rows_out, *rows_mid,
            shape((classes, mid), f32), shape((1, classes), f32), shape((1, 1), f32),
        ),
        cost_estimate=cost(0, 20_000_000),
        name="finish",
    )(place_code, pay, first_inv, pack, pack_other, feat, xcat, w, gain, mask, mid_bg)
    flat = lambda v: v.reshape(-1)
    return (
        logits,
        mean_loss.reshape(()),
        jnp.transpose(feature_grad, (1, 0, 2)),
        jnp.transpose(branch_weight_grad, (1, 0, 2)),
        flat(branch_gain_grad),
        flat(branch_bias_grad),
        flat(first_slope_grad),
        flat(second_slope_grad),
        mid_weight_grad,
        flat(mid_gain_grad),
        flat(mid_bias_grad),
        flat(mid_slope_grad),
        out_weight_grad.T,
        flat(out_bias_grad),
    )


def solution(mesh):
    devices = mesh.shape["dp"] * mesh.shape["rep"]

    def body(*arrays):
        return on_device(devices, *arrays)

    nodes = P(("dp", "rep"))
    return jax.shard_map(
        body,
        mesh=mesh,
        in_specs=(P(None, None, ("dp", "rep")),) + (P(),) * 11 + (nodes, nodes),
        out_specs=(P(None, ("dp", "rep")), P(), P(None, None, ("dp", "rep"))) + (P(),) * 11,
        check_vma=False,
    )
```

```python
import functools

import jax
import jax.numpy as jnp
from jax import lax
from jax.experimental import pallas as pl
from jax.experimental.pallas import tpu as pltpu
from jax.sharding import PartitionSpec as P

epsilon = 1e-05
axes = ("dp", "rep")
exact = lax.Precision.HIGHEST
f32 = jnp.float32
bf16 = jnp.bfloat16
LANES = 128
CHUNK = 256
PIECES = 16
HOP_ROWS = 104
HEAD_ROWS = 56
CLASS_ROWS = 48


def dot(left, right, precision=None):
    return lax.dot_general(
        left, right, (((1,), (0,)), ((), ())), precision=precision, preferred_element_type=f32
    )


def dot_nt(left, right, precision=None):
    return lax.dot_general(
        left, right, (((1,), (1,)), ((), ())), precision=precision, preferred_element_type=f32
    )


def split(values):
    high = values.astype(bf16)
    return high, (values - high.astype(f32)).astype(bf16)


def as_column(row):
    return jnp.broadcast_to(row, (LANES, row.shape[1])).T


def wide(column, width):
    return jnp.concatenate([column] * (width // LANES), axis=1)


def fold(values):
    total = values[:, :LANES]
    for start in range(LANES, values.shape[1], LANES):
        total = total + values[:, start : start + LANES]
    return total


def total_row(partial):
    return jnp.sum(partial.T, axis=0, keepdims=True)


def pad_rows(values, rows):
    return jnp.concatenate(
        [values, jnp.zeros((rows - values.shape[0], values.shape[1]), values.dtype)], axis=0
    )


def weave(products, slabs):
    done = 0
    for j, product in enumerate(products):
        until = (j + 1) * len(slabs) // len(products)
        for slab in slabs[done:until]:
            slab()
        done = until
        product()


def cost(flops=0, bytes_accessed=0):
    return pl.CostEstimate(flops=flops, bytes_accessed=bytes_accessed, transcendentals=0)


def call(kernel, mib, **options):
    return pl.pallas_call(
        kernel, compiler_params=pltpu.CompilerParams(vmem_limit_bytes=mib * 1024 * 1024), **options
    )


class Copies:
    def __init__(self, sems):
        self.sems = sems
        self.used = 0
        self.waiting = []

    def start(self, source, target):
        copy = pltpu.make_async_copy(source, target, self.sems.at[self.used])
        self.used += 1
        copy.start()
        return copy

    def send(self, source, target):
        self.waiting.append(self.start(source, target))

    def finish(self):
        for copy in self.waiting:
            copy.wait()


anywhere = pl.BlockSpec(memory_space=pl.ANY)
vmem = pl.BlockSpec(memory_space=pltpu.VMEM)
smem = pl.BlockSpec(memory_space=pltpu.SMEM)


def aligned(index, step):
    return pl.ds(pl.multiple_of(index * step, step), step)


def stats_kernel(
    x_hbm, w_hbm, mask_ref,
    pay_ref, gram_ref, xcat_hbm, w_out,
    x_scr, w_scr, xcat_ref, row_ref, sems,
):
    copies = Copies(sems)
    hops, feats, _ = x_scr.shape
    x_in, w_in = [], []
    for h in range(hops):
        x_in.append(copies.start(x_hbm.at[:, h, :], x_scr.at[h]))
        w_in.append(copies.start(w_hbm.at[:, h, :], w_scr.at[h]))
    keep = mask_ref[...].reshape(1, -1).astype(f32)
    count = jnp.sum(keep, axis=1, keepdims=True)
    safe = jnp.maximum(count, 1.0)
    row_ref[...] = jnp.zeros_like(row_ref)
    for h in range(hops):
        x_in[h].wait()
        x = x_scr[h]
        mean = jnp.sum(x * keep, axis=1, keepdims=True) / safe
        high, low = split(pad_rows(x - mean, LANES))
        xcat_ref[h, :LANES, :] = high
        xcat_ref[h, LANES:, :] = low
        copies.send(xcat_ref.at[h], xcat_hbm.at[h])
        w_in[h].wait()
        copies.send(w_scr.at[h], w_out.at[h])
        real = jnp.concatenate([high, low], axis=0) * keep.astype(bf16)
        gram = dot_nt(real, real)
        gram = (gram[:LANES, :LANES] + gram[LANES:, LANES:]) + (
            gram[:LANES, LANES:] + gram[LANES:, :LANES]
        )
        gram_ref[h] = gram
        w = pad_rows(w_scr[h], LANES)
        square = jnp.sum(dot(gram, w, exact) * w, axis=0, keepdims=True)
        tiles = w.shape[1] // LANES
        for i in range(tiles):
            row_ref[h * 5 + i : h * 5 + i + 1, :] = square[:, i * LANES : (i + 1) * LANES]
        mean = pad_rows(jnp.broadcast_to(mean, (feats, LANES)), LANES).T
        row_ref[h * 5 + 4 : h * 5 + 5, :] = mean[:1]
        row_ref[h * 5 + 4 : h * 5 + 5, LANES - 1 :] = count
    pay_ref[...] = jnp.broadcast_to(row_ref[...][None], pay_ref.shape)
    copies.finish()


def real_nodes(pay_ref):
    return pay_ref[:, 4, LANES - 1 :]


def feature_shift(pay_ref, h):
    means = pay_ref[:, h * 5 + 4, :]
    counts = means[:, LANES - 1 :]
    total = jnp.sum(counts, axis=0, keepdims=True)
    return means - jnp.sum(counts * means, axis=0, keepdims=True) / total


def prepare_kernel(xcat_hbm, w_ref, w2_hbm, pre_hbm, w2cat_hbm, xcat, w2, pre, w2cat, sems):
    copies = Copies(sems)
    hops, _, width = w_ref.shape
    nodes = xcat.shape[2]
    step = 2 * CHUNK
    quarter = width // 4
    ready = []
    for h in range(hops):
        ready.append(copies.start(xcat_hbm.at[h], xcat.at[h]))
        ready.append(copies.start(w2_hbm.at[h * width : (h + 1) * width, :], w2.at[h]))
    for h in range(hops):
        high, low = split(pad_rows(w_ref[h], LANES).T)
        wcat = jnp.concatenate(
            [jnp.concatenate([high, high], axis=1), jnp.concatenate([low, low], axis=1)], axis=0
        )

        def product(start):
            cols = slice(start, start + step)
            value = dot(wcat, xcat[h, :, cols])
            pre[h, :, cols] = value[:width] + value[width:]

        def turn(i):
            at = i * quarter
            high, low = split(w2[h, at : at + quarter, :].T)
            w2cat[h, :, at : at + quarter] = high
            w2cat[h, :, width + at : width + at + quarter] = low

        ready[2 * h].wait()
        ready[2 * h + 1].wait()
        weave(
            [functools.partial(product, start) for start in range(0, nodes, step)],
            [functools.partial(turn, i) for i in range(4)],
        )
        copies.send(pre.at[h], pre_hbm.at[h * width : (h + 1) * width, :])
        copies.send(w2cat.at[h], w2cat_hbm.at[h])
    copies.finish()


def columns_of(pack):
    rows = pack.shape[0]
    return [jnp.broadcast_to(pack[:, i : i + 1], (rows, LANES)) for i in range(6)]


def forward_kernel(
    code_ref, pay_ref, w_ref, gain_ref, bias_ref, slope1_ref, slope2_ref, mask_ref, pre_hbm, w2cat_hbm,
    mid_ref, stat_ref, inv_ref, colpack_ref, act,
    pre, w2cat, shift_ref, row_ref, sems,
):
    copies = Copies(sems)
    hops, _, width = w_ref.shape
    nodes = mid_ref.shape[1]
    ready = []
    for h in range(hops):
        rows = slice(h * width, (h + 1) * width)
        ready.append((
            copies.start(pre_hbm.at[rows, :], pre.at[h]),
            copies.start(w2cat_hbm.at[h], w2cat.at[h]),
        ))
    counts = real_nodes(pay_ref)
    total = jnp.sum(counts, axis=0, keepdims=True)
    for h in range(hops):
        shift = dot(feature_shift(pay_ref, h), pad_rows(w_ref[h], LANES), exact)
        shift_ref[h] = shift
        squares = rows_of(pay_ref, h * 5, width // LANES)
        square = jnp.sum(squares + counts * shift * shift, axis=0, keepdims=True)
        inverse = lax.rsqrt(square / total + epsilon)
        inv_ref[h] = inverse
        scale = 0.5 * gain_ref[h] * inverse
        rows = [
            scale,
            shift_ref[h, pl.ds(code_ref[0], 1), :] * scale + 0.5 * bias_ref[h],
            0.5 + 0.5 * slope1_ref[h],
            0.5 - 0.5 * slope1_ref[h],
            1.0 + slope2_ref[h],
            1.0 - slope2_ref[h],
        ]
        colpack_ref[h] = pad_rows(jnp.concatenate(rows, axis=0), LANES).T

    def slabs(h):
        rows = 16

        def slab(r):
            rs = slice(r, r + rows)
            columns = columns_of(colpack_ref[h, rs, :])
            scale, shift, p1, q1, p2, q2 = (wide(c, nodes) for c in columns)
            half = pre[h, rs, :] * scale + shift
            half = half * (p1 + q1 * jnp.tanh(half))
            high, low = split(half * (p2 + q2 * jnp.tanh(half)))
            act[0, h * width + r : h * width + r + rows, :] = high
            act[1, h * width + r : h * width + r + rows, :] = low

        return [functools.partial(slab, r) for r in range(0, width, rows)]

    def products(h):
        def product(start):
            cols = slice(start, start + CHUNK)
            own = slice(h * width, (h + 1) * width)
            high, low = act[0, own, cols], act[1, own, cols]
            w2_high, w2_low = w2cat[h, :, :width], w2cat[h, :, width:]
            value = dot(
                jnp.concatenate([w2_high, w2_high, w2_low], axis=1),
                jnp.concatenate([high, low, high], axis=0),
            )
            mid_ref[:, cols] = value if h == 0 else mid_ref[:, cols] + value

        return [functools.partial(product, start) for start in range(0, nodes, CHUNK)]

    for h in range(hops + 1):
        if h < hops:
            for copy in ready[h]:
                copy.wait()
        weave(products(h - 1) if h else [lambda: None], slabs(h) if h < hops else [])
    keep = mask_ref[...].reshape(1, -1).astype(f32)
    count = jnp.maximum(jnp.sum(keep, axis=1, keepdims=True), 1.0)
    mid = mid_ref[...]
    average = total_row(fold(mid * keep)) / count
    off = mid - wide(as_column(average), nodes)
    square = total_row(fold(off * off * keep))
    put_rows(row_ref, average, square)
    stat_ref[...] = jnp.broadcast_to(row_ref[...][None], stat_ref.shape)


def put_rows(row_ref, *rows):
    at = 0
    for row in rows:
        for start in range(0, row.shape[1], LANES):
            row_ref[at : at + 1, :] = row[:, start : start + LANES]
            at += 1


def rows_of(ref, first, count):
    return jnp.concatenate([ref[:, i, :] for i in range(first, first + count)], axis=1)


def head_kernel(
    pay_ref, stat_ref, gain_ref, bias_ref, slope_ref, ow_ref, ob_ref, label_ref, mask_ref, mid_ref,
    logit_ref, inv_ref, sums_ref, misc_ref, up_ref, norm_ref,
    ow_scr, ob_scr, row_ref, half_ref, tan_ref, acat_ref, col_ref, back_ref, acc_ref, misc_scr,
):
    width, nodes = mid_ref.shape
    classes = ow_ref.shape[0]
    tiles = width // LANES
    counts = real_nodes(pay_ref)
    total = jnp.sum(counts, axis=0, keepdims=True)
    means = rows_of(stat_ref, 0, tiles)
    average = jnp.sum(counts * means, axis=0, keepdims=True) / total
    off = means - average
    square = jnp.sum(rows_of(stat_ref, tiles, tiles) + counts * off * off, axis=0, keepdims=True)
    inverse = lax.rsqrt(square / total + epsilon)
    inv_ref[...] = inverse
    col_ref[0] = as_column(average)
    col_ref[1] = as_column(inverse)
    col_ref[2] = 0.5 * as_column(gain_ref[...])
    col_ref[3] = 0.5 * as_column(bias_ref[...])
    slope = as_column(slope_ref[...])
    col_ref[4] = 0.5 + 0.5 * slope
    col_ref[5] = 0.5 - 0.5 * slope
    ow_scr[...] = jnp.zeros_like(ow_scr)
    ow_scr[:classes, :] = ow_ref[...]
    ow_t = split(ow_scr[:CLASS_ROWS, :])
    ow = split(ow_scr[...].T)
    ob_scr[...] = jnp.zeros_like(ob_scr)
    ob_scr[:, :classes] = ob_ref[...]
    ob_col = wide(as_column(ob_scr[...])[:CLASS_ROWS], nodes)
    rows = 16
    for r in range(0, width, rows):
        rs = slice(r, r + rows)
        mean, inv, gain, bias, p, q = (wide(col_ref[i, rs], nodes) for i in range(6))
        normed = (mid_ref[rs, :] - mean) * inv
        norm_ref[rs, :] = normed
        half = normed * gain + bias
        tangent = jnp.tanh(half)
        half_ref[rs, :] = half
        tan_ref[rs, :] = tangent
        high, low = split(2.0 * half * (p + q * tangent))
        acat_ref[rs, :] = high
        acat_ref[slice(width + r, width + r + rows), :] = low
    high, low = acat_ref[:width, :], acat_ref[width:, :]
    logits = dot(jnp.concatenate([ow_t[0], ow_t[0]], axis=1), acat_ref[...]) + dot(ow_t[1], high)
    logits = logits + ob_col
    logit_ref[...] = logits[:classes]
    keep = mask_ref[...].reshape(1, -1).astype(f32)
    place = lax.broadcasted_iota(jnp.int32, (CLASS_ROWS, nodes), 0)
    logits = jnp.where(place < classes, logits, -3.0e38)
    shifted = logits - jnp.max(logits, axis=0, keepdims=True)
    weights = jnp.exp(shifted)
    norm = jnp.sum(weights, axis=0, keepdims=True)
    onehot = place == label_ref[...].reshape(1, -1)
    picked = jnp.sum(jnp.where(onehot, shifted, 0.0), axis=0, keepdims=True)
    loss = jnp.sum(fold(keep * (jnp.log(norm) - picked)), axis=1, keepdims=True)
    grad = keep * (weights * (1.0 / norm) - jnp.where(onehot, 1.0, 0.0))
    grad_sum = fold(grad)
    grad_high, grad_low = split(pad_rows(grad, LANES))
    gcat = jnp.concatenate([grad_high, grad_low, grad_high], axis=0)
    owcat = jnp.concatenate([ow[0], ow[0], ow[1]], axis=1)

    def back(start):
        back_ref[:, start : start + CHUNK] = dot(owcat, gcat[:, start : start + CHUNK])

    for start in range(0, nodes, CHUNK):
        back(start)
    both = jnp.concatenate([grad_high, grad_low], axis=0)

    def weight_grad():
        value = dot_nt(both, high)
        value = value[:CLASS_ROWS] + value[LANES : LANES + CLASS_ROWS]
        misc_scr[:CLASS_ROWS, :] = value + dot_nt(grad_high[:CLASS_ROWS], low)

    def slab(r):
        rs = slice(r, r + rows)
        p, q = wide(col_ref[4, rs], nodes), wide(col_ref[5, rs], nodes)
        half, tangent, act_grad = half_ref[rs, :], tan_ref[rs, :], back_ref[rs, :]
        away = half * (1.0 - tangent)
        acc_ref[0, rs] = fold(act_grad * away)
        up = act_grad * (p + q * (tangent + away * (1.0 + tangent)))
        up_ref[rs, :] = up
        acc_ref[1, rs] = fold(up)
        acc_ref[2, rs] = fold(up * norm_ref[rs, :])

    slabs = [functools.partial(slab, r) for r in range(0, width, rows)]
    weave([weight_grad, lambda: None], slabs)
    put_rows(row_ref, total_row(acc_ref[1]), total_row(acc_ref[2]))
    sums_ref[...] = jnp.broadcast_to(row_ref[...][None], sums_ref.shape)
    misc_scr[CLASS_ROWS:, :] = jnp.zeros((HEAD_ROWS - CLASS_ROWS, width), f32)
    misc_scr[CLASS_ROWS : CLASS_ROWS + 1, :] = total_row(acc_ref[0])
    misc_scr[CLASS_ROWS + 1 : CLASS_ROWS + 2, :LANES] = total_row(pad_rows(grad_sum, LANES))
    misc_scr[CLASS_ROWS + 2 : CLASS_ROWS + 3, :1] = loss
    for t in range(tiles):
        misc_ref[t] = misc_scr[:, t * LANES : (t + 1) * LANES]


def mid_grad_kernel(
    code_ref, pay_ref, sums_ref, inv_ref, gain_ref, mask_ref, up_ref, norm_ref, act,
    out_ref, bg_ref, gcat,
):
    width, nodes = up_ref.shape
    tiles = width // LANES
    total = jnp.sum(real_nodes(pay_ref), axis=0, keepdims=True)
    bias_sum = jnp.sum(rows_of(sums_ref, 0, tiles), axis=0, keepdims=True)
    gain_sum = jnp.sum(rows_of(sums_ref, tiles, tiles), axis=0, keepdims=True)
    bg_ref[0:1, :] = bias_sum
    bg_ref[1:2, :] = gain_sum
    scale = as_column(gain_ref[...] * inv_ref[...])
    bias_col = as_column(bias_sum / total)
    gain_col = as_column(gain_sum / total)
    keep = mask_ref[...].reshape(1, -1).astype(f32)
    rows = 16
    for r in range(0, width, rows):
        rs = slice(r, r + rows)
        bias, gain = wide(bias_col[rs], nodes), wide(gain_col[rs], nodes)
        grad = up_ref[rs, :] - bias - norm_ref[rs, :] * gain
        high, low = split(keep * (wide(scale[rs], nodes) * grad))
        gcat[rs, :] = high
        gcat[width + r : width + r + rows, :] = low
    mid_product(1, code_ref, act, gcat, out_ref)


def mid_product(half_sel, code_ref, act, gcat, out_ref):
    parts, width, mid = out_ref.shape
    rows = width // PIECES

    def part(s, carry):
        code = code_ref[s]
        here = aligned(s * 2 + (half_sel ^ (code >> 4)), width)
        value = dot_nt(act[0, here, :], gcat[:mid, :])
        value = value + dot_nt(act[0, here, :], gcat[mid:, :])
        value = value + dot_nt(act[1, here, :], gcat[:mid, :])
        for i in range(PIECES):
            out_ref[s, aligned(i ^ (code & (PIECES - 1)), rows), :] = value[i * rows : (i + 1) * rows]
        return carry

    lax.fori_loop(0, parts, part, 0)


def mid_grad_rest_kernel(code_ref, gcat, act, out_ref):
    mid_product(0, code_ref, act, gcat, out_ref)


def backward_kernel(
    code_ref, pay_ref, inv_ref, gain_ref, bias_ref, colpack_ref, w_ref, gram_ref, misc_ref,
    g, w2_hbm, pre_hbm, xcat_hbm,
    pack_ref, feat_hbm,
    w2, pre, xcat, feat, col, down, ucat, acc, prod, rows_scr, sems,
):
    copies = Copies(sems)
    hops, feats, width = w_ref.shape
    mid, nodes = g.shape[0] // 2, g.shape[1]
    tiles = mid // LANES
    size = 2 * CHUNK
    chunks = [slice(start, start + size) for start in range(0, nodes, size)]
    count = len(chunks)
    stages = [(h, j) for h in range(hops) for j in range(count)]
    w_in, z_in, x_in = {}, {}, {}
    for h in range(hops):
        own = slice(h * width, (h + 1) * width)
        w_in[h] = copies.start(w2_hbm.at[own, :], w2.at[h])
        for j, c in enumerate(chunks):
            z_in[h, j] = copies.start(pre_hbm.at[own, c], pre.at[h, :, c])
        x_in[h] = copies.start(xcat_hbm.at[h], xcat.at[h])
    devices = pay_ref.shape[0]
    flip = code_ref[1] * (tiles // 2)
    at = hops * HOP_ROWS
    for t in range(tiles):
        pack_ref[t ^ flip, at : at + HEAD_ROWS, :] = misc_ref[t]
    w2cat, wcat = {}, {}

    def columns(h):
        rows = 64
        for r in range(0, width, rows):
            for k, values in enumerate(columns_of(colpack_ref[h, r : r + rows, :])):
                col[h % 2, k, r : r + rows, :] = values
        acc[h % 2] = jnp.zeros(acc.shape[1:], f32)

    def weights(h):
        high, low = split(pad_rows(w_ref[h], LANES) * (gain_ref[h] * inv_ref[h]))
        wcat[h] = (jnp.concatenate([high, low], axis=0), high)
        high, low = split(0.5 * w2[h])
        w2cat[h] = jnp.concatenate([high, high, low], axis=1)

    def part_of(j, part):
        return slice(chunks[j].start + part * CHUNK, chunks[j].start + (part + 1) * CHUNK)

    def down_product(index, part):
        h, j = stages[index]
        cs = part_of(j, part)
        high, low = g[:mid, cs], g[mid:, cs]
        value = dot(w2cat[h], jnp.concatenate([high, low, high], axis=0))
        down[index % 2, :, part * CHUNK : (part + 1) * CHUNK] = value

    def slab(index, r, rows):
        h, j = stages[index]
        two = h % 2
        rs, cs = slice(r, r + rows), chunks[j]
        scale, shift, p1, q1, p2, q2 = (wide(col[two, k, rs], size) for k in range(6))
        half1 = pre[h, rs, cs] * scale + shift
        grad2 = down[index % 2, rs, :]
        tan1 = jnp.tanh(half1)
        half2 = half1 * (p1 + q1 * tan1)
        tan2 = jnp.tanh(half2)
        away2 = half2 * (1.0 - tan2)
        acc[two, 0, rs] += fold(grad2 * away2)
        grad1 = grad2 * (p2 + q2 * (tan2 + away2 * (1.0 + tan2)))
        away1 = half1 * (1.0 - tan1)
        acc[two, 1, rs] += fold(grad1 * away1)
        grad = grad1 * (p1 + q1 * (tan1 + away1 * (1.0 + tan1)))
        acc[two, 2, rs] += fold(grad)
        acc[two, 3, rs] += fold(grad * half1)
        high, low = split(grad)
        ucat[two, rs, cs] = high
        ucat[two, width + r : width + r + rows, cs] = low

    def feature_product(index, part):
        h, j = stages[index]
        cs = part_of(j, part)
        value = dot(wcat[h][0], ucat[h % 2, :width, cs])
        value = value[:LANES] + value[LANES:] + dot(wcat[h][1], ucat[h % 2, width:, cs])
        feat[h, :, cs] = value[:feats]

    def weight_product(h):
        value = dot_nt(xcat[h], ucat[h % 2, :width, :])
        low = dot_nt(xcat[h, :LANES, :], ucat[h % 2, width:, :])
        prod[h % 2] = value[:LANES] + value[LANES:] + low

    def pack(h):
        two = h % 2
        bias_sum = total_row(acc[two, 2])
        shift = feature_shift(pay_ref, h)
        rows_scr[:devices, :] = shift
        rows_scr[devices:, :] = jnp.broadcast_to(real_nodes(pay_ref), shift.shape)
        own_shift = rows_scr[pl.ds(code_ref[0], 1), :]
        own_count = rows_scr[pl.ds(devices + code_ref[0], 1), :]
        column = as_column(own_shift)
        prod[two] = prod[two] + wide(column, mid) * bias_sum
        prod[two, feats : feats + 1, :] = total_row(acc[two, 1])
        prod[two, feats + 1 : feats + 2, :] = 2.0 * total_row(acc[two, 0])
        prod[two, feats + 2 : feats + 3, :] = bias_sum
        prod[two, feats + 3 : feats + 4, :] = (
            2.0 * total_row(acc[two, 3]) - bias_ref[h] * bias_sum
        ) / gain_ref[h]
        for t in range(tiles):
            pack_ref[t ^ flip, h * HOP_ROWS : (h + 1) * HOP_ROWS, :] = prod[
                two, :HOP_ROWS, t * LANES : (t + 1) * LANES
            ]
        gram = gram_ref[h] + column * (own_shift * own_count)
        pack_ref[h ^ flip, at + HEAD_ROWS :, :] = gram[:HOP_ROWS]

    rows = 16
    columns(0)
    w_in[0].wait()
    weights(0)
    for part in (0, 1):
        down_product(0, part)
    for index, (h, j) in enumerate(stages):
        products = []
        z_in[h, j].wait()
        if j + 1 == count:
            x_in[h].wait()
            if h + 1 < hops:
                w_in[h + 1].wait()
                weights(h + 1)
                columns(h + 1)
        if index + 1 < len(stages):
            products += [functools.partial(down_product, index + 1, part) for part in (0, 1)]
        if index >= 1:
            products += [functools.partial(feature_product, index - 1, part) for part in (0, 1)]
        if j == 0 and h >= 1:
            products.append(functools.partial(weight_product, h - 1))
        if j == 1 and h >= 1:
            copies.send(feat.at[h - 1], feat_hbm.at[h - 1])
            pack(h - 1)
        weave(products, [functools.partial(slab, index, r, rows) for r in range(0, width, rows)])
    for part in (0, 1):
        feature_product(len(stages) - 1, part)
    copies.send(feat.at[hops - 1], feat_hbm.at[hops - 1])
    weight_product(hops - 1)
    pack(hops - 1)
    copies.finish()


def spread_kernel(parts_ref, out_ref):
    total = parts_ref[0]
    for i in range(1, parts_ref.shape[0]):
        total = total + parts_ref[i]
    out_ref[...] = jnp.broadcast_to(total[None], out_ref.shape)


def finish_kernel(
    code_ref, pay_ref, inv_ref, mine_ref, other_ref, w_ref, gain_ref, mask_ref, bg_ref, xcat_hbm,
    feat_hbm, fgrad_hbm, wgrad_hbm, gain_out, bias_out, slope1_out, slope2_out, mgain_out, mbias_out, mslope_out,
    owg_out, obg_out, loss_out,
    sum_ref, rows_scr, fgrad, wgrad, feat, xcat, sems,
):
    hops, feats, width = w_ref.shape
    tiles = mine_ref.shape[0] * 2
    half = tiles // 2
    flip = code_ref[1]
    copies = Copies(sems)
    ready = []
    for h in range(hops):
        ready.append((copies.start(feat_hbm.at[h], feat.at[h]), copies.start(xcat_hbm.at[h], xcat.at[h])))

    @pl.when(flip == 0)
    def _():
        for t in range(half):
            sum_ref[:, t * LANES : (t + 1) * LANES] = mine_ref[t]
            sum_ref[:, (half + t) * LANES : (half + t + 1) * LANES] = other_ref[t]

    @pl.when(flip != 0)
    def _():
        for t in range(half):
            sum_ref[:, t * LANES : (t + 1) * LANES] = other_ref[t]
            sum_ref[:, (half + t) * LANES : (half + t + 1) * LANES] = mine_ref[t]

    counts = real_nodes(pay_ref)
    total = jnp.sum(counts, axis=0, keepdims=True)
    keep = mask_ref[...].reshape(1, -1).astype(f32)
    at = hops * HOP_ROWS
    for h in range(hops):
        base = h * HOP_ROWS
        w = pad_rows(w_ref[h], LANES)
        inverse = inv_ref[h]
        scale = gain_ref[h] * inverse
        slope1_out[h] = sum_ref[base + feats : base + feats + 1, :]
        slope2_out[h] = sum_ref[base + feats + 1 : base + feats + 2, :]
        bias_sum = sum_ref[base + feats + 2 : base + feats + 3, :]
        gain_sum = sum_ref[base + feats + 3 : base + feats + 4, :]
        bias_out[h] = bias_sum
        gain_out[h] = gain_sum
        gram = sum_ref[at + HEAD_ROWS : at + HEAD_ROWS + HOP_ROWS, h * LANES : (h + 1) * LANES]
        inner = dot(gram, w, exact)[:feats] * (inverse * gain_sum / total)
        wgrad[h] = scale * (sum_ref[base : base + feats, :] - inner)
        copies.send(wgrad.at[h], wgrad_hbm.at[:, h, :])
        shift = feature_shift(pay_ref, h)
        rows_scr[...] = shift
        own_shift = rows_scr[pl.ds(code_ref[0], 1), :]
        mix = dot_nt(w * (scale * inverse * gain_sum / total), w, exact)
        lane = lax.broadcasted_iota(jnp.int32, (1, LANES), 1)
        off = jnp.sum(w * (scale * bias_sum / total), axis=1, keepdims=True)
        off = off + jnp.sum(mix * jnp.where(lane < feats, own_shift, 0.0), axis=1, keepdims=True)
        high, low = split(mix)
        for copy in ready[h]:
            copy.wait()
        mixed = dot(jnp.concatenate([high, high], axis=1), xcat[h]) + dot(low, xcat[h, :LANES])
        fgrad[h] = keep * (feat[h] - (mixed + off)[:feats])
        copies.send(fgrad.at[h], fgrad_hbm.at[:, h, :])
    owg_out[...] = sum_ref[at : at + owg_out.shape[0], :]
    mslope_out[...] = sum_ref[at + CLASS_ROWS : at + CLASS_ROWS + 1, :]
    obg_out[...] = sum_ref[at + CLASS_ROWS + 1 : at + CLASS_ROWS + 2, : obg_out.shape[1]]
    loss_out[...] = sum_ref[at + CLASS_ROWS + 2 : at + CLASS_ROWS + 3, :1] / total
    mbias_out[...] = bg_ref[0:1, :]
    mgain_out[...] = bg_ref[1:2, :]
    copies.finish()


def place_kernel(pieces, code_ref, *refs):
    out_ref, sems = refs[-2:]
    copies = Copies(sems)
    for ref, (s, first, rows) in zip(refs, pieces):
        for i in range(ref.shape[0] // rows):
            block = s * 2 * PIECES + ((first + i) ^ code_ref[s])
            copies.send(ref.at[pl.ds(i * rows, rows)], out_ref.at[aligned(block, rows)])
    copies.finish()


def exchange(values, bit, devices):
    return lax.ppermute(values, axes, [(i, i ^ (1 << bit)) for i in range(devices)])


def code_of(me, order):
    code = 0
    for bit in order:
        code = code * 2 + ((me >> bit) & 1)
    return code


def after(values, *others):
    return lax.optimization_barrier((values, *others))[0]


def on_device(
    devices,
    hop_features,
    branch_weight,
    branch_gain,
    branch_bias,
    first_slope,
    second_slope,
    mid_weight,
    mid_gain,
    mid_bias,
    mid_slope,
    out_weight,
    out_bias,
    labels,
    valid_mask,
):
    hops, feats, nodes = hop_features.shape
    width = branch_weight.shape[2]
    mid = mid_weight.shape[1]
    classes = out_weight.shape[1]
    tiles = mid // LANES
    bits = devices.bit_length() - 1
    me = lax.axis_index(axes).astype(jnp.int32)
    rest = tuple(range(5, bits))
    codes = jnp.stack([code_of(me, (0, 1, 2, 3, 4)), code_of(me, (0, 2, 1, 3, 4))])
    place_code = jnp.stack([me, me & 1])
    shape = jax.ShapeDtypeStruct
    by_hop = lambda v: v.reshape(hops, 1, width)
    gain, bias, slope1, slope2 = map(by_hop, (branch_gain, branch_bias, first_slope, second_slope))
    row = lambda v: v.reshape(1, -1)
    gather = functools.partial(
        lax.all_to_all, axis_name=axes, split_axis=0, concat_axis=0, tiled=True
    )
    dma = pltpu.SemaphoreType.DMA
    scratch = lambda dtype, *dims: pltpu.VMEM(dims, dtype)
    mask = valid_mask

    pay, gram, xcat, w = call(
        stats_kernel,
        60,
        in_specs=[anywhere, anywhere, vmem],
        out_specs=[vmem, vmem, anywhere, anywhere],
        out_shape=(
            shape((devices, 24, LANES), f32), shape((hops, LANES, LANES), f32),
            shape((hops, 2 * LANES, nodes), bf16), shape((hops, feats, width), f32),
        ),
        scratch_shapes=[
            scratch(f32, hops, feats, nodes), scratch(f32, hops, feats, width),
            scratch(bf16, hops, 2 * LANES, nodes), scratch(f32, 24, LANES), dma((4 * hops,)),
        ],
        cost_estimate=cost(1_000_000_000, 8_000_000),
        name="first_stats",
    )(jnp.transpose(hop_features, (1, 0, 2)), jnp.transpose(branch_weight, (1, 0, 2)), mask)
    pay = gather(after(pay, codes, place_code))

    pre, w2cat = call(
        prepare_kernel,
        60,
        in_specs=[anywhere, vmem, anywhere],
        out_specs=[anywhere] * 2,
        out_shape=(shape((hops * width, nodes), f32), shape((hops, mid, 2 * width), bf16)),
        scratch_shapes=[
            scratch(bf16, hops, 2 * LANES, nodes), scratch(f32, hops, width, mid),
            scratch(f32, hops, width, nodes), scratch(bf16, hops, mid, 2 * width), dma((4 * hops,)),
        ],
        cost_estimate=cost(4 * 2 * 4 * hops * LANES * width * nodes, 20_000_000),
        name="prepare",
    )(xcat, w, mid_weight)

    mid_pre, stat, first_inv, colpack, act = call(
        forward_kernel,
        45,
        in_specs=[smem] + [vmem] * 7 + [anywhere] * 2,
        out_specs=[vmem] * 5,
        out_shape=(
            shape((mid, nodes), f32), shape((devices, 8, LANES), f32), shape((hops, 1, width), f32),
            shape((hops, width, LANES), f32), shape((2, hops * width, nodes), bf16),
        ),
        scratch_shapes=[
            scratch(f32, hops, width, nodes), scratch(bf16, hops, mid, 2 * width),
            scratch(f32, hops, devices, width), scratch(f32, 8, LANES), dma((2 * hops,)),
        ],
        cost_estimate=cost(3 * 2 * hops * width * mid * nodes, 20_000_000),
        name="forward",
    )(place_code, pay, w, gain, bias, slope1, slope2, mask, pre, w2cat)
    stat = gather(stat)

    logits, mid_inv, sums, misc, up, normed = call(
        head_kernel,
        40,
        in_specs=[vmem] * 10,
        out_specs=[vmem] * 6,
        out_shape=(
            shape((classes, nodes), f32), shape((1, mid), f32), shape((devices, 8, LANES), f32),
            shape((tiles, HEAD_ROWS, LANES), f32), shape((mid, nodes), f32), shape((mid, nodes), f32),
        ),
        scratch_shapes=[
            scratch(f32, LANES, mid), scratch(f32, 1, LANES), scratch(f32, 8, LANES),
            scratch(f32, mid, nodes), scratch(f32, mid, nodes), scratch(bf16, 2 * mid, nodes),
            scratch(f32, 6, mid, LANES), scratch(f32, mid, nodes), scratch(f32, 3, mid, LANES),
            scratch(f32, HEAD_ROWS, mid),
        ],
        cost_estimate=cost(2_000_000_000, 10_000_000),
        name="head",
    )(pay, stat, row(mid_gain), row(mid_bias), row(mid_slope), out_weight.T, row(out_bias), labels, mask, mid_pre)
    sums = gather(sums)

    product_cost = cost(2 * 3 * 2 * width * mid * nodes, 10_000_000)
    send, mid_bg, gcat = call(
        mid_grad_kernel,
        36,
        in_specs=[smem] + [vmem] * 8,
        out_specs=[vmem] * 3,
        out_shape=(
            shape((2, width, mid), f32), shape((2, mid), f32), shape((2 * mid, nodes), bf16),
        ),
        cost_estimate=product_cost,
        name="mid_grad_send",
    )(codes, pay, sums, mid_inv, row(mid_gain), mask, up, normed, act)
    came = exchange(send, 0, devices)
    kept = call(
        mid_grad_rest_kernel,
        40,
        in_specs=[smem, vmem, vmem],
        out_specs=vmem,
        out_shape=shape((2, width, mid), f32),
        cost_estimate=product_cost,
        name="mid_grad_keep",
    )(codes, gcat, act)

    pack_rows = hops * HOP_ROWS + HEAD_ROWS + HOP_ROWS

    def backward(gcat):
        return call(
            backward_kernel,
            52,
            in_specs=[smem] + [vmem] * 9 + [anywhere] * 3,
            out_specs=[vmem, anywhere],
            scratch_shapes=[
                scratch(f32, hops, width, mid), scratch(f32, hops, width, nodes),
                scratch(bf16, hops, 2 * LANES, nodes),
                scratch(f32, hops, feats, nodes), scratch(f32, 2, 6, width, LANES),
                scratch(f32, 2, width, 2 * CHUNK), scratch(bf16, 2, 2 * width, nodes),
                scratch(f32, 2, 4, width, LANES), scratch(f32, 2, LANES, mid),
                scratch(f32, 2 * devices, LANES), dma((3 * hops + (hops + 1) * nodes // CHUNK,)),
            ],
            out_shape=(shape((tiles, pack_rows, LANES), f32), shape((hops, feats, nodes), f32)),
            cost_estimate=cost(hops * 2 * 4 * width * mid * nodes, 24_000_000),
            name="backward",
        )(place_code, pay, first_inv, gain, bias, colpack, w, gram, misc, gcat, mid_weight, pre, xcat)

    a, b = kept[0] + came[0], kept[1] + came[1]
    size = a.shape[0] // 2
    send_a, send_b = a[size:], b[size:]
    ra = exchange(send_a, 1, devices)
    rb = exchange(send_b, 2, devices)
    pack, feat = backward(after(gcat, send_a, send_b))
    a, b = a[:size] + after(ra, pack), b[:size] + after(rb, pack)
    size = a.shape[0] // 2
    send_a, send_b = a[size:], b[size:]
    ra = exchange(send_a, 2, devices)
    rb = exchange(send_b, 1, devices)

    half = tiles // 2
    blocks = devices // 2
    groups = [[i for i in range(devices) if i % 2 == c] for c in (0, 1)]
    spread = functools.partial(
        lax.all_to_all, axis_name=axes, split_axis=0, concat_axis=0, axis_index_groups=groups, tiled=True
    )
    pack = after(pack, send_a, send_b)
    pack = pack[:half] + exchange(pack[half:], 0, devices)
    a, b = a[:size] + after(ra, pack), b[:size] + after(rb, pack)
    pack = spread(pack.reshape(blocks, -1, LANES))
    part = a.shape[0] // 4
    both = jnp.stack([a.reshape(4, part, mid), b.reshape(4, part, mid)], axis=1)
    pack = call(
        spread_kernel,
        16,
        in_specs=[vmem],
        out_specs=vmem,
        out_shape=shape(pack.shape, f32),
        cost_estimate=cost(0, 2_000_000),
        name="spread",
    )(after(pack, both))
    both = after(both, pack)
    for bit in (3, 4):
        size = both.shape[0] // 2
        both = both[:size] + exchange(both[size:], bit, devices)
    for bit in rest:
        both = both + exchange(both, bit, devices)
    both = jnp.concatenate([both, exchange(both, 4, devices)])
    both = jnp.concatenate([both, exchange(both, 3, devices)])
    pack = spread(after(pack, both)).reshape(half, pack_rows, LANES)
    a, b = both[:, 0].reshape(-1, mid), both[:, 1].reshape(-1, mid)
    ra = exchange(a, 2, devices)
    rb = exchange(b, 1, devices)
    a, b = jnp.concatenate([a, ra]), jnp.concatenate([b, rb])
    ra = exchange(a, 1, devices)
    rb = exchange(b, 2, devices)
    other_a, other_b = exchange(a, 0, devices), exchange(b, 0, devices)
    pack_other = exchange(after(pack, other_a), 0, devices)

    rows_out = [shape((hops, 1, width), f32)] * 4
    rows_mid = [shape((1, mid), f32)] * 3
    (
        feature_grad, branch_weight_grad, branch_gain_grad, branch_bias_grad, first_slope_grad,
        second_slope_grad, mid_gain_grad, mid_bias_grad, mid_slope_grad, out_weight_grad,
        out_bias_grad, mean_loss,
    ) = call(
        finish_kernel,
        24,
        in_specs=[smem] + [vmem] * 8 + [anywhere] * 2,
        out_specs=[anywhere, anywhere] + [vmem] * 10,
        scratch_shapes=[
            scratch(f32, pack_rows, mid), scratch(f32, devices, LANES), scratch(f32, hops, feats, nodes),
            scratch(f32, hops, feats, width), scratch(f32, hops, feats, nodes),
            scratch(bf16, hops, 2 * LANES, nodes), dma((4 * hops,)),
        ],
        out_shape=(
            shape((feats, hops, nodes), f32), shape((feats, hops, width), f32), *rows_out, *rows_mid,
            shape((classes, mid), f32), shape((1, classes), f32), shape((1, 1), f32),
        ),
        cost_estimate=cost(0, 20_000_000),
        name="finish",
    )(place_code, pay, first_inv, pack, pack_other, w, gain, mask, mid_bg, xcat, feat)

    rows = mid_weight.shape[0] // (4 * PIECES)
    eight = PIECES // 2

    def place(pieces, *base):
        values = [value for value, *_ in pieces]
        kinds = [(s, first, rows) for _, s, first in pieces]
        return call(
            functools.partial(place_kernel, kinds),
            16,
            in_specs=[smem] + [vmem] * len(values) + [anywhere] * len(base),
            out_specs=anywhere,
            scratch_shapes=[dma((len(values) * eight,))],
            out_shape=shape(mid_weight.shape, f32),
            input_output_aliases={1 + len(values): 0} if base else {},
            cost_estimate=cost(0, 4_000_000),
            name="place",
        )(codes, *values, *base)

    grad = place(
        [(a, 0, 0), (b, 1, 0), (other_a, 0, PIECES), (after(other_b, mid_bias_grad), 1, PIECES)]
    )
    ra, rb = after(ra, grad), after(rb, grad)
    other_ra, other_rb = exchange(ra, 0, devices), exchange(rb, 0, devices)
    grad = place([(ra, 0, eight), (rb, 1, eight)], grad)
    mid_weight_grad = place(
        [(other_ra, 0, PIECES + eight), (after(other_rb, grad), 1, PIECES + eight)], grad
    )

    flat = lambda v: v.reshape(-1)
    return (
        logits,
        mean_loss.reshape(()),
        jnp.transpose(feature_grad, (1, 0, 2)),
        jnp.transpose(branch_weight_grad, (1, 0, 2)),
        flat(branch_gain_grad),
        flat(branch_bias_grad),
        flat(first_slope_grad),
        flat(second_slope_grad),
        mid_weight_grad,
        flat(mid_gain_grad),
        flat(mid_bias_grad),
        flat(mid_slope_grad),
        out_weight_grad.T,
        flat(out_bias_grad),
    )


def solution(mesh):
    devices = mesh.shape["dp"] * mesh.shape["rep"]

    def body(*arrays):
        return on_device(devices, *arrays)

    nodes = P(("dp", "rep"))
    return jax.shard_map(
        body,
        mesh=mesh,
        in_specs=(P(None, None, ("dp", "rep")),) + (P(),) * 11 + (nodes, nodes),
        out_specs=(P(None, ("dp", "rep")), P(), P(None, None, ("dp", "rep"))) + (P(),) * 11,
        check_vma=False,
    )
```

```python
import functools

import jax
import jax.numpy as jnp
from jax import lax
from jax.experimental import pallas as pl
from jax.experimental.pallas import tpu as pltpu
from jax.sharding import PartitionSpec as P

epsilon = 1e-05
axes = ("dp", "rep")
exact = lax.Precision.HIGHEST
f32 = jnp.float32
bf16 = jnp.bfloat16
LANES = 128
CHUNK = 256
PIECES = 16
HOP_ROWS = 104
HEAD_ROWS = 56
CLASS_ROWS = 48


def dot(left, right, precision=None):
    return lax.dot_general(
        left, right, (((1,), (0,)), ((), ())), precision=precision, preferred_element_type=f32
    )


def dot_nt(left, right, precision=None):
    return lax.dot_general(
        left, right, (((1,), (1,)), ((), ())), precision=precision, preferred_element_type=f32
    )


def split(values):
    high = values.astype(bf16)
    return high, (values - high.astype(f32)).astype(bf16)


def as_column(row):
    return jnp.broadcast_to(row, (LANES, row.shape[1])).T


def wide(column, width):
    return jnp.concatenate([column] * (width // LANES), axis=1)


def fold(values):
    total = values[:, :LANES]
    for start in range(LANES, values.shape[1], LANES):
        total = total + values[:, start : start + LANES]
    return total


def total_row(partial):
    return jnp.sum(partial.T, axis=0, keepdims=True)


def pad_rows(values, rows):
    return jnp.concatenate(
        [values, jnp.zeros((rows - values.shape[0], values.shape[1]), values.dtype)], axis=0
    )


def weave(products, slabs):
    done = 0
    for j, product in enumerate(products):
        until = (j + 1) * len(slabs) // len(products)
        for slab in slabs[done:until]:
            slab()
        done = until
        product()


def cost(flops=0, bytes_accessed=0):
    return pl.CostEstimate(flops=flops, bytes_accessed=bytes_accessed, transcendentals=0)


def call(kernel, mib, **options):
    return pl.pallas_call(
        kernel, compiler_params=pltpu.CompilerParams(vmem_limit_bytes=mib * 1024 * 1024), **options
    )


class Copies:
    def __init__(self, sems):
        self.sems = sems
        self.used = 0
        self.waiting = []

    def start(self, source, target):
        copy = pltpu.make_async_copy(source, target, self.sems.at[self.used])
        self.used += 1
        copy.start()
        return copy

    def send(self, source, target):
        self.waiting.append(self.start(source, target))

    def finish(self):
        for copy in self.waiting:
            copy.wait()


anywhere = pl.BlockSpec(memory_space=pl.ANY)
vmem = pl.BlockSpec(memory_space=pltpu.VMEM)
smem = pl.BlockSpec(memory_space=pltpu.SMEM)


def aligned(index, step):
    return pl.ds(pl.multiple_of(index * step, step), step)


def stats_kernel(
    x_hbm, w_hbm, mask_ref,
    pay_ref, gram_ref, xcat_hbm, w_out,
    x_scr, w_scr, xcat_ref, row_ref, sems,
):
    copies = Copies(sems)
    hops, feats, _ = x_scr.shape
    x_in, w_in = [], []
    for h in range(hops):
        x_in.append(copies.start(x_hbm.at[:, h, :], x_scr.at[h]))
        w_in.append(copies.start(w_hbm.at[:, h, :], w_scr.at[h]))
    keep = mask_ref[...].reshape(1, -1).astype(f32)
    count = jnp.sum(keep, axis=1, keepdims=True)
    safe = jnp.maximum(count, 1.0)
    row_ref[...] = jnp.zeros_like(row_ref)
    for h in range(hops):
        x_in[h].wait()
        x = x_scr[h]
        mean = jnp.sum(x * keep, axis=1, keepdims=True) / safe
        high, low = split(pad_rows(x - mean, LANES))
        xcat_ref[h, :LANES, :] = high
        xcat_ref[h, LANES:, :] = low
        copies.send(xcat_ref.at[h], xcat_hbm.at[h])
        w_in[h].wait()
        copies.send(w_scr.at[h], w_out.at[h])
        real = jnp.concatenate([high, low], axis=0) * keep.astype(bf16)
        gram = dot_nt(real, real)
        gram = (gram[:LANES, :LANES] + gram[LANES:, LANES:]) + (
            gram[:LANES, LANES:] + gram[LANES:, :LANES]
        )
        gram_ref[h] = gram
        w = pad_rows(w_scr[h], LANES)
        square = jnp.sum(dot(gram, w, exact) * w, axis=0, keepdims=True)
        tiles = w.shape[1] // LANES
        for i in range(tiles):
            row_ref[h * 5 + i : h * 5 + i + 1, :] = square[:, i * LANES : (i + 1) * LANES]
        mean = pad_rows(jnp.broadcast_to(mean, (feats, LANES)), LANES).T
        row_ref[h * 5 + 4 : h * 5 + 5, :] = mean[:1]
        row_ref[h * 5 + 4 : h * 5 + 5, LANES - 1 :] = count
    pay_ref[...] = jnp.broadcast_to(row_ref[...][None], pay_ref.shape)
    copies.finish()


def real_nodes(pay_ref):
    return pay_ref[:, 4, LANES - 1 :]


def feature_shift(pay_ref, h):
    means = pay_ref[:, h * 5 + 4, :]
    counts = means[:, LANES - 1 :]
    total = jnp.sum(counts, axis=0, keepdims=True)
    return means - jnp.sum(counts * means, axis=0, keepdims=True) / total


def prepare_kernel(xcat_hbm, w_ref, w2_hbm, pre_hbm, w2cat_hbm, xcat, w2, pre, w2cat, sems):
    copies = Copies(sems)
    hops, _, width = w_ref.shape
    nodes = xcat.shape[2]
    step = 2 * CHUNK
    quarter = width // 4
    ready = []
    for h in range(hops):
        ready.append(copies.start(xcat_hbm.at[h], xcat.at[h]))
        ready.append(copies.start(w2_hbm.at[h * width : (h + 1) * width, :], w2.at[h]))
    for h in range(hops):
        high, low = split(pad_rows(w_ref[h], LANES).T)
        wcat = jnp.concatenate(
            [jnp.concatenate([high, high], axis=1), jnp.concatenate([low, low], axis=1)], axis=0
        )

        def product(start):
            cols = slice(start, start + step)
            value = dot(wcat, xcat[h, :, cols])
            pre[h, :, cols] = value[:width] + value[width:]

        def turn(i):
            at = i * quarter
            high, low = split(w2[h, at : at + quarter, :].T)
            w2cat[h, :, at : at + quarter] = high
            w2cat[h, :, width + at : width + at + quarter] = low

        ready[2 * h].wait()
        ready[2 * h + 1].wait()
        weave(
            [functools.partial(product, start) for start in range(0, nodes, step)],
            [functools.partial(turn, i) for i in range(4)],
        )
        copies.send(pre.at[h], pre_hbm.at[h * width : (h + 1) * width, :])
        copies.send(w2cat.at[h], w2cat_hbm.at[h])
    copies.finish()


def columns_of(pack):
    rows = pack.shape[0]
    return [jnp.broadcast_to(pack[:, i : i + 1], (rows, LANES)) for i in range(6)]


def forward_kernel(
    code_ref, pay_ref, w_ref, gain_ref, bias_ref, slope1_ref, slope2_ref, mask_ref, pre_hbm, w2cat_hbm,
    mid_ref, stat_ref, inv_ref, colpack_ref, act_hbm,
    pre, w2cat, act, shift_ref, row_ref, sems,
):
    copies = Copies(sems)
    hops, _, width = w_ref.shape
    nodes = mid_ref.shape[1]
    ready = []
    for h in range(hops):
        rows = slice(h * width, (h + 1) * width)
        ready.append((
            copies.start(pre_hbm.at[rows, :], pre.at[h]),
            copies.start(w2cat_hbm.at[h], w2cat.at[h]),
        ))
    counts = real_nodes(pay_ref)
    total = jnp.sum(counts, axis=0, keepdims=True)
    for h in range(hops):
        shift = dot(feature_shift(pay_ref, h), pad_rows(w_ref[h], LANES), exact)
        shift_ref[h] = shift
        squares = rows_of(pay_ref, h * 5, width // LANES)
        square = jnp.sum(squares + counts * shift * shift, axis=0, keepdims=True)
        inverse = lax.rsqrt(square / total + epsilon)
        inv_ref[h] = inverse
        scale = 0.5 * gain_ref[h] * inverse
        rows = [
            scale,
            shift_ref[h, pl.ds(code_ref[0], 1), :] * scale + 0.5 * bias_ref[h],
            0.5 + 0.5 * slope1_ref[h],
            0.5 - 0.5 * slope1_ref[h],
            1.0 + slope2_ref[h],
            1.0 - slope2_ref[h],
        ]
        colpack_ref[h] = pad_rows(jnp.concatenate(rows, axis=0), LANES).T

    def slabs(h):
        rows = 16

        def slab(r):
            rs = slice(r, r + rows)
            columns = columns_of(colpack_ref[h, rs, :])
            scale, shift, p1, q1, p2, q2 = (wide(c, nodes) for c in columns)
            half = pre[h, rs, :] * scale + shift
            half = half * (p1 + q1 * jnp.tanh(half))
            high, low = split(half * (p2 + q2 * jnp.tanh(half)))
            act[h, 0, rs, :] = high
            act[h, 1, rs, :] = low

        return [functools.partial(slab, r) for r in range(0, width, rows)]

    def products(h):
        def product(start):
            cols = slice(start, start + CHUNK)
            high, low = act[h, 0, :, cols], act[h, 1, :, cols]
            w2_high, w2_low = w2cat[h, :, :width], w2cat[h, :, width:]
            value = dot(
                jnp.concatenate([w2_high, w2_high, w2_low], axis=1),
                jnp.concatenate([high, low, high], axis=0),
            )
            mid_ref[:, cols] = value if h == 0 else mid_ref[:, cols] + value

        return [functools.partial(product, start) for start in range(0, nodes, CHUNK)]

    for h in range(hops + 1):
        if h < hops:
            for copy in ready[h]:
                copy.wait()
        weave(products(h - 1) if h else [lambda: None], slabs(h) if h < hops else [])
        if h < hops:
            rows = slice(h * width, (h + 1) * width)
            copies.send(act.at[h, 0], act_hbm.at[0, rows, :])
            copies.send(act.at[h, 1], act_hbm.at[1, rows, :])
    keep = mask_ref[...].reshape(1, -1).astype(f32)
    count = jnp.maximum(jnp.sum(keep, axis=1, keepdims=True), 1.0)
    mid = mid_ref[...]
    average = total_row(fold(mid * keep)) / count
    off = mid - wide(as_column(average), nodes)
    square = total_row(fold(off * off * keep))
    put_rows(row_ref, average, square)
    stat_ref[...] = jnp.broadcast_to(row_ref[...][None], stat_ref.shape)
    copies.finish()


def put_rows(row_ref, *rows):
    at = 0
    for row in rows:
        for start in range(0, row.shape[1], LANES):
            row_ref[at : at + 1, :] = row[:, start : start + LANES]
            at += 1


def rows_of(ref, first, count):
    return jnp.concatenate([ref[:, i, :] for i in range(first, first + count)], axis=1)


def head_kernel(
    pay_ref, stat_ref, gain_ref, bias_ref, slope_ref, ow_ref, ob_ref, label_ref, mask_ref, mid_ref,
    logit_ref, inv_ref, sums_ref, misc_ref, up_ref, norm_ref,
    ow_scr, ob_scr, row_ref, half_ref, tan_ref, acat_ref, col_ref, back_ref, acc_ref, misc_scr,
):
    width, nodes = mid_ref.shape
    classes = ow_ref.shape[0]
    tiles = width // LANES
    counts = real_nodes(pay_ref)
    total = jnp.sum(counts, axis=0, keepdims=True)
    means = rows_of(stat_ref, 0, tiles)
    average = jnp.sum(counts * means, axis=0, keepdims=True) / total
    off = means - average
    square = jnp.sum(rows_of(stat_ref, tiles, tiles) + counts * off * off, axis=0, keepdims=True)
    inverse = lax.rsqrt(square / total + epsilon)
    inv_ref[...] = inverse
    col_ref[0] = as_column(average)
    col_ref[1] = as_column(inverse)
    col_ref[2] = 0.5 * as_column(gain_ref[...])
    col_ref[3] = 0.5 * as_column(bias_ref[...])
    slope = as_column(slope_ref[...])
    col_ref[4] = 0.5 + 0.5 * slope
    col_ref[5] = 0.5 - 0.5 * slope
    ow_scr[...] = jnp.zeros_like(ow_scr)
    ow_scr[:classes, :] = ow_ref[...]
    ow_t = split(ow_scr[:CLASS_ROWS, :])
    ow = split(ow_scr[...].T)
    ob_scr[...] = jnp.zeros_like(ob_scr)
    ob_scr[:, :classes] = ob_ref[...]
    ob_col = wide(as_column(ob_scr[...])[:CLASS_ROWS], nodes)
    rows = 16
    for r in range(0, width, rows):
        rs = slice(r, r + rows)
        mean, inv, gain, bias, p, q = (wide(col_ref[i, rs], nodes) for i in range(6))
        normed = (mid_ref[rs, :] - mean) * inv
        norm_ref[rs, :] = normed
        half = normed * gain + bias
        tangent = jnp.tanh(half)
        half_ref[rs, :] = half
        tan_ref[rs, :] = tangent
        high, low = split(2.0 * half * (p + q * tangent))
        acat_ref[rs, :] = high
        acat_ref[slice(width + r, width + r + rows), :] = low
    high, low = acat_ref[:width, :], acat_ref[width:, :]
    logits = dot(jnp.concatenate([ow_t[0], ow_t[0]], axis=1), acat_ref[...]) + dot(ow_t[1], high)
    logits = logits + ob_col
    logit_ref[...] = logits[:classes]
    keep = mask_ref[...].reshape(1, -1).astype(f32)
    place = lax.broadcasted_iota(jnp.int32, (CLASS_ROWS, nodes), 0)
    logits = jnp.where(place < classes, logits, -3.0e38)
    shifted = logits - jnp.max(logits, axis=0, keepdims=True)
    weights = jnp.exp(shifted)
    norm = jnp.sum(weights, axis=0, keepdims=True)
    onehot = place == label_ref[...].reshape(1, -1)
    picked = jnp.sum(jnp.where(onehot, shifted, 0.0), axis=0, keepdims=True)
    loss = jnp.sum(fold(keep * (jnp.log(norm) - picked)), axis=1, keepdims=True)
    grad = keep * (weights * (1.0 / norm) - jnp.where(onehot, 1.0, 0.0))
    grad_sum = fold(grad)
    grad_high, grad_low = split(pad_rows(grad, LANES))
    gcat = jnp.concatenate([grad_high, grad_low, grad_high], axis=0)
    owcat = jnp.concatenate([ow[0], ow[0], ow[1]], axis=1)

    def back(start):
        back_ref[:, start : start + CHUNK] = dot(owcat, gcat[:, start : start + CHUNK])

    for start in range(0, nodes, CHUNK):
        back(start)
    both = jnp.concatenate([grad_high, grad_low], axis=0)

    def weight_grad():
        value = dot_nt(both, high)
        value = value[:CLASS_ROWS] + value[LANES : LANES + CLASS_ROWS]
        misc_scr[:CLASS_ROWS, :] = value + dot_nt(grad_high[:CLASS_ROWS], low)

    def slab(r):
        rs = slice(r, r + rows)
        p, q = wide(col_ref[4, rs], nodes), wide(col_ref[5, rs], nodes)
        half, tangent, act_grad = half_ref[rs, :], tan_ref[rs, :], back_ref[rs, :]
        away = half * (1.0 - tangent)
        acc_ref[0, rs] = fold(act_grad * away)
        up = act_grad * (p + q * (tangent + away * (1.0 + tangent)))
        up_ref[rs, :] = up
        acc_ref[1, rs] = fold(up)
        acc_ref[2, rs] = fold(up * norm_ref[rs, :])

    slabs = [functools.partial(slab, r) for r in range(0, width, rows)]
    weave([weight_grad, lambda: None], slabs)
    put_rows(row_ref, total_row(acc_ref[1]), total_row(acc_ref[2]))
    sums_ref[...] = jnp.broadcast_to(row_ref[...][None], sums_ref.shape)
    misc_scr[CLASS_ROWS:, :] = jnp.zeros((HEAD_ROWS - CLASS_ROWS, width), f32)
    misc_scr[CLASS_ROWS : CLASS_ROWS + 1, :] = total_row(acc_ref[0])
    misc_scr[CLASS_ROWS + 1 : CLASS_ROWS + 2, :LANES] = total_row(pad_rows(grad_sum, LANES))
    misc_scr[CLASS_ROWS + 2 : CLASS_ROWS + 3, :1] = loss
    for t in range(tiles):
        misc_ref[t] = misc_scr[:, t * LANES : (t + 1) * LANES]


def mid_grad_kernel(
    code_ref, pay_ref, sums_ref, inv_ref, gain_ref, mask_ref, up_ref, norm_ref, act_hbm,
    out_ref, bg_ref, gcat,
    act, sems,
):
    width, nodes = up_ref.shape
    ready = act_in(1, code_ref, Copies(sems), act_hbm, act)
    tiles = width // LANES
    total = jnp.sum(real_nodes(pay_ref), axis=0, keepdims=True)
    bias_sum = jnp.sum(rows_of(sums_ref, 0, tiles), axis=0, keepdims=True)
    gain_sum = jnp.sum(rows_of(sums_ref, tiles, tiles), axis=0, keepdims=True)
    bg_ref[0:1, :] = bias_sum
    bg_ref[1:2, :] = gain_sum
    scale = as_column(gain_ref[...] * inv_ref[...])
    bias_col = as_column(bias_sum / total)
    gain_col = as_column(gain_sum / total)
    keep = mask_ref[...].reshape(1, -1).astype(f32)
    rows = 16
    for r in range(0, width, rows):
        rs = slice(r, r + rows)
        bias, gain = wide(bias_col[rs], nodes), wide(gain_col[rs], nodes)
        grad = up_ref[rs, :] - bias - norm_ref[rs, :] * gain
        high, low = split(keep * (wide(scale[rs], nodes) * grad))
        gcat[rs, :] = high
        gcat[width + r : width + r + rows, :] = low
    mid_product(code_ref, ready, act, gcat, out_ref)


def act_in(half_sel, code_ref, copies, act_hbm, act):
    parts, _, width, _ = act.shape
    rows = width // 2
    ready = []
    for s in range(parts):
        for r in (0, 1):
            block = (s * 2 + (half_sel ^ (code_ref[s] >> 4))) * 2 + r
            ready.append([
                copies.start(act_hbm.at[i, aligned(block, rows)], act.at[s, i, r * rows : (r + 1) * rows])
                for i in (0, 1)
            ])
    return ready


def mid_product(code_ref, ready, act, gcat, out_ref):
    parts, width, mid = out_ref.shape
    rows = width // PIECES
    size = width // 2
    for s in range(parts):
        code = code_ref[s] & (PIECES - 1)
        for r in (0, 1):
            for copy in ready[s * 2 + r]:
                copy.wait()
            here = slice(r * size, (r + 1) * size)
            value = dot_nt(act[s, 0, here, :], gcat[:mid, :])
            value = value + dot_nt(act[s, 0, here, :], gcat[mid:, :])
            value = value + dot_nt(act[s, 1, here, :], gcat[:mid, :])
            for i in range(size // rows):
                place = (r * (size // rows) + i) ^ code
                out_ref[s, aligned(place, rows), :] = value[i * rows : (i + 1) * rows]


def mid_grad_rest_kernel(code_ref, gcat, act_hbm, out_ref, act, sems):
    ready = act_in(0, code_ref, Copies(sems), act_hbm, act)
    mid_product(code_ref, ready, act, gcat, out_ref)


def backward_kernel(
    code_ref, pay_ref, inv_ref, gain_ref, bias_ref, colpack_ref, w_ref, gram_ref, misc_ref,
    g, w2_hbm, pre_hbm, xcat_hbm,
    pack_ref, feat_hbm,
    w2, pre, xcat, feat, col, down, ucat, acc, prod, rows_scr, sems,
):
    copies = Copies(sems)
    hops, feats, width = w_ref.shape
    mid, nodes = g.shape[0] // 2, g.shape[1]
    tiles = mid // LANES
    size = 2 * CHUNK
    chunks = [slice(start, start + size) for start in range(0, nodes, size)]
    count = len(chunks)
    stages = [(h, j) for h in range(hops) for j in range(count)]
    w_in, z_in, x_in = {}, {}, {}
    for h in range(hops):
        own = slice(h * width, (h + 1) * width)
        w_in[h] = copies.start(w2_hbm.at[own, :], w2.at[h])
        for j, c in enumerate(chunks):
            z_in[h, j] = copies.start(pre_hbm.at[own, c], pre.at[h, :, c])
        x_in[h] = copies.start(xcat_hbm.at[h], xcat.at[h])
    devices = pay_ref.shape[0]
    flip = code_ref[1] * (tiles // 2)
    at = hops * HOP_ROWS
    for t in range(tiles):
        pack_ref[t ^ flip, at : at + HEAD_ROWS, :] = misc_ref[t]
    w2cat, wcat = {}, {}

    def columns(h):
        rows = 64
        for r in range(0, width, rows):
            for k, values in enumerate(columns_of(colpack_ref[h, r : r + rows, :])):
                col[h % 2, k, r : r + rows, :] = values
        acc[h % 2] = jnp.zeros(acc.shape[1:], f32)

    def weights(h):
        high, low = split(pad_rows(w_ref[h], LANES) * (gain_ref[h] * inv_ref[h]))
        wcat[h] = (jnp.concatenate([high, low], axis=0), high)
        high, low = split(0.5 * w2[h])
        w2cat[h] = jnp.concatenate([high, high, low], axis=1)

    def part_of(j, part):
        return slice(chunks[j].start + part * CHUNK, chunks[j].start + (part + 1) * CHUNK)

    def down_product(index, part):
        h, j = stages[index]
        cs = part_of(j, part)
        high, low = g[:mid, cs], g[mid:, cs]
        value = dot(w2cat[h], jnp.concatenate([high, low, high], axis=0))
        down[index % 2, :, part * CHUNK : (part + 1) * CHUNK] = value

    def slab(index, r, rows):
        h, j = stages[index]
        two = h % 2
        rs, cs = slice(r, r + rows), chunks[j]
        scale, shift, p1, q1, p2, q2 = (wide(col[two, k, rs], size) for k in range(6))
        half1 = pre[h, rs, cs] * scale + shift
        grad2 = down[index % 2, rs, :]
        tan1 = jnp.tanh(half1)
        half2 = half1 * (p1 + q1 * tan1)
        tan2 = jnp.tanh(half2)
        away2 = half2 * (1.0 - tan2)
        acc[two, 0, rs] += fold(grad2 * away2)
        grad1 = grad2 * (p2 + q2 * (tan2 + away2 * (1.0 + tan2)))
        away1 = half1 * (1.0 - tan1)
        acc[two, 1, rs] += fold(grad1 * away1)
        grad = grad1 * (p1 + q1 * (tan1 + away1 * (1.0 + tan1)))
        acc[two, 2, rs] += fold(grad)
        acc[two, 3, rs] += fold(grad * half1)
        high, low = split(grad)
        ucat[two, rs, cs] = high
        ucat[two, width + r : width + r + rows, cs] = low

    def feature_product(index, part):
        h, j = stages[index]
        cs = part_of(j, part)
        value = dot(wcat[h][0], ucat[h % 2, :width, cs])
        value = value[:LANES] + value[LANES:] + dot(wcat[h][1], ucat[h % 2, width:, cs])
        feat[h, :, cs] = value[:feats]

    def weight_product(h):
        value = dot_nt(xcat[h], ucat[h % 2, :width, :])
        low = dot_nt(xcat[h, :LANES, :], ucat[h % 2, width:, :])
        prod[h % 2] = value[:LANES] + value[LANES:] + low

    def pack(h):
        two = h % 2
        bias_sum = total_row(acc[two, 2])
        shift = feature_shift(pay_ref, h)
        rows_scr[:devices, :] = shift
        rows_scr[devices:, :] = jnp.broadcast_to(real_nodes(pay_ref), shift.shape)
        own_shift = rows_scr[pl.ds(code_ref[0], 1), :]
        own_count = rows_scr[pl.ds(devices + code_ref[0], 1), :]
        column = as_column(own_shift)
        prod[two] = prod[two] + wide(column, mid) * bias_sum
        prod[two, feats : feats + 1, :] = total_row(acc[two, 1])
        prod[two, feats + 1 : feats + 2, :] = 2.0 * total_row(acc[two, 0])
        prod[two, feats + 2 : feats + 3, :] = bias_sum
        prod[two, feats + 3 : feats + 4, :] = (
            2.0 * total_row(acc[two, 3]) - bias_ref[h] * bias_sum
        ) / gain_ref[h]
        for t in range(tiles):
            pack_ref[t ^ flip, h * HOP_ROWS : (h + 1) * HOP_ROWS, :] = prod[
                two, :HOP_ROWS, t * LANES : (t + 1) * LANES
            ]
        gram = gram_ref[h] + column * (own_shift * own_count)
        pack_ref[h ^ flip, at + HEAD_ROWS :, :] = gram[:HOP_ROWS]

    rows = 16
    columns(0)
    w_in[0].wait()
    weights(0)
    for part in (0, 1):
        down_product(0, part)
    for index, (h, j) in enumerate(stages):
        products = []
        z_in[h, j].wait()
        if j + 1 == count:
            x_in[h].wait()
            if h + 1 < hops:
                w_in[h + 1].wait()
                weights(h + 1)
                columns(h + 1)
        if index + 1 < len(stages):
            products += [functools.partial(down_product, index + 1, part) for part in (0, 1)]
        if index >= 1:
            products += [functools.partial(feature_product, index - 1, part) for part in (0, 1)]
        if j == 0 and h >= 1:
            products.append(functools.partial(weight_product, h - 1))
        if j == 1 and h >= 1:
            copies.send(feat.at[h - 1], feat_hbm.at[h - 1])
            pack(h - 1)
        weave(products, [functools.partial(slab, index, r, rows) for r in range(0, width, rows)])
    for part in (0, 1):
        feature_product(len(stages) - 1, part)
    copies.send(feat.at[hops - 1], feat_hbm.at[hops - 1])
    weight_product(hops - 1)
    pack(hops - 1)
    copies.finish()


def finish_kernel(
    code_ref, pay_ref, inv_ref, mine_ref, other_ref, w_ref, gain_ref, mask_ref, bg_ref, xcat_hbm,
    feat_hbm, fgrad_hbm, wgrad_hbm, gain_out, bias_out, slope1_out, slope2_out, mgain_out, mbias_out, mslope_out,
    owg_out, obg_out, loss_out,
    sum_ref, rows_scr, fgrad, wgrad, feat, xcat, sems,
):
    hops, feats, width = w_ref.shape
    tiles = mine_ref.shape[0] * 2
    half = tiles // 2
    flip = code_ref[1]
    copies = Copies(sems)
    ready = []
    for h in range(hops):
        ready.append((copies.start(feat_hbm.at[h], feat.at[h]), copies.start(xcat_hbm.at[h], xcat.at[h])))

    @pl.when(flip == 0)
    def _():
        for t in range(half):
            sum_ref[:, t * LANES : (t + 1) * LANES] = mine_ref[t]
            sum_ref[:, (half + t) * LANES : (half + t + 1) * LANES] = other_ref[t]

    @pl.when(flip != 0)
    def _():
        for t in range(half):
            sum_ref[:, t * LANES : (t + 1) * LANES] = other_ref[t]
            sum_ref[:, (half + t) * LANES : (half + t + 1) * LANES] = mine_ref[t]

    counts = real_nodes(pay_ref)
    total = jnp.sum(counts, axis=0, keepdims=True)
    keep = mask_ref[...].reshape(1, -1).astype(f32)
    at = hops * HOP_ROWS
    for h in range(hops):
        base = h * HOP_ROWS
        w = pad_rows(w_ref[h], LANES)
        inverse = inv_ref[h]
        scale = gain_ref[h] * inverse
        slope1_out[h] = sum_ref[base + feats : base + feats + 1, :]
        slope2_out[h] = sum_ref[base + feats + 1 : base + feats + 2, :]
        bias_sum = sum_ref[base + feats + 2 : base + feats + 3, :]
        gain_sum = sum_ref[base + feats + 3 : base + feats + 4, :]
        bias_out[h] = bias_sum
        gain_out[h] = gain_sum
        gram = sum_ref[at + HEAD_ROWS : at + HEAD_ROWS + HOP_ROWS, h * LANES : (h + 1) * LANES]
        inner = dot(gram, w, exact)[:feats] * (inverse * gain_sum / total)
        wgrad[h] = scale * (sum_ref[base : base + feats, :] - inner)
        copies.send(wgrad.at[h], wgrad_hbm.at[:, h, :])
        shift = feature_shift(pay_ref, h)
        rows_scr[...] = shift
        own_shift = rows_scr[pl.ds(code_ref[0], 1), :]
        mix = dot_nt(w * (scale * inverse * gain_sum / total), w, exact)
        lane = lax.broadcasted_iota(jnp.int32, (1, LANES), 1)
        off = jnp.sum(w * (scale * bias_sum / total), axis=1, keepdims=True)
        off = off + jnp.sum(mix * jnp.where(lane < feats, own_shift, 0.0), axis=1, keepdims=True)
        high, low = split(mix)
        for copy in ready[h]:
            copy.wait()
        mixed = dot(jnp.concatenate([high, high], axis=1), xcat[h]) + dot(low, xcat[h, :LANES])
        fgrad[h] = keep * (feat[h] - (mixed + off)[:feats])
        copies.send(fgrad.at[h], fgrad_hbm.at[:, h, :])
    owg_out[...] = sum_ref[at : at + owg_out.shape[0], :]
    mslope_out[...] = sum_ref[at + CLASS_ROWS : at + CLASS_ROWS + 1, :]
    obg_out[...] = sum_ref[at + CLASS_ROWS + 1 : at + CLASS_ROWS + 2, : obg_out.shape[1]]
    loss_out[...] = sum_ref[at + CLASS_ROWS + 2 : at + CLASS_ROWS + 3, :1] / total
    mbias_out[...] = bg_ref[0:1, :]
    mgain_out[...] = bg_ref[1:2, :]
    copies.finish()


def place_kernel(pieces, code_ref, *refs):
    out_ref, sems = refs[-2:]
    copies = Copies(sems)
    for ref, (s, first, rows) in zip(refs, pieces):
        for i in range(ref.shape[0] // rows):
            block = s * 2 * PIECES + ((first + i) ^ code_ref[s])
            copies.send(ref.at[pl.ds(i * rows, rows)], out_ref.at[aligned(block, rows)])
    copies.finish()


def exchange(values, bit, devices):
    return lax.ppermute(values, axes, [(i, i ^ (1 << bit)) for i in range(devices)])


def exchange_two(a, bit_a, b, bit_b, devices):
    a, b = lax.optimization_barrier((a, b))
    return lax.optimization_barrier((exchange(a, bit_a, devices), exchange(b, bit_b, devices)))


def swap_halves(a, bit_a, b, bit_b, devices):
    size = a.shape[0] // 2
    ra, rb = exchange_two(a[size:], bit_a, b[size:], bit_b, devices)
    return a[:size] + ra, b[:size] + rb


def code_of(me, order):
    code = 0
    for bit in order:
        code = code * 2 + ((me >> bit) & 1)
    return code


def after(values, *others):
    return lax.optimization_barrier((values, *others))[0]


def on_device(
    devices,
    hop_features,
    branch_weight,
    branch_gain,
    branch_bias,
    first_slope,
    second_slope,
    mid_weight,
    mid_gain,
    mid_bias,
    mid_slope,
    out_weight,
    out_bias,
    labels,
    valid_mask,
):
    hops, feats, nodes = hop_features.shape
    width = branch_weight.shape[2]
    mid = mid_weight.shape[1]
    classes = out_weight.shape[1]
    tiles = mid // LANES
    bits = devices.bit_length() - 1
    me = lax.axis_index(axes).astype(jnp.int32)
    rest = tuple(range(5, bits))
    codes = jnp.stack([code_of(me, (0, 1, 2, 3, 4)), code_of(me, (0, 2, 1, 3, 4))])
    place_code = jnp.stack([me, me & 1])
    shape = jax.ShapeDtypeStruct
    by_hop = lambda v: v.reshape(hops, 1, width)
    gain, bias, slope1, slope2 = map(by_hop, (branch_gain, branch_bias, first_slope, second_slope))
    row = lambda v: v.reshape(1, -1)
    gather = functools.partial(
        lax.all_to_all, axis_name=axes, split_axis=0, concat_axis=0, tiled=True
    )
    dma = pltpu.SemaphoreType.DMA
    scratch = lambda dtype, *dims: pltpu.VMEM(dims, dtype)
    mask = valid_mask

    pay, gram, xcat, w = call(
        stats_kernel,
        60,
        in_specs=[anywhere, anywhere, vmem],
        out_specs=[vmem, vmem, anywhere, anywhere],
        out_shape=(
            shape((devices, 24, LANES), f32), shape((hops, LANES, LANES), f32),
            shape((hops, 2 * LANES, nodes), bf16), shape((hops, feats, width), f32),
        ),
        scratch_shapes=[
            scratch(f32, hops, feats, nodes), scratch(f32, hops, feats, width),
            scratch(bf16, hops, 2 * LANES, nodes), scratch(f32, 24, LANES), dma((4 * hops,)),
        ],
        cost_estimate=cost(1_000_000_000, 8_000_000),
        name="first_stats",
    )(jnp.transpose(hop_features, (1, 0, 2)), jnp.transpose(branch_weight, (1, 0, 2)), mask)
    pay = gather(after(pay, codes, place_code))

    pre, w2cat = call(
        prepare_kernel,
        60,
        in_specs=[anywhere, vmem, anywhere],
        out_specs=[anywhere] * 2,
        out_shape=(shape((hops * width, nodes), f32), shape((hops, mid, 2 * width), bf16)),
        scratch_shapes=[
            scratch(bf16, hops, 2 * LANES, nodes), scratch(f32, hops, width, mid),
            scratch(f32, hops, width, nodes), scratch(bf16, hops, mid, 2 * width), dma((4 * hops,)),
        ],
        cost_estimate=cost(4 * 2 * 4 * hops * LANES * width * nodes, 20_000_000),
        name="prepare",
    )(xcat, w, mid_weight)

    mid_pre, stat, first_inv, colpack, act = call(
        forward_kernel,
        45,
        in_specs=[smem] + [vmem] * 7 + [anywhere] * 2,
        out_specs=[vmem] * 4 + [anywhere],
        out_shape=(
            shape((mid, nodes), f32), shape((devices, 8, LANES), f32), shape((hops, 1, width), f32),
            shape((hops, width, LANES), f32), shape((2, hops * width, nodes), bf16),
        ),
        scratch_shapes=[
            scratch(f32, hops, width, nodes), scratch(bf16, hops, mid, 2 * width),
            scratch(bf16, hops, 2, width, nodes), scratch(f32, hops, devices, width),
            scratch(f32, 8, LANES), dma((4 * hops,)),
        ],
        cost_estimate=cost(3 * 2 * hops * width * mid * nodes, 20_000_000),
        name="forward",
    )(place_code, pay, w, gain, bias, slope1, slope2, mask, pre, w2cat)
    stat = gather(stat)

    logits, mid_inv, sums, misc, up, normed = call(
        head_kernel,
        40,
        in_specs=[vmem] * 10,
        out_specs=[vmem] * 6,
        out_shape=(
            shape((classes, nodes), f32), shape((1, mid), f32), shape((devices, 8, LANES), f32),
            shape((tiles, HEAD_ROWS, LANES), f32), shape((mid, nodes), f32), shape((mid, nodes), f32),
        ),
        scratch_shapes=[
            scratch(f32, LANES, mid), scratch(f32, 1, LANES), scratch(f32, 8, LANES),
            scratch(f32, mid, nodes), scratch(f32, mid, nodes), scratch(bf16, 2 * mid, nodes),
            scratch(f32, 6, mid, LANES), scratch(f32, mid, nodes), scratch(f32, 3, mid, LANES),
            scratch(f32, HEAD_ROWS, mid),
        ],
        cost_estimate=cost(2_000_000_000, 10_000_000),
        name="head",
    )(pay, stat, row(mid_gain), row(mid_bias), row(mid_slope), out_weight.T, row(out_bias), labels, mask, mid_pre)
    sums = gather(sums)

    product_cost = cost(2 * 3 * 2 * width * mid * nodes, 10_000_000)
    send, mid_bg, gcat = call(
        mid_grad_kernel,
        36,
        in_specs=[smem] + [vmem] * 7 + [anywhere],
        out_specs=[vmem] * 3,
        out_shape=(
            shape((2, width, mid), f32), shape((2, mid), f32), shape((2 * mid, nodes), bf16),
        ),
        scratch_shapes=[scratch(bf16, 2, 2, width, nodes), dma((8,))],
        cost_estimate=product_cost,
        name="mid_grad_send",
    )(codes, pay, sums, mid_inv, row(mid_gain), mask, up, normed, act)
    came = exchange(send, 0, devices)
    kept = call(
        mid_grad_rest_kernel,
        40,
        in_specs=[smem, vmem, anywhere],
        out_specs=vmem,
        out_shape=shape((2, width, mid), f32),
        scratch_shapes=[scratch(bf16, 2, 2, width, nodes), dma((8,))],
        cost_estimate=product_cost,
        name="mid_grad_keep",
    )(codes, gcat, act)

    pack_rows = hops * HOP_ROWS + HEAD_ROWS + HOP_ROWS

    def backward(gcat):
        return call(
            backward_kernel,
            52,
            in_specs=[smem] + [vmem] * 9 + [anywhere] * 3,
            out_specs=[vmem, anywhere],
            scratch_shapes=[
                scratch(f32, hops, width, mid), scratch(f32, hops, width, nodes),
                scratch(bf16, hops, 2 * LANES, nodes),
                scratch(f32, hops, feats, nodes), scratch(f32, 2, 6, width, LANES),
                scratch(f32, 2, width, 2 * CHUNK), scratch(bf16, 2, 2 * width, nodes),
                scratch(f32, 2, 4, width, LANES), scratch(f32, 2, LANES, mid),
                scratch(f32, 2 * devices, LANES), dma((3 * hops + (hops + 1) * nodes // CHUNK,)),
            ],
            out_shape=(shape((tiles, pack_rows, LANES), f32), shape((hops, feats, nodes), f32)),
            cost_estimate=cost(hops * 2 * 4 * width * mid * nodes, 24_000_000),
            name="backward",
        )(place_code, pay, first_inv, gain, bias, colpack, w, gram, misc, gcat, mid_weight, pre, xcat)

    a, b = kept[0] + came[0], kept[1] + came[1]
    size = a.shape[0] // 2
    send_a, send_b = a[size:], b[size:]
    ra = exchange(send_a, 1, devices)
    rb = exchange(send_b, 2, devices)
    pack, feat = backward(after(gcat, send_a, send_b))
    a, b = a[:size] + after(ra, pack), b[:size] + after(rb, pack)

    half = tiles // 2
    groups = {}
    for i in range(devices):
        groups.setdefault(i & ~14, []).append(i)
    spread = functools.partial(
        lax.all_to_all, axis_name=axes, split_axis=0, concat_axis=0,
        axis_index_groups=list(groups.values()), tiled=True,
    )
    pack = after(pack, a, b)
    pack = pack[:half] + exchange(pack[half:], 0, devices)
    a, b, pack = lax.optimization_barrier((a, b, pack))
    a, b = swap_halves(a, 2, b, 1, devices)
    pack = spread(pack.reshape(8, -1, LANES))
    part = a.shape[0] // 4
    both = jnp.stack([a.reshape(4, part, mid), b.reshape(4, part, mid)], axis=1)
    both = both[:2] + exchange(both[2:], 3, devices)
    pack = pack.sum(axis=0)
    pack, both = lax.optimization_barrier((pack, both))
    came, pack_came = lax.optimization_barrier(
        (exchange(both[1:], 4, devices), exchange(pack, 4, devices))
    )
    both, pack = both[:1] + came, pack + pack_came
    for bit in rest:
        both, pack = both + exchange(both, bit, devices), pack + exchange(pack, bit, devices)
    pack = jnp.broadcast_to(pack[None], (8,) + pack.shape)
    pack, both = lax.optimization_barrier((pack, both))
    pack = spread(pack).reshape(half, pack_rows, LANES)
    both = jnp.concatenate([both, exchange(both, 4, devices)])
    both = jnp.concatenate([both, exchange(both, 3, devices)])
    a, b = both[:, 0].reshape(-1, mid), both[:, 1].reshape(-1, mid)
    ra, rb = exchange_two(a, 2, b, 1, devices)
    a, b = jnp.concatenate([a, ra]), jnp.concatenate([b, rb])
    a, b = lax.optimization_barrier((a, b))
    ra, rb = exchange(a, 1, devices), exchange(b, 2, devices)
    other_a, other_b = exchange(a, 0, devices), exchange(b, 0, devices)
    pack_other = exchange(pack, 0, devices)

    rows_out = [shape((hops, 1, width), f32)] * 4
    rows_mid = [shape((1, mid), f32)] * 3
    (
        feature_grad, branch_weight_grad, branch_gain_grad, branch_bias_grad, first_slope_grad,
        second_slope_grad, mid_gain_grad, mid_bias_grad, mid_slope_grad, out_weight_grad,
        out_bias_grad, mean_loss,
    ) = call(
        finish_kernel,
        60,
        in_specs=[smem] + [vmem] * 8 + [anywhere] * 2,
        out_specs=[anywhere, anywhere] + [vmem] * 10,
        scratch_shapes=[
            scratch(f32, pack_rows, mid), scratch(f32, devices, LANES), scratch(f32, hops, feats, nodes),
            scratch(f32, hops, feats, width), scratch(f32, hops, feats, nodes),
            scratch(bf16, hops, 2 * LANES, nodes), dma((4 * hops,)),
        ],
        out_shape=(
            shape((feats, hops, nodes), f32), shape((feats, hops, width), f32), *rows_out, *rows_mid,
            shape((classes, mid), f32), shape((1, classes), f32), shape((1, 1), f32),
        ),
        cost_estimate=cost(0, 20_000_000),
        name="finish",
    )(place_code, pay, first_inv, pack, pack_other, w, gain, mask, mid_bg, xcat, feat)

    rows = mid_weight.shape[0] // (4 * PIECES)
    eight = PIECES // 2

    def place(pieces, *base):
        values = [value for value, *_ in pieces]
        kinds = [(s, first, rows) for _, s, first in pieces]
        return call(
            functools.partial(place_kernel, kinds),
            16,
            in_specs=[smem] + [vmem] * len(values) + [anywhere] * len(base),
            out_specs=anywhere,
            scratch_shapes=[dma((len(values) * eight,))],
            out_shape=shape(mid_weight.shape, f32),
            input_output_aliases={1 + len(values): 0} if base else {},
            cost_estimate=cost(0, 4_000_000),
            name="place",
        )(codes, *values, *base)

    grad = place(
        [(a, 0, 0), (b, 1, 0), (other_a, 0, PIECES), (after(other_b, mid_bias_grad), 1, PIECES)]
    )
    ra, rb, grad = lax.optimization_barrier((ra, rb, grad))
    other_ra, other_rb = exchange(ra, 0, devices), exchange(rb, 0, devices)
    grad = place([(ra, 0, eight), (rb, 1, eight)], grad)
    mid_weight_grad = place(
        [(other_ra, 0, PIECES + eight), (after(other_rb, grad), 1, PIECES + eight)], grad
    )

    flat = lambda v: v.reshape(-1)
    return (
        logits,
        mean_loss.reshape(()),
        jnp.transpose(feature_grad, (1, 0, 2)),
        jnp.transpose(branch_weight_grad, (1, 0, 2)),
        flat(branch_gain_grad),
        flat(branch_bias_grad),
        flat(first_slope_grad),
        flat(second_slope_grad),
        mid_weight_grad,
        flat(mid_gain_grad),
        flat(mid_bias_grad),
        flat(mid_slope_grad),
        out_weight_grad.T,
        flat(out_bias_grad),
    )


def solution(mesh):
    devices = mesh.shape["dp"] * mesh.shape["rep"]

    def body(*arrays):
        return on_device(devices, *arrays)

    nodes = P(("dp", "rep"))
    return jax.shard_map(
        body,
        mesh=mesh,
        in_specs=(P(None, None, ("dp", "rep")),) + (P(),) * 11 + (nodes, nodes),
        out_specs=(P(None, ("dp", "rep")), P(), P(None, None, ("dp", "rep"))) + (P(),) * 11,
        check_vma=False,
    )
```

```python
import functools

import jax
import jax.numpy as jnp
from jax import lax
from jax.experimental import pallas as pl
from jax.experimental.pallas import tpu as pltpu
from jax.sharding import PartitionSpec as P

epsilon = 1e-05
axes = ("dp", "rep")
exact = lax.Precision.HIGHEST
f32 = jnp.float32
bf16 = jnp.bfloat16
LANES = 128
CHUNK = 256
PIECES = 16
HOP_ROWS = 104
HEAD_ROWS = 56
CLASS_ROWS = 48


def dot(left, right, precision=None):
    return lax.dot_general(
        left, right, (((1,), (0,)), ((), ())), precision=precision, preferred_element_type=f32
    )


def dot_nt(left, right, precision=None):
    return lax.dot_general(
        left, right, (((1,), (1,)), ((), ())), precision=precision, preferred_element_type=f32
    )


def split(values):
    high = values.astype(bf16)
    return high, (values - high.astype(f32)).astype(bf16)


def as_column(row):
    return jnp.broadcast_to(row, (LANES, row.shape[1])).T


def wide(column, width):
    return jnp.concatenate([column] * (width // LANES), axis=1)


def fold(values):
    total = values[:, :LANES]
    for start in range(LANES, values.shape[1], LANES):
        total = total + values[:, start : start + LANES]
    return total


def total_row(partial):
    return jnp.sum(partial.T, axis=0, keepdims=True)


def pad_rows(values, rows):
    return jnp.concatenate(
        [values, jnp.zeros((rows - values.shape[0], values.shape[1]), values.dtype)], axis=0
    )


def weave(products, slabs):
    done = 0
    for j, product in enumerate(products):
        until = (j + 1) * len(slabs) // len(products)
        for slab in slabs[done:until]:
            slab()
        done = until
        product()


def cost(flops=0, bytes_accessed=0):
    return pl.CostEstimate(flops=flops, bytes_accessed=bytes_accessed, transcendentals=0)


def call(kernel, mib, **options):
    return pl.pallas_call(
        kernel, compiler_params=pltpu.CompilerParams(vmem_limit_bytes=mib * 1024 * 1024), **options
    )


class Copies:
    def __init__(self, sems):
        self.sems = sems
        self.used = 0
        self.waiting = []

    def start(self, source, target):
        copy = pltpu.make_async_copy(source, target, self.sems.at[self.used])
        self.used += 1
        copy.start()
        return copy

    def send(self, source, target):
        self.waiting.append(self.start(source, target))

    def finish(self):
        for copy in self.waiting:
            copy.wait()


anywhere = pl.BlockSpec(memory_space=pl.ANY)
vmem = pl.BlockSpec(memory_space=pltpu.VMEM)
smem = pl.BlockSpec(memory_space=pltpu.SMEM)


def aligned(index, step):
    return pl.ds(pl.multiple_of(index * step, step), step)


def stats_kernel(
    x_hbm, w_hbm, mask_ref,
    pay_ref, gram_ref, xcat_hbm, w_out,
    x_scr, w_scr, xcat_ref, row_ref, sems,
):
    copies = Copies(sems)
    hops, feats, _ = x_scr.shape
    x_in, w_in = [], []
    for h in range(hops):
        x_in.append(copies.start(x_hbm.at[:, h, :], x_scr.at[h]))
        w_in.append(copies.start(w_hbm.at[:, h, :], w_scr.at[h]))
    keep = mask_ref[...].reshape(1, -1).astype(f32)
    count = jnp.sum(keep, axis=1, keepdims=True)
    safe = jnp.maximum(count, 1.0)
    row_ref[...] = jnp.zeros_like(row_ref)
    means, grams = [], []
    place = lax.broadcasted_iota(jnp.int32, (LANES, x_scr.shape[2]), 0)
    for h in range(hops):
        x_in[h].wait()
        x = x_scr[h]
        means.append(jnp.sum(x * keep, axis=1, keepdims=True) / safe)
        high, low = split(jnp.where(place == feats, 1.0, pad_rows(x - means[h], LANES)))
        xcat_ref[h, :LANES, :] = high
        xcat_ref[h, LANES:, :] = low
        copies.send(xcat_ref.at[h], xcat_hbm.at[h])
    for h in range(hops):
        real = xcat_ref[h] * keep.astype(bf16)
        gram = dot_nt(real, real)
        grams.append(
            (gram[:LANES, :LANES] + gram[LANES:, LANES:]) + (gram[:LANES, LANES:] + gram[LANES:, :LANES])
        )
        gram_ref[h] = grams[h]
    for h in range(hops):
        w_in[h].wait()
        copies.send(w_scr.at[h], w_out.at[h])
    for h in range(hops):
        w = pad_rows(w_scr[h], LANES)
        width = w.shape[1]
        row_ref[h : h + 1, :width] = jnp.sum(dot(grams[h], w, exact) * w, axis=0, keepdims=True)
        mean = pad_rows(jnp.broadcast_to(means[h], (feats, LANES)), LANES).T
        row_ref[h : h + 1, width:] = mean[:1]
        row_ref[h : h + 1, width + LANES - 1 :] = count
    pay_ref[...] = jnp.broadcast_to(row_ref[...][None], pay_ref.shape)
    copies.finish()


def real_nodes(pay_ref):
    return pay_ref[:, 0, pay_ref.shape[2] - 1 :]


def feature_shift(pay_ref, h):
    means = pay_ref[:, h, pay_ref.shape[2] - LANES :]
    counts = means[:, LANES - 1 :]
    total = jnp.sum(counts, axis=0, keepdims=True)
    return means - jnp.sum(counts * means, axis=0, keepdims=True) / total


def prepare_kernel(xcat_hbm, w_ref, w2_hbm, pre_hbm, w2cat_hbm, xcat, w2, pre, w2cat, sems):
    copies = Copies(sems)
    hops, _, width = w_ref.shape
    nodes = xcat.shape[2]
    step = 2 * CHUNK
    quarter = width // 4
    ready = []
    for h in range(hops):
        ready.append(copies.start(xcat_hbm.at[h], xcat.at[h]))
        ready.append(copies.start(w2_hbm.at[h * width : (h + 1) * width, :], w2.at[h]))
    for h in range(hops):
        high, low = split(pad_rows(w_ref[h], LANES).T)
        wcat = jnp.concatenate(
            [jnp.concatenate([high, high], axis=1), jnp.concatenate([low, low], axis=1)], axis=0
        )

        def product(start):
            cols = slice(start, start + step)
            value = dot(wcat, xcat[h, :, cols])
            pre[h, :, cols] = value[:width] + value[width:]

        def turn(i):
            at = i * quarter
            high, low = split(w2[h, at : at + quarter, :].T)
            w2cat[h, :, at : at + quarter] = high
            w2cat[h, :, width + at : width + at + quarter] = low

        ready[2 * h].wait()
        ready[2 * h + 1].wait()
        weave(
            [functools.partial(product, start) for start in range(0, nodes, step)],
            [functools.partial(turn, i) for i in range(4)],
        )
        copies.send(pre.at[h], pre_hbm.at[h * width : (h + 1) * width, :])
        copies.send(w2cat.at[h], w2cat_hbm.at[h])
    copies.finish()


def columns_of(pack):
    rows = pack.shape[0]
    return [jnp.broadcast_to(pack[:, i : i + 1], (rows, LANES)) for i in range(6)]


def forward_kernel(
    code_ref, pay_ref, w_ref, gain_ref, bias_ref, slope1_ref, slope2_ref, mask_ref, pre_hbm, w2cat_hbm,
    mid_ref, stat_ref, inv_ref, colpack_ref, act_hbm,
    pre, w2cat, act, shift_ref, row_ref, sems,
):
    copies = Copies(sems)
    hops, _, width = w_ref.shape
    nodes = mid_ref.shape[1]
    ready = []
    for h in range(hops):
        rows = slice(h * width, (h + 1) * width)
        ready.append((
            copies.start(pre_hbm.at[rows, :], pre.at[h]),
            copies.start(w2cat_hbm.at[h], w2cat.at[h]),
        ))
    counts = real_nodes(pay_ref)
    total = jnp.sum(counts, axis=0, keepdims=True)
    for h in range(hops):
        shift = dot(feature_shift(pay_ref, h), pad_rows(w_ref[h], LANES), exact)
        shift_ref[h] = shift
        squares = pay_ref[:, h, :width]
        square = jnp.sum(squares + counts * shift * shift, axis=0, keepdims=True)
        inverse = lax.rsqrt(square / total + epsilon)
        inv_ref[h] = inverse
        scale = 0.5 * gain_ref[h] * inverse
        rows = [
            scale,
            shift_ref[h, pl.ds(code_ref[0], 1), :] * scale + 0.5 * bias_ref[h],
            0.5 + 0.5 * slope1_ref[h],
            0.5 - 0.5 * slope1_ref[h],
            1.0 + slope2_ref[h],
            1.0 - slope2_ref[h],
        ]
        colpack_ref[h] = pad_rows(jnp.concatenate(rows, axis=0), LANES).T

    size = width // 2
    units = [(h, start) for h in range(hops) for start in (0, size)]

    def slabs(h, start):
        rows = 16

        def slab(r):
            rs = slice(r, r + rows)
            columns = columns_of(colpack_ref[h, rs, :])
            scale, shift, p1, q1, p2, q2 = (wide(c, nodes) for c in columns)
            half = pre[h, rs, :] * scale + shift
            half = half * (p1 + q1 * jnp.tanh(half))
            high, low = split(half * (p2 + q2 * jnp.tanh(half)))
            act[h, 0, rs, :] = high
            act[h, 1, rs, :] = low

        return [functools.partial(slab, r) for r in range(start, start + size, rows)]

    def products(h, start):
        own = slice(start, start + size)
        w2_high, w2_low = w2cat[h, :, own], w2cat[h, :, width + start : width + start + size]
        w2_parts = jnp.concatenate([w2_high, w2_high, w2_low], axis=1)

        def product(at):
            cols = slice(at, at + CHUNK)
            high, low = act[h, 0, own, cols], act[h, 1, own, cols]
            value = dot(w2_parts, jnp.concatenate([high, low, high], axis=0))
            mid_ref[:, cols] = value if (h, start) == units[0] else mid_ref[:, cols] + value

        return [functools.partial(product, at) for at in range(0, nodes, CHUNK)]

    for i in range(len(units) + 1):
        if i < len(units) and units[i][1] == 0:
            for copy in ready[units[i][0]]:
                copy.wait()
        weave(
            products(*units[i - 1]) if i else [lambda: None],
            slabs(*units[i]) if i < len(units) else [],
        )
        if i < len(units) and units[i][1] == size:
            h = units[i][0]
            rows = slice(h * width, (h + 1) * width)
            copies.send(act.at[h, 0], act_hbm.at[0, rows, :])
            copies.send(act.at[h, 1], act_hbm.at[1, rows, :])
    keep = mask_ref[...].reshape(1, -1).astype(f32)
    count = jnp.maximum(jnp.sum(keep, axis=1, keepdims=True), 1.0)
    mid = mid_ref[...]
    average = total_row(fold(mid * keep)) / count
    off = mid - wide(as_column(average), nodes)
    square = total_row(fold(off * off * keep))
    put_rows(row_ref, average, square)
    stat_ref[...] = jnp.broadcast_to(row_ref[...][None], stat_ref.shape)
    copies.finish()


def put_rows(row_ref, *rows):
    at = 0
    for row in rows:
        for start in range(0, row.shape[1], LANES):
            row_ref[at : at + 1, :] = row[:, start : start + LANES]
            at += 1


def rows_of(ref, first, count):
    return jnp.concatenate([ref[:, i, :] for i in range(first, first + count)], axis=1)


def head_kernel(
    pay_ref, stat_ref, gain_ref, bias_ref, slope_ref, ow_ref, ob_ref, label_ref, mask_ref, mid_ref,
    logit_ref, inv_ref, sums_ref, misc_ref, up_ref, norm_ref,
    ow_scr, ob_scr, row_ref, half_ref, tan_ref, acat_ref, col_ref, back_ref, acc_ref, misc_scr,
):
    width, nodes = mid_ref.shape
    classes = ow_ref.shape[0]
    tiles = width // LANES
    counts = real_nodes(pay_ref)
    total = jnp.sum(counts, axis=0, keepdims=True)
    means = rows_of(stat_ref, 0, tiles)
    average = jnp.sum(counts * means, axis=0, keepdims=True) / total
    off = means - average
    square = jnp.sum(rows_of(stat_ref, tiles, tiles) + counts * off * off, axis=0, keepdims=True)
    inverse = lax.rsqrt(square / total + epsilon)
    inv_ref[...] = inverse
    col_ref[0] = as_column(average)
    col_ref[1] = as_column(inverse)
    col_ref[2] = 0.5 * as_column(gain_ref[...])
    col_ref[3] = 0.5 * as_column(bias_ref[...])
    slope = as_column(slope_ref[...])
    col_ref[4] = 0.5 + 0.5 * slope
    col_ref[5] = 0.5 - 0.5 * slope
    ow_scr[...] = jnp.zeros_like(ow_scr)
    ow_scr[:classes, :] = ow_ref[...]
    ow_t = split(ow_scr[:CLASS_ROWS, :])
    ow = split(ow_scr[...].T)
    ob_scr[...] = jnp.zeros_like(ob_scr)
    ob_scr[:, :classes] = ob_ref[...]
    ob_col = wide(as_column(ob_scr[...])[:CLASS_ROWS], nodes)
    rows = 16
    for r in range(0, width, rows):
        rs = slice(r, r + rows)
        mean, inv, gain, bias, p, q = (wide(col_ref[i, rs], nodes) for i in range(6))
        normed = (mid_ref[rs, :] - mean) * inv
        norm_ref[rs, :] = normed
        half = normed * gain + bias
        tangent = jnp.tanh(half)
        half_ref[rs, :] = half
        tan_ref[rs, :] = tangent
        high, low = split(2.0 * half * (p + q * tangent))
        acat_ref[rs, :] = high
        acat_ref[slice(width + r, width + r + rows), :] = low
    high, low = acat_ref[:width, :], acat_ref[width:, :]
    logits = dot(jnp.concatenate([ow_t[0], ow_t[0]], axis=1), acat_ref[...]) + dot(ow_t[1], high)
    logits = logits + ob_col
    logit_ref[...] = logits[:classes]
    keep = mask_ref[...].reshape(1, -1).astype(f32)
    place = lax.broadcasted_iota(jnp.int32, (CLASS_ROWS, nodes), 0)
    logits = jnp.where(place < classes, logits, -3.0e38)
    shifted = logits - jnp.max(logits, axis=0, keepdims=True)
    weights = jnp.exp(shifted)
    norm = jnp.sum(weights, axis=0, keepdims=True)
    onehot = place == label_ref[...].reshape(1, -1)
    picked = jnp.sum(jnp.where(onehot, shifted, 0.0), axis=0, keepdims=True)
    loss = jnp.sum(fold(keep * (jnp.log(norm) - picked)), axis=1, keepdims=True)
    grad = keep * (weights * (1.0 / norm) - jnp.where(onehot, 1.0, 0.0))
    grad_sum = fold(grad)
    grad_high, grad_low = split(pad_rows(grad, LANES))
    gcat = jnp.concatenate([grad_high, grad_low, grad_high], axis=0)
    owcat = jnp.concatenate([ow[0], ow[0], ow[1]], axis=1)

    def back(start):
        back_ref[:, start : start + CHUNK] = dot(owcat, gcat[:, start : start + CHUNK])

    for start in range(0, nodes, CHUNK):
        back(start)
    both = jnp.concatenate([grad_high, grad_low], axis=0)

    def weight_grad():
        value = dot_nt(both, high)
        value = value[:CLASS_ROWS] + value[LANES : LANES + CLASS_ROWS]
        misc_scr[:CLASS_ROWS, :] = value + dot_nt(grad_high[:CLASS_ROWS], low)

    def slab(r):
        rs = slice(r, r + rows)
        p, q = wide(col_ref[4, rs], nodes), wide(col_ref[5, rs], nodes)
        half, tangent, act_grad = half_ref[rs, :], tan_ref[rs, :], back_ref[rs, :]
        away = half * (1.0 - tangent)
        acc_ref[0, rs] = fold(act_grad * away)
        up = act_grad * (p + q * (tangent + away * (1.0 + tangent)))
        up_ref[rs, :] = up
        acc_ref[1, rs] = fold(up)
        acc_ref[2, rs] = fold(up * norm_ref[rs, :])

    slabs = [functools.partial(slab, r) for r in range(0, width, rows)]
    weave([weight_grad, lambda: None], slabs)
    put_rows(row_ref, total_row(acc_ref[1]), total_row(acc_ref[2]))
    sums_ref[...] = jnp.broadcast_to(row_ref[...][None], sums_ref.shape)
    misc_scr[CLASS_ROWS:, :] = jnp.zeros((HEAD_ROWS - CLASS_ROWS, width), f32)
    misc_scr[CLASS_ROWS : CLASS_ROWS + 1, :] = total_row(acc_ref[0])
    misc_scr[CLASS_ROWS + 1 : CLASS_ROWS + 2, :LANES] = total_row(pad_rows(grad_sum, LANES))
    misc_scr[CLASS_ROWS + 2 : CLASS_ROWS + 3, :1] = loss
    for t in range(tiles):
        misc_ref[t] = misc_scr[:, t * LANES : (t + 1) * LANES]


def mid_grad_kernel(
    code_ref, pay_ref, sums_ref, inv_ref, gain_ref, mask_ref, up_ref, norm_ref, act_hbm,
    out_ref, bg_ref, gcat,
    act, sems,
):
    width, nodes = up_ref.shape
    ready = act_in(1, code_ref, Copies(sems), act_hbm, act)
    tiles = width // LANES
    total = jnp.sum(real_nodes(pay_ref), axis=0, keepdims=True)
    bias_sum = jnp.sum(rows_of(sums_ref, 0, tiles), axis=0, keepdims=True)
    gain_sum = jnp.sum(rows_of(sums_ref, tiles, tiles), axis=0, keepdims=True)
    bg_ref[0:1, :] = bias_sum
    bg_ref[1:2, :] = gain_sum
    scale = as_column(gain_ref[...] * inv_ref[...])
    bias_col = as_column(bias_sum / total)
    gain_col = as_column(gain_sum / total)
    keep = mask_ref[...].reshape(1, -1).astype(f32)
    rows = 16
    for r in range(0, width, rows):
        rs = slice(r, r + rows)
        bias, gain = wide(bias_col[rs], nodes), wide(gain_col[rs], nodes)
        grad = up_ref[rs, :] - bias - norm_ref[rs, :] * gain
        high, low = split(keep * (wide(scale[rs], nodes) * grad))
        gcat[rs, :] = high
        gcat[width + r : width + r + rows, :] = low
    mid_product(code_ref, ready, act, gcat, out_ref)


def act_in(half_sel, code_ref, copies, act_hbm, act):
    parts, _, width, _ = act.shape
    rows = width // 2
    ready = []
    for s in range(parts):
        for r in (0, 1):
            block = (s * 2 + (half_sel ^ (code_ref[s] >> 4))) * 2 + r
            ready.append([
                copies.start(act_hbm.at[i, aligned(block, rows)], act.at[s, i, r * rows : (r + 1) * rows])
                for i in (0, 1)
            ])
    return ready


def mid_product(code_ref, ready, act, gcat, out_ref):
    parts, width, mid = out_ref.shape
    rows = width // PIECES
    size = width // 2
    for s in range(parts):
        code = code_ref[s] & (PIECES - 1)
        for r in (0, 1):
            for copy in ready[s * 2 + r]:
                copy.wait()
            here = slice(r * size, (r + 1) * size)
            value = dot_nt(act[s, 0, here, :], gcat[:mid, :])
            value = value + dot_nt(act[s, 0, here, :], gcat[mid:, :])
            value = value + dot_nt(act[s, 1, here, :], gcat[:mid, :])
            for i in range(size // rows):
                place = (r * (size // rows) + i) ^ code
                out_ref[s, aligned(place, rows), :] = value[i * rows : (i + 1) * rows]


def mid_grad_rest_kernel(code_ref, gcat, act_hbm, out_ref, act, sems):
    ready = act_in(0, code_ref, Copies(sems), act_hbm, act)
    mid_product(code_ref, ready, act, gcat, out_ref)


def backward_kernel(
    code_ref, pay_ref, inv_ref, gain_ref, colpack_ref, w_ref, gram_ref, misc_ref,
    g, w2_hbm, pre_hbm, xcat_hbm,
    pack_ref, feat_hbm,
    w2, pre, xcat, feat, col, down, ucat, acc, prod, rows_scr, shift_col, sems,
):
    copies = Copies(sems)
    hops, feats, width = w_ref.shape
    mid, nodes = g.shape[0] // 2, g.shape[1]
    tiles = mid // LANES
    size = 2 * CHUNK
    chunks = [slice(start, start + size) for start in range(0, nodes, size)]
    count = len(chunks)
    stages = [(h, j) for h in range(hops) for j in range(count)]
    w_in, z_in, x_in = {}, {}, {}
    for h in range(hops):
        own = slice(h * width, (h + 1) * width)
        w_in[h] = copies.start(w2_hbm.at[own, :], w2.at[h])
        for j, c in enumerate(chunks):
            z_in[h, j] = copies.start(pre_hbm.at[own, c], pre.at[h, :, c])
        x_in[h] = copies.start(xcat_hbm.at[h], xcat.at[h])
    devices = pay_ref.shape[0]
    flip = code_ref[1] * (tiles // 2)
    at = hops * HOP_ROWS
    for t in range(tiles):
        pack_ref[t ^ flip, at : at + HEAD_ROWS, :] = misc_ref[t]
    w2cat, wcat = {}, {}

    def columns(h):
        rows = 64
        for r in range(0, width, rows):
            for k, values in enumerate(columns_of(colpack_ref[h, r : r + rows, :])):
                col[h % 2, k, r : r + rows, :] = values
        acc[h % 2] = jnp.zeros(acc.shape[1:], f32)

    def weights(h):
        high, low = split(pad_rows(w_ref[h], LANES) * (gain_ref[h] * inv_ref[h]))
        wcat[h] = (jnp.concatenate([high, low], axis=0), high)
        high, low = split(0.5 * w2[h])
        w2cat[h] = jnp.concatenate([high, high, low], axis=1)

    def part_of(j, part):
        return slice(chunks[j].start + part * CHUNK, chunks[j].start + (part + 1) * CHUNK)

    def down_product(index, part):
        h, j = stages[index]
        cs = part_of(j, part)
        high, low = g[:mid, cs], g[mid:, cs]
        value = dot(w2cat[h], jnp.concatenate([high, low, high], axis=0))
        down[index % 2, :, part * CHUNK : (part + 1) * CHUNK] = value

    def slab(index, r, rows):
        h, j = stages[index]
        two = h % 2
        rs, cs = slice(r, r + rows), chunks[j]
        scale, shift, p1, q1, p2, q2 = (wide(col[two, k, rs], size) for k in range(6))
        half1 = pre[h, rs, cs] * scale + shift
        grad2 = down[index % 2, rs, :]
        tan1 = jnp.tanh(half1)
        half2 = half1 * (p1 + q1 * tan1)
        tan2 = jnp.tanh(half2)
        away2 = half2 * (1.0 - tan2)
        acc[two, 0, rs] += fold(grad2 * away2)
        grad1 = grad2 * (p2 + q2 * (tan2 + away2 * (1.0 + tan2)))
        away1 = half1 * (1.0 - tan1)
        acc[two, 1, rs] += fold(grad1 * away1)
        grad = grad1 * (p1 + q1 * (tan1 + away1 * (1.0 + tan1)))
        high, low = split(grad)
        ucat[two, rs, cs] = high
        ucat[two, width + r : width + r + rows, cs] = low

    def feature_product(index, part):
        h, j = stages[index]
        cs = part_of(j, part)
        value = dot(wcat[h][0], ucat[h % 2, :width, cs])
        value = value[:LANES] + value[LANES:] + dot(wcat[h][1], ucat[h % 2, width:, cs])
        feat[h, :, cs] = value[:feats]

    def weight_product(h):
        value = dot_nt(xcat[h], ucat[h % 2, :width, :])
        low = dot_nt(xcat[h, :LANES, :], ucat[h % 2, width:, :])
        prod[h % 2] = value[:LANES] + value[LANES:] + low

    def shifts(h):
        shift = feature_shift(pay_ref, h)
        rows_scr[h, :devices, :] = shift
        rows_scr[h, devices:, :] = jnp.broadcast_to(real_nodes(pay_ref), shift.shape)
        own_shift = rows_scr[h, pl.ds(code_ref[0], 1), :]
        own_count = rows_scr[h, pl.ds(devices + code_ref[0], 1), :]
        shift_col[h] = as_column(own_shift)
        gram = gram_ref[h] + shift_col[h] * (own_shift * own_count)
        pack_ref[h ^ flip, at + HEAD_ROWS :, :] = gram[:HOP_ROWS]

    def pack(h):
        two = h % 2
        bias_sum = prod[two, feats : feats + 1, :]
        prod[two] = prod[two] + wide(shift_col[h], mid) * bias_sum
        prod[two, feats + 1 : feats + 2, :] = total_row(acc[two, 1])
        prod[two, feats + 2 : feats + 3, :] = 2.0 * total_row(acc[two, 0])
        for t in range(tiles):
            pack_ref[t ^ flip, h * HOP_ROWS : (h + 1) * HOP_ROWS, :] = prod[
                two, :HOP_ROWS, t * LANES : (t + 1) * LANES
            ]

    for h in range(hops):
        shifts(h)
    rows = 16
    columns(0)
    w_in[0].wait()
    weights(0)
    for part in (0, 1):
        down_product(0, part)
    for index, (h, j) in enumerate(stages):
        products = []
        z_in[h, j].wait()
        if j + 1 == count:
            x_in[h].wait()
            if h + 1 < hops:
                w_in[h + 1].wait()
                weights(h + 1)
                columns(h + 1)
        if index + 1 < len(stages):
            products += [functools.partial(down_product, index + 1, part) for part in (0, 1)]
        if index >= 1:
            products += [functools.partial(feature_product, index - 1, part) for part in (0, 1)]
        if j == 0 and h >= 1:
            products.append(functools.partial(weight_product, h - 1))
        slabs = [functools.partial(slab, index, r, rows) for r in range(0, width, rows)]
        if j == 1 and h >= 1:
            copies.send(feat.at[h - 1], feat_hbm.at[h - 1])
            slabs.insert(len(slabs) // 2, functools.partial(pack, h - 1))
        weave(products, slabs)
    for part in (0, 1):
        feature_product(len(stages) - 1, part)
    copies.send(feat.at[hops - 1], feat_hbm.at[hops - 1])
    weight_product(hops - 1)
    pack(hops - 1)
    copies.finish()


def finish_kernel(
    code_ref, pay_ref, inv_ref, mine_ref, other_ref, w_ref, gain_ref, mask_ref, bg_ref, xcat_hbm,
    feat_hbm, fgrad_hbm, wgrad_hbm, gain_out, bias_out, slope1_out, slope2_out, mgain_out, mbias_out, mslope_out,
    owg_out, obg_out, loss_out,
    sum_ref, rows_scr, fgrad, wgrad, feat, xcat, sems,
):
    hops, feats, width = w_ref.shape
    tiles = mine_ref.shape[0] * 2
    half = tiles // 2
    flip = code_ref[1]
    copies = Copies(sems)
    ready = []
    for h in range(hops):
        ready.append((copies.start(feat_hbm.at[h], feat.at[h]), copies.start(xcat_hbm.at[h], xcat.at[h])))

    @pl.when(flip == 0)
    def _():
        for t in range(half):
            sum_ref[:, t * LANES : (t + 1) * LANES] = mine_ref[t]
            sum_ref[:, (half + t) * LANES : (half + t + 1) * LANES] = other_ref[t]

    @pl.when(flip != 0)
    def _():
        for t in range(half):
            sum_ref[:, t * LANES : (t + 1) * LANES] = other_ref[t]
            sum_ref[:, (half + t) * LANES : (half + t + 1) * LANES] = mine_ref[t]

    counts = real_nodes(pay_ref)
    total = jnp.sum(counts, axis=0, keepdims=True)
    keep = mask_ref[...].reshape(1, -1).astype(f32)
    at = hops * HOP_ROWS
    for h in range(hops):
        base = h * HOP_ROWS
        w = pad_rows(w_ref[h], LANES)
        inverse = inv_ref[h]
        scale = gain_ref[h] * inverse
        bias_sum = sum_ref[base + feats : base + feats + 1, :]
        slope1_out[h] = sum_ref[base + feats + 1 : base + feats + 2, :]
        slope2_out[h] = sum_ref[base + feats + 2 : base + feats + 3, :]
        products = sum_ref[base : base + feats, :]
        gain_sum = inverse * jnp.sum(w_ref[h] * products, axis=0, keepdims=True)
        bias_out[h] = bias_sum
        gain_out[h] = gain_sum
        gram = sum_ref[at + HEAD_ROWS : at + HEAD_ROWS + HOP_ROWS, h * LANES : (h + 1) * LANES]
        inner = dot(gram, w, exact)[:feats] * (inverse * gain_sum / total)
        wgrad[h] = scale * (products - inner)
        copies.send(wgrad.at[h], wgrad_hbm.at[:, h, :])
        shift = feature_shift(pay_ref, h)
        rows_scr[...] = shift
        own_shift = rows_scr[pl.ds(code_ref[0], 1), :]
        mix = dot_nt(w * (scale * inverse * gain_sum / total), w, exact)
        lane = lax.broadcasted_iota(jnp.int32, (1, LANES), 1)
        off = jnp.sum(w * (scale * bias_sum / total), axis=1, keepdims=True)
        off = off + jnp.sum(mix * jnp.where(lane < feats, own_shift, 0.0), axis=1, keepdims=True)
        high, low = split(mix)
        for copy in ready[h]:
            copy.wait()
        mixed = dot(jnp.concatenate([high, high], axis=1), xcat[h]) + dot(low, xcat[h, :LANES])
        fgrad[h] = keep * (feat[h] - (mixed + off)[:feats])
        copies.send(fgrad.at[h], fgrad_hbm.at[:, h, :])
    owg_out[...] = sum_ref[at : at + owg_out.shape[0], :]
    mslope_out[...] = sum_ref[at + CLASS_ROWS : at + CLASS_ROWS + 1, :]
    obg_out[...] = sum_ref[at + CLASS_ROWS + 1 : at + CLASS_ROWS + 2, : obg_out.shape[1]]
    loss_out[...] = sum_ref[at + CLASS_ROWS + 2 : at + CLASS_ROWS + 3, :1] / total
    mbias_out[...] = bg_ref[0:1, :]
    mgain_out[...] = bg_ref[1:2, :]
    copies.finish()


def place_kernel(pieces, code_ref, *refs):
    out_ref, sems = refs[-2:]
    copies = Copies(sems)
    for ref, (s, first, rows) in zip(refs, pieces):
        for i in range(ref.shape[0] // rows):
            block = s * 2 * PIECES + ((first + i) ^ code_ref[s])
            copies.send(ref.at[pl.ds(i * rows, rows)], out_ref.at[aligned(block, rows)])
    copies.finish()


def exchange(values, bit, devices):
    return lax.ppermute(values, axes, [(i, i ^ (1 << bit)) for i in range(devices)])


def exchange_two(a, bit_a, b, bit_b, devices):
    a, b = lax.optimization_barrier((a, b))
    return lax.optimization_barrier((exchange(a, bit_a, devices), exchange(b, bit_b, devices)))


def swap_halves(a, bit_a, b, bit_b, devices):
    size = a.shape[0] // 2
    ra, rb = exchange_two(a[size:], bit_a, b[size:], bit_b, devices)
    return a[:size] + ra, b[:size] + rb


def code_of(me, order):
    code = 0
    for bit in order:
        code = code * 2 + ((me >> bit) & 1)
    return code


def after(values, *others):
    return lax.optimization_barrier((values, *others))[0]


def on_device(
    devices,
    hop_features,
    branch_weight,
    branch_gain,
    branch_bias,
    first_slope,
    second_slope,
    mid_weight,
    mid_gain,
    mid_bias,
    mid_slope,
    out_weight,
    out_bias,
    labels,
    valid_mask,
):
    hops, feats, nodes = hop_features.shape
    width = branch_weight.shape[2]
    mid = mid_weight.shape[1]
    classes = out_weight.shape[1]
    tiles = mid // LANES
    bits = devices.bit_length() - 1
    me = lax.axis_index(axes).astype(jnp.int32)
    rest = tuple(range(5, bits))
    codes = jnp.stack([code_of(me, (0, 1, 2, 3, 4)), code_of(me, (0, 2, 1, 3, 4))])
    place_code = jnp.stack([me, me & 1])
    shape = jax.ShapeDtypeStruct
    by_hop = lambda v: v.reshape(hops, 1, width)
    gain, bias, slope1, slope2 = map(by_hop, (branch_gain, branch_bias, first_slope, second_slope))
    row = lambda v: v.reshape(1, -1)
    gather = functools.partial(
        lax.all_to_all, axis_name=axes, split_axis=0, concat_axis=0, tiled=True
    )
    dma = pltpu.SemaphoreType.DMA
    scratch = lambda dtype, *dims: pltpu.VMEM(dims, dtype)
    mask = valid_mask

    pay, gram, xcat, w = call(
        stats_kernel,
        60,
        in_specs=[anywhere, anywhere, vmem],
        out_specs=[vmem, vmem, anywhere, anywhere],
        out_shape=(
            shape((devices, hops, width + LANES), f32), shape((hops, LANES, LANES), f32),
            shape((hops, 2 * LANES, nodes), bf16), shape((hops, feats, width), f32),
        ),
        scratch_shapes=[
            scratch(f32, hops, feats, nodes), scratch(f32, hops, feats, width),
            scratch(bf16, hops, 2 * LANES, nodes), scratch(f32, hops, width + LANES), dma((4 * hops,)),
        ],
        cost_estimate=cost(1_000_000_000, 8_000_000),
        name="first_stats",
    )(jnp.transpose(hop_features, (1, 0, 2)), jnp.transpose(branch_weight, (1, 0, 2)), mask)
    pay = gather(after(pay, codes, place_code))

    pre, w2cat = call(
        prepare_kernel,
        60,
        in_specs=[anywhere, vmem, anywhere],
        out_specs=[anywhere] * 2,
        out_shape=(shape((hops * width, nodes), f32), shape((hops, mid, 2 * width), bf16)),
        scratch_shapes=[
            scratch(bf16, hops, 2 * LANES, nodes), scratch(f32, hops, width, mid),
            scratch(f32, hops, width, nodes), scratch(bf16, hops, mid, 2 * width), dma((4 * hops,)),
        ],
        cost_estimate=cost(4 * 2 * 4 * hops * LANES * width * nodes, 20_000_000),
        name="prepare",
    )(xcat, w, mid_weight)

    mid_pre, stat, first_inv, colpack, act = call(
        forward_kernel,
        45,
        in_specs=[smem] + [vmem] * 7 + [anywhere] * 2,
        out_specs=[vmem] * 4 + [anywhere],
        out_shape=(
            shape((mid, nodes), f32), shape((devices, 8, LANES), f32), shape((hops, 1, width), f32),
            shape((hops, width, LANES), f32), shape((2, hops * width, nodes), bf16),
        ),
        scratch_shapes=[
            scratch(f32, hops, width, nodes), scratch(bf16, hops, mid, 2 * width),
            scratch(bf16, hops, 2, width, nodes), scratch(f32, hops, devices, width),
            scratch(f32, 8, LANES), dma((4 * hops,)),
        ],
        cost_estimate=cost(3 * 2 * hops * width * mid * nodes, 20_000_000),
        name="forward",
    )(place_code, pay, w, gain, bias, slope1, slope2, mask, pre, w2cat)
    stat = gather(stat)

    logits, mid_inv, sums, misc, up, normed = call(
        head_kernel,
        40,
        in_specs=[vmem] * 10,
        out_specs=[vmem] * 6,
        out_shape=(
            shape((classes, nodes), f32), shape((1, mid), f32), shape((devices, 8, LANES), f32),
            shape((tiles, HEAD_ROWS, LANES), f32), shape((mid, nodes), f32), shape((mid, nodes), f32),
        ),
        scratch_shapes=[
            scratch(f32, LANES, mid), scratch(f32, 1, LANES), scratch(f32, 8, LANES),
            scratch(f32, mid, nodes), scratch(f32, mid, nodes), scratch(bf16, 2 * mid, nodes),
            scratch(f32, 6, mid, LANES), scratch(f32, mid, nodes), scratch(f32, 3, mid, LANES),
            scratch(f32, HEAD_ROWS, mid),
        ],
        cost_estimate=cost(2_000_000_000, 10_000_000),
        name="head",
    )(pay, stat, row(mid_gain), row(mid_bias), row(mid_slope), out_weight.T, row(out_bias), labels, mask, mid_pre)
    sums = gather(sums)

    product_cost = cost(2 * 3 * 2 * width * mid * nodes, 10_000_000)
    send, mid_bg, gcat = call(
        mid_grad_kernel,
        36,
        in_specs=[smem] + [vmem] * 7 + [anywhere],
        out_specs=[vmem] * 3,
        out_shape=(
            shape((2, width, mid), f32), shape((2, mid), f32), shape((2 * mid, nodes), bf16),
        ),
        scratch_shapes=[scratch(bf16, 2, 2, width, nodes), dma((8,))],
        cost_estimate=product_cost,
        name="mid_grad_send",
    )(codes, pay, sums, mid_inv, row(mid_gain), mask, up, normed, act)
    came = exchange(send, 0, devices)
    kept = call(
        mid_grad_rest_kernel,
        40,
        in_specs=[smem, vmem, anywhere],
        out_specs=vmem,
        out_shape=shape((2, width, mid), f32),
        scratch_shapes=[scratch(bf16, 2, 2, width, nodes), dma((8,))],
        cost_estimate=product_cost,
        name="mid_grad_keep",
    )(codes, gcat, act)

    pack_rows = hops * HOP_ROWS + HEAD_ROWS + HOP_ROWS

    def backward(gcat):
        return call(
            backward_kernel,
            46,
            in_specs=[smem] + [vmem] * 8 + [anywhere] * 3,
            out_specs=[vmem, anywhere],
            scratch_shapes=[
                scratch(f32, hops, width, mid), scratch(f32, hops, width, nodes),
                scratch(bf16, hops, 2 * LANES, nodes),
                scratch(f32, hops, feats, nodes), scratch(f32, 2, 6, width, LANES),
                scratch(f32, 2, width, 2 * CHUNK), scratch(bf16, 2, 2 * width, nodes),
                scratch(f32, 2, 2, width, LANES), scratch(f32, 2, LANES, mid),
                scratch(f32, hops, 2 * devices, LANES), scratch(f32, hops, LANES, LANES),
                dma((3 * hops + (hops + 1) * nodes // CHUNK,)),
            ],
            out_shape=(shape((tiles, pack_rows, LANES), f32), shape((hops, feats, nodes), f32)),
            cost_estimate=cost(hops * 2 * 4 * width * mid * nodes, 24_000_000),
            name="backward",
        )(place_code, pay, first_inv, gain, colpack, w, gram, misc, gcat, mid_weight, pre, xcat)

    a, b = kept[0] + came[0], kept[1] + came[1]
    size = a.shape[0] // 2
    send_a, send_b = a[size:], b[size:]
    ra = exchange(send_a, 1, devices)
    rb = exchange(send_b, 2, devices)
    pack, feat = backward(after(gcat, send_a, send_b))
    a, b = a[:size] + after(ra, pack), b[:size] + after(rb, pack)

    half = tiles // 2
    groups = {}
    for i in range(devices):
        groups.setdefault(i & ~14, []).append(i)
    spread = functools.partial(
        lax.all_to_all, axis_name=axes, split_axis=0, concat_axis=0,
        axis_index_groups=list(groups.values()), tiled=True,
    )
    pack = after(pack, a, b)
    pack = pack[:half] + exchange(pack[half:], 0, devices)
    a, b, pack = lax.optimization_barrier((a, b, pack))
    a, b = swap_halves(a, 2, b, 1, devices)
    pack = spread(pack.reshape(8, -1, LANES))
    part = a.shape[0] // 4
    both = jnp.stack([a.reshape(4, part, mid), b.reshape(4, part, mid)], axis=1)
    both = both[:2] + exchange(both[2:], 3, devices)
    pack = pack.sum(axis=0)
    pack, both = lax.optimization_barrier((pack, both))
    came, pack_came = lax.optimization_barrier(
        (exchange(both[1:], 4, devices), exchange(pack, 4, devices))
    )
    both, pack = both[:1] + came, pack + pack_came
    for bit in rest:
        both, pack = both + exchange(both, bit, devices), pack + exchange(pack, bit, devices)
    pack = jnp.broadcast_to(pack[None], (8,) + pack.shape)
    pack, both = lax.optimization_barrier((pack, both))
    pack = spread(pack).reshape(half, pack_rows, LANES)
    both = jnp.concatenate([both, exchange(both, 4, devices)])
    both = jnp.concatenate([both, exchange(both, 3, devices)])
    a, b = both[:, 0].reshape(-1, mid), both[:, 1].reshape(-1, mid)
    ra, rb = exchange_two(a, 2, b, 1, devices)
    a, b = jnp.concatenate([a, ra]), jnp.concatenate([b, rb])
    a, b = lax.optimization_barrier((a, b))
    ra, rb = exchange(a, 1, devices), exchange(b, 2, devices)
    other_a, other_b = exchange(a, 0, devices), exchange(b, 0, devices)
    pack_other = exchange(pack, 0, devices)

    rows_out = [shape((hops, 1, width), f32)] * 4
    rows_mid = [shape((1, mid), f32)] * 3
    (
        feature_grad, branch_weight_grad, branch_gain_grad, branch_bias_grad, first_slope_grad,
        second_slope_grad, mid_gain_grad, mid_bias_grad, mid_slope_grad, out_weight_grad,
        out_bias_grad, mean_loss,
    ) = call(
        finish_kernel,
        60,
        in_specs=[smem] + [vmem] * 8 + [anywhere] * 2,
        out_specs=[anywhere, anywhere] + [vmem] * 10,
        scratch_shapes=[
            scratch(f32, pack_rows, mid), scratch(f32, devices, LANES), scratch(f32, hops, feats, nodes),
            scratch(f32, hops, feats, width), scratch(f32, hops, feats, nodes),
            scratch(bf16, hops, 2 * LANES, nodes), dma((4 * hops,)),
        ],
        out_shape=(
            shape((feats, hops, nodes), f32), shape((feats, hops, width), f32), *rows_out, *rows_mid,
            shape((classes, mid), f32), shape((1, classes), f32), shape((1, 1), f32),
        ),
        cost_estimate=cost(0, 20_000_000),
        name="finish",
    )(place_code, pay, first_inv, pack, pack_other, w, gain, mask, mid_bg, xcat, feat)

    rows = mid_weight.shape[0] // (4 * PIECES)
    eight = PIECES // 2

    def place(pieces, *base):
        values = [value for value, *_ in pieces]
        kinds = [(s, first, rows) for _, s, first in pieces]
        return call(
            functools.partial(place_kernel, kinds),
            16,
            in_specs=[smem] + [vmem] * len(values) + [anywhere] * len(base),
            out_specs=anywhere,
            scratch_shapes=[dma((len(values) * eight,))],
            out_shape=shape(mid_weight.shape, f32),
            input_output_aliases={1 + len(values): 0} if base else {},
            cost_estimate=cost(0, 4_000_000),
            name="place",
        )(codes, *values, *base)

    grad = place(
        [(a, 0, 0), (b, 1, 0), (other_a, 0, PIECES), (after(other_b, mid_bias_grad), 1, PIECES)]
    )
    ra, rb, grad = lax.optimization_barrier((ra, rb, grad))
    other_ra, other_rb = exchange(ra, 0, devices), exchange(rb, 0, devices)
    grad = place([(ra, 0, eight), (rb, 1, eight)], grad)
    mid_weight_grad = place(
        [(other_ra, 0, PIECES + eight), (after(other_rb, grad), 1, PIECES + eight)], grad
    )

    flat = lambda v: v.reshape(-1)
    return (
        logits,
        mean_loss.reshape(()),
        jnp.transpose(feature_grad, (1, 0, 2)),
        jnp.transpose(branch_weight_grad, (1, 0, 2)),
        flat(branch_gain_grad),
        flat(branch_bias_grad),
        flat(first_slope_grad),
        flat(second_slope_grad),
        mid_weight_grad,
        flat(mid_gain_grad),
        flat(mid_bias_grad),
        flat(mid_slope_grad),
        out_weight_grad.T,
        flat(out_bias_grad),
    )


def solution(mesh):
    devices = mesh.shape["dp"] * mesh.shape["rep"]

    def body(*arrays):
        return on_device(devices, *arrays)

    nodes = P(("dp", "rep"))
    return jax.shard_map(
        body,
        mesh=mesh,
        in_specs=(P(None, None, ("dp", "rep")),) + (P(),) * 11 + (nodes, nodes),
        out_specs=(P(None, ("dp", "rep")), P(), P(None, None, ("dp", "rep"))) + (P(),) * 11,
        check_vma=False,
    )
```

```python
import functools

import jax
import jax.numpy as jnp
from jax import lax
from jax.experimental import pallas as pl
from jax.experimental.pallas import tpu as pltpu
from jax.sharding import PartitionSpec as P

epsilon = 1e-05
axes = ("dp", "rep")
exact = lax.Precision.HIGHEST
f32 = jnp.float32
bf16 = jnp.bfloat16
LANES = 128
CHUNK = 256
PIECES = 16
HOP_ROWS = 104
HEAD_ROWS = 56
CLASS_ROWS = 48


def dot(left, right, precision=None):
    return lax.dot_general(
        left, right, (((1,), (0,)), ((), ())), precision=precision, preferred_element_type=f32
    )


def dot_nt(left, right, precision=None):
    return lax.dot_general(
        left, right, (((1,), (1,)), ((), ())), precision=precision, preferred_element_type=f32
    )


def split(values):
    high = values.astype(bf16)
    return high, (values - high.astype(f32)).astype(bf16)


def as_column(row):
    return jnp.broadcast_to(row, (LANES, row.shape[1])).T


def wide(column, width):
    return jnp.concatenate([column] * (width // LANES), axis=1)


def fold(values):
    total = values[:, :LANES]
    for start in range(LANES, values.shape[1], LANES):
        total = total + values[:, start : start + LANES]
    return total


def total_row(partial):
    return jnp.sum(partial.T, axis=0, keepdims=True)


def pad_rows(values, rows):
    return jnp.concatenate(
        [values, jnp.zeros((rows - values.shape[0], values.shape[1]), values.dtype)], axis=0
    )


def weave(products, slabs):
    done = 0
    for j, product in enumerate(products):
        until = (j + 1) * len(slabs) // len(products)
        for slab in slabs[done:until]:
            slab()
        done = until
        product()


def cost(flops=0, bytes_accessed=0):
    return pl.CostEstimate(flops=flops, bytes_accessed=bytes_accessed, transcendentals=0)


def call(kernel, mib, **options):
    return pl.pallas_call(
        kernel, compiler_params=pltpu.CompilerParams(vmem_limit_bytes=mib * 1024 * 1024), **options
    )


class Copies:
    def __init__(self, sems):
        self.sems = sems
        self.used = 0
        self.waiting = []

    def start(self, source, target):
        copy = pltpu.make_async_copy(source, target, self.sems.at[self.used])
        self.used += 1
        copy.start()
        return copy

    def send(self, source, target):
        self.waiting.append(self.start(source, target))

    def finish(self):
        for copy in self.waiting:
            copy.wait()


anywhere = pl.BlockSpec(memory_space=pl.ANY)
vmem = pl.BlockSpec(memory_space=pltpu.VMEM)
smem = pl.BlockSpec(memory_space=pltpu.SMEM)


def aligned(index, step):
    return pl.ds(pl.multiple_of(index * step, step), step)


def stats_kernel(
    x_hbm, w_hbm, mask_ref,
    pay_ref, gram_ref, xcat_hbm, w_out,
    x_scr, w_scr, xcat_ref, row_ref, sems,
):
    copies = Copies(sems)
    hops, feats, _ = x_scr.shape
    x_in, w_in = [], []
    for h in range(hops):
        x_in.append(copies.start(x_hbm.at[:, h, :], x_scr.at[h]))
        w_in.append(copies.start(w_hbm.at[:, h, :], w_scr.at[h]))
    keep = mask_ref[...].reshape(1, -1).astype(f32)
    count = jnp.sum(keep, axis=1, keepdims=True)
    safe = jnp.maximum(count, 1.0)
    row_ref[...] = jnp.zeros_like(row_ref)
    means, grams = [], []
    place = lax.broadcasted_iota(jnp.int32, (LANES, x_scr.shape[2]), 0)
    for h in range(hops):
        x_in[h].wait()
        x = x_scr[h]
        means.append(jnp.sum(x * keep, axis=1, keepdims=True) / safe)
        high, low = split(jnp.where(place == feats, 1.0, pad_rows(x - means[h], LANES)))
        xcat_ref[h, :LANES, :] = high
        xcat_ref[h, LANES:, :] = low
        copies.send(xcat_ref.at[h], xcat_hbm.at[h])
    for h in range(hops):
        real = xcat_ref[h] * keep.astype(bf16)
        gram = dot_nt(real, real)
        grams.append(
            (gram[:LANES, :LANES] + gram[LANES:, LANES:]) + (gram[:LANES, LANES:] + gram[LANES:, :LANES])
        )
        gram_ref[h] = grams[h]
    for h in range(hops):
        w_in[h].wait()
        copies.send(w_scr.at[h], w_out.at[h])
    for h in range(hops):
        w = pad_rows(w_scr[h], LANES)
        width = w.shape[1]
        row_ref[h : h + 1, :width] = jnp.sum(dot(grams[h], w, exact) * w, axis=0, keepdims=True)
        mean = pad_rows(jnp.broadcast_to(means[h], (feats, LANES)), LANES).T
        row_ref[h : h + 1, width:] = mean[:1]
        row_ref[h : h + 1, width + LANES - 1 :] = count
    pay_ref[...] = jnp.broadcast_to(row_ref[...][None], pay_ref.shape)
    copies.finish()


def real_nodes(pay_ref):
    return pay_ref[:, 0, pay_ref.shape[2] - 1 :]


def feature_shift(pay_ref, h):
    means = pay_ref[:, h, pay_ref.shape[2] - LANES :]
    counts = means[:, LANES - 1 :]
    total = jnp.sum(counts, axis=0, keepdims=True)
    return means - jnp.sum(counts * means, axis=0, keepdims=True) / total


def prepare_kernel(xcat_hbm, w_ref, w2_hbm, pre_hbm, w2cat_hbm, xcat, w2, pre, w2cat, sems):
    copies = Copies(sems)
    hops, _, width = w_ref.shape
    nodes = xcat.shape[2]
    step = 2 * CHUNK
    quarter = width // 4
    ready = []
    for h in range(hops):
        ready.append(copies.start(xcat_hbm.at[h], xcat.at[h]))
        ready.append(copies.start(w2_hbm.at[h * width : (h + 1) * width, :], w2.at[h]))
    for h in range(hops):
        high, low = split(pad_rows(w_ref[h], LANES).T)
        wcat = jnp.concatenate(
            [jnp.concatenate([high, high], axis=1), jnp.concatenate([low, low], axis=1)], axis=0
        )

        def product(start):
            cols = slice(start, start + step)
            value = dot(wcat, xcat[h, :, cols])
            pre[h, :, cols] = value[:width] + value[width:]

        def turn(i):
            at = i * quarter
            high, low = split(w2[h, at : at + quarter, :].T)
            w2cat[h, :, at : at + quarter] = high
            w2cat[h, :, width + at : width + at + quarter] = low

        ready[2 * h].wait()
        ready[2 * h + 1].wait()
        weave(
            [functools.partial(product, start) for start in range(0, nodes, step)],
            [functools.partial(turn, i) for i in range(4)],
        )
        copies.send(pre.at[h], pre_hbm.at[h * width : (h + 1) * width, :])
        copies.send(w2cat.at[h], w2cat_hbm.at[h])
    copies.finish()


def columns_of(pack):
    rows = pack.shape[0]
    return [jnp.broadcast_to(pack[:, i : i + 1], (rows, LANES)) for i in range(6)]


def forward_kernel(
    code_ref, pay_ref, w_ref, gain_ref, bias_ref, slope1_ref, slope2_ref, mask_ref, pre_hbm, w2cat_hbm,
    mid_ref, stat_ref, inv_ref, colpack_ref, act_hbm,
    pre, w2cat, act, shift_ref, row_ref, sems,
):
    copies = Copies(sems)
    hops, _, width = w_ref.shape
    nodes = mid_ref.shape[1]
    ready = []
    for h in range(hops):
        rows = slice(h * width, (h + 1) * width)
        ready.append((
            copies.start(pre_hbm.at[rows, :], pre.at[h]),
            copies.start(w2cat_hbm.at[h], w2cat.at[h]),
        ))
    counts = real_nodes(pay_ref)
    total = jnp.sum(counts, axis=0, keepdims=True)
    for h in range(hops):
        shift = dot(feature_shift(pay_ref, h), pad_rows(w_ref[h], LANES), exact)
        shift_ref[h] = shift
        squares = pay_ref[:, h, :width]
        square = jnp.sum(squares + counts * shift * shift, axis=0, keepdims=True)
        inverse = lax.rsqrt(square / total + epsilon)
        inv_ref[h] = inverse
        scale = 0.5 * gain_ref[h] * inverse
        rows = [
            scale,
            shift_ref[h, pl.ds(code_ref[0], 1), :] * scale + 0.5 * bias_ref[h],
            0.5 + 0.5 * slope1_ref[h],
            0.5 - 0.5 * slope1_ref[h],
            1.0 + slope2_ref[h],
            1.0 - slope2_ref[h],
        ]
        colpack_ref[h] = pad_rows(jnp.concatenate(rows, axis=0), LANES).T

    size = width // 2
    units = [(h, start) for h in range(hops) for start in (0, size)]

    def slabs(h, start):
        rows = 16

        def slab(r):
            rs = slice(r, r + rows)
            columns = columns_of(colpack_ref[h, rs, :])
            scale, shift, p1, q1, p2, q2 = (wide(c, nodes) for c in columns)
            half = pre[h, rs, :] * scale + shift
            half = half * (p1 + q1 * jnp.tanh(half))
            high, low = split(half * (p2 + q2 * jnp.tanh(half)))
            act[h, 0, rs, :] = high
            act[h, 1, rs, :] = low

        return [functools.partial(slab, r) for r in range(start, start + size, rows)]

    def products(h, start):
        own = slice(start, start + size)
        w2_high, w2_low = w2cat[h, :, own], w2cat[h, :, width + start : width + start + size]
        w2_parts = jnp.concatenate([w2_high, w2_high, w2_low], axis=1)

        def product(at):
            cols = slice(at, at + CHUNK)
            high, low = act[h, 0, own, cols], act[h, 1, own, cols]
            value = dot(w2_parts, jnp.concatenate([high, low, high], axis=0))
            mid_ref[:, cols] = value if (h, start) == units[0] else mid_ref[:, cols] + value

        return [functools.partial(product, at) for at in range(0, nodes, CHUNK)]

    for i in range(len(units) + 1):
        if i < len(units) and units[i][1] == 0:
            for copy in ready[units[i][0]]:
                copy.wait()
        weave(
            products(*units[i - 1]) if i else [lambda: None],
            slabs(*units[i]) if i < len(units) else [],
        )
        if i < len(units) and units[i][1] == size:
            h = units[i][0]
            rows = slice(h * width, (h + 1) * width)
            copies.send(act.at[h, 0], act_hbm.at[0, rows, :])
            copies.send(act.at[h, 1], act_hbm.at[1, rows, :])
    keep = mask_ref[...].reshape(1, -1).astype(f32)
    count = jnp.maximum(jnp.sum(keep, axis=1, keepdims=True), 1.0)
    mid = mid_ref[...]
    average = total_row(fold(mid * keep)) / count
    off = mid - wide(as_column(average), nodes)
    square = total_row(fold(off * off * keep))
    put_rows(row_ref, average, square)
    stat_ref[...] = jnp.broadcast_to(row_ref[...][None], stat_ref.shape)
    copies.finish()


def put_rows(row_ref, *rows):
    at = 0
    for row in rows:
        for start in range(0, row.shape[1], LANES):
            row_ref[at : at + 1, :] = row[:, start : start + LANES]
            at += 1


def rows_of(ref, first, count):
    return jnp.concatenate([ref[:, i, :] for i in range(first, first + count)], axis=1)


def head_kernel(
    pay_ref, stat_ref, gain_ref, bias_ref, slope_ref, ow_ref, ob_ref, label_ref, mask_ref, mid_ref,
    logit_ref, inv_ref, sums_ref, misc_ref, up_ref, norm_ref,
    ow_scr, ob_scr, row_ref, half_ref, tan_ref, acat_ref, col_ref, back_ref, acc_ref, misc_scr,
):
    width, nodes = mid_ref.shape
    classes = ow_ref.shape[0]
    tiles = width // LANES
    counts = real_nodes(pay_ref)
    total = jnp.sum(counts, axis=0, keepdims=True)
    means = rows_of(stat_ref, 0, tiles)
    average = jnp.sum(counts * means, axis=0, keepdims=True) / total
    off = means - average
    square = jnp.sum(rows_of(stat_ref, tiles, tiles) + counts * off * off, axis=0, keepdims=True)
    inverse = lax.rsqrt(square / total + epsilon)
    inv_ref[...] = inverse
    col_ref[0] = as_column(average)
    col_ref[1] = as_column(inverse)
    col_ref[2] = 0.5 * as_column(gain_ref[...])
    col_ref[3] = 0.5 * as_column(bias_ref[...])
    slope = as_column(slope_ref[...])
    col_ref[4] = 0.5 + 0.5 * slope
    col_ref[5] = 0.5 - 0.5 * slope
    ow_scr[...] = jnp.zeros_like(ow_scr)
    ow_scr[:classes, :] = ow_ref[...]
    ow_t = split(ow_scr[:CLASS_ROWS, :])
    ow = split(ow_scr[...].T)
    ob_scr[...] = jnp.zeros_like(ob_scr)
    ob_scr[:, :classes] = ob_ref[...]
    ob_col = wide(as_column(ob_scr[...])[:CLASS_ROWS], nodes)
    rows = 16
    for r in range(0, width, rows):
        rs = slice(r, r + rows)
        mean, inv, gain, bias, p, q = (wide(col_ref[i, rs], nodes) for i in range(6))
        normed = (mid_ref[rs, :] - mean) * inv
        norm_ref[rs, :] = normed
        half = normed * gain + bias
        tangent = jnp.tanh(half)
        half_ref[rs, :] = half
        tan_ref[rs, :] = tangent
        high, low = split(2.0 * half * (p + q * tangent))
        acat_ref[rs, :] = high
        acat_ref[slice(width + r, width + r + rows), :] = low
    high, low = acat_ref[:width, :], acat_ref[width:, :]
    logits = dot(jnp.concatenate([ow_t[0], ow_t[0]], axis=1), acat_ref[...]) + dot(ow_t[1], high)
    logits = logits + ob_col
    logit_ref[...] = logits[:classes]
    keep = mask_ref[...].reshape(1, -1).astype(f32)
    place = lax.broadcasted_iota(jnp.int32, (CLASS_ROWS, nodes), 0)
    logits = jnp.where(place < classes, logits, -3.0e38)
    shifted = logits - jnp.max(logits, axis=0, keepdims=True)
    weights = jnp.exp(shifted)
    norm = jnp.sum(weights, axis=0, keepdims=True)
    onehot = place == label_ref[...].reshape(1, -1)
    picked = jnp.sum(jnp.where(onehot, shifted, 0.0), axis=0, keepdims=True)
    loss = jnp.sum(fold(keep * (jnp.log(norm) - picked)), axis=1, keepdims=True)
    grad = keep * (weights * (1.0 / norm) - jnp.where(onehot, 1.0, 0.0))
    grad_sum = fold(grad)
    grad_high, grad_low = split(pad_rows(grad, LANES))
    gcat = jnp.concatenate([grad_high, grad_low, grad_high], axis=0)
    owcat = jnp.concatenate([ow[0], ow[0], ow[1]], axis=1)

    def back(start):
        back_ref[:, start : start + CHUNK] = dot(owcat, gcat[:, start : start + CHUNK])

    for start in range(0, nodes, CHUNK):
        back(start)
    both = jnp.concatenate([grad_high, grad_low], axis=0)

    def weight_grad():
        value = dot_nt(both, high)
        value = value[:CLASS_ROWS] + value[LANES : LANES + CLASS_ROWS]
        misc_scr[:CLASS_ROWS, :] = value + dot_nt(grad_high[:CLASS_ROWS], low)

    def slab(r):
        rs = slice(r, r + rows)
        p, q = wide(col_ref[4, rs], nodes), wide(col_ref[5, rs], nodes)
        half, tangent, act_grad = half_ref[rs, :], tan_ref[rs, :], back_ref[rs, :]
        away = half * (1.0 - tangent)
        acc_ref[0, rs] = fold(act_grad * away)
        up = act_grad * (p + q * (tangent + away * (1.0 + tangent)))
        up_ref[rs, :] = up
        acc_ref[1, rs] = fold(up)
        acc_ref[2, rs] = fold(up * norm_ref[rs, :])

    slabs = [functools.partial(slab, r) for r in range(0, width, rows)]
    weave([weight_grad, lambda: None], slabs)
    put_rows(row_ref, total_row(acc_ref[1]), total_row(acc_ref[2]))
    sums_ref[...] = jnp.broadcast_to(row_ref[...][None], sums_ref.shape)
    misc_scr[CLASS_ROWS:, :] = jnp.zeros((HEAD_ROWS - CLASS_ROWS, width), f32)
    misc_scr[CLASS_ROWS : CLASS_ROWS + 1, :] = total_row(acc_ref[0])
    misc_scr[CLASS_ROWS + 1 : CLASS_ROWS + 2, :LANES] = total_row(pad_rows(grad_sum, LANES))
    misc_scr[CLASS_ROWS + 2 : CLASS_ROWS + 3, :1] = loss
    for t in range(tiles):
        misc_ref[t] = misc_scr[:, t * LANES : (t + 1) * LANES]


def mid_grad_kernel(
    code_ref, pay_ref, sums_ref, inv_ref, gain_ref, mask_ref, up_ref, norm_ref, act_hbm,
    out_ref, bg_ref, gcat,
    act, sems,
):
    width, nodes = up_ref.shape
    ready = act_in(1, code_ref, Copies(sems), act_hbm, act)
    tiles = width // LANES
    total = jnp.sum(real_nodes(pay_ref), axis=0, keepdims=True)
    bias_sum = jnp.sum(rows_of(sums_ref, 0, tiles), axis=0, keepdims=True)
    gain_sum = jnp.sum(rows_of(sums_ref, tiles, tiles), axis=0, keepdims=True)
    bg_ref[0:1, :] = bias_sum
    bg_ref[1:2, :] = gain_sum
    scale = as_column(gain_ref[...] * inv_ref[...])
    bias_col = as_column(bias_sum / total)
    gain_col = as_column(gain_sum / total)
    keep = mask_ref[...].reshape(1, -1).astype(f32)
    rows = 16
    for r in range(0, width, rows):
        rs = slice(r, r + rows)
        bias, gain = wide(bias_col[rs], nodes), wide(gain_col[rs], nodes)
        grad = up_ref[rs, :] - bias - norm_ref[rs, :] * gain
        high, low = split(keep * (wide(scale[rs], nodes) * grad))
        gcat[rs, :] = high
        gcat[width + r : width + r + rows, :] = low
    mid_product(code_ref, ready, act, gcat, out_ref)


def act_in(half_sel, code_ref, copies, act_hbm, act):
    parts, _, width, _ = act.shape
    rows = width // 2
    ready = []
    for s in range(parts):
        for r in (0, 1):
            block = (s * 2 + (half_sel ^ (code_ref[s] >> 4))) * 2 + r
            ready.append([
                copies.start(act_hbm.at[i, aligned(block, rows)], act.at[s, i, r * rows : (r + 1) * rows])
                for i in (0, 1)
            ])
    return ready


def mid_product(code_ref, ready, act, gcat, out_ref):
    parts, width, mid = out_ref.shape
    rows = width // PIECES
    size = width // 2
    for s in range(parts):
        code = code_ref[s] & (PIECES - 1)
        for r in (0, 1):
            for copy in ready[s * 2 + r]:
                copy.wait()
            here = slice(r * size, (r + 1) * size)
            high, low = act[s, 0, here, :], act[s, 1, here, :]
            value = dot_nt(
                jnp.concatenate([high, high, low], axis=1),
                jnp.concatenate([gcat[:mid, :], gcat[mid:, :], gcat[:mid, :]], axis=1),
            )
            for i in range(size // rows):
                place = (r * (size // rows) + i) ^ code
                out_ref[s, aligned(place, rows), :] = value[i * rows : (i + 1) * rows]


def mid_grad_rest_kernel(code_ref, gcat, act_hbm, out_ref, act, sems):
    ready = act_in(0, code_ref, Copies(sems), act_hbm, act)
    mid_product(code_ref, ready, act, gcat, out_ref)


def backward_kernel(
    code_ref, pay_ref, inv_ref, gain_ref, colpack_ref, w_ref, gram_ref, misc_ref,
    g, w2, pre_hbm, xcat_hbm,
    pack_ref, feat_hbm,
    pre, xcat, feat, col, down, ucat, acc, prod, rows_scr, shift_col, sems,
):
    copies = Copies(sems)
    hops, feats, width = w_ref.shape
    mid, nodes = g.shape[0] // 2, g.shape[1]
    tiles = mid // LANES
    size = 2 * CHUNK
    chunks = [slice(start, start + size) for start in range(0, nodes, size)]
    count = len(chunks)
    stages = [(h, j) for h in range(hops) for j in range(count)]
    z_in, x_in = {}, {}
    for h in range(hops):
        own = slice(h * width, (h + 1) * width)
        for j, c in enumerate(chunks):
            z_in[h, j] = copies.start(pre_hbm.at[own, c], pre.at[h, :, c])
        x_in[h] = copies.start(xcat_hbm.at[h], xcat.at[h])
    devices = pay_ref.shape[0]
    flip = code_ref[1] * (tiles // 2)
    at = hops * HOP_ROWS
    for t in range(tiles):
        pack_ref[t ^ flip, at : at + HEAD_ROWS, :] = misc_ref[t]
    w2cat, wcat = {}, {}

    def columns(h):
        rows = 64
        for r in range(0, width, rows):
            for k, values in enumerate(columns_of(colpack_ref[h, r : r + rows, :])):
                col[h % 2, k, r : r + rows, :] = values

    def weights(h):
        high, low = split(pad_rows(w_ref[h], LANES) * (gain_ref[h] * inv_ref[h]))
        wcat[h] = (jnp.concatenate([high, low], axis=0), high)
        high, low = split(0.5 * w2[h * width : (h + 1) * width, :])
        w2cat[h] = jnp.concatenate([high, high, low], axis=1)

    def part_of(j, part):
        return slice(chunks[j].start + part * CHUNK, chunks[j].start + (part + 1) * CHUNK)

    def down_product(index, part):
        h, j = stages[index]
        cs = part_of(j, part)
        high, low = g[:mid, cs], g[mid:, cs]
        value = dot(w2cat[h], jnp.concatenate([high, low, high], axis=0))
        down[index % 2, :, part * CHUNK : (part + 1) * CHUNK] = value

    def slab(index, r, rows):
        h, j = stages[index]
        two = h % 2
        rs, cs = slice(r, r + rows), chunks[j]
        scale, shift, p1, q1, p2, q2 = (wide(col[two, k, rs], size) for k in range(6))
        half1 = pre[h, rs, cs] * scale + shift
        grad2 = down[index % 2, rs, :]
        tan1 = jnp.tanh(half1)
        half2 = half1 * (p1 + q1 * tan1)
        tan2 = jnp.tanh(half2)
        away2 = half2 * (1.0 - tan2)
        add(acc, two, 0, rs, j, fold(grad2 * away2))
        grad1 = grad2 * (p2 + q2 * (tan2 + away2 * (1.0 + tan2)))
        away1 = half1 * (1.0 - tan1)
        add(acc, two, 1, rs, j, fold(grad1 * away1))
        grad = grad1 * (p1 + q1 * (tan1 + away1 * (1.0 + tan1)))
        high, low = split(grad)
        ucat[two, rs, cs] = high
        ucat[two, width + r : width + r + rows, cs] = low

    def add(acc, two, k, rs, j, value):
        acc[two, k, rs] = value if j == 0 else acc[two, k, rs] + value

    def feature_product(index, part):
        h, j = stages[index]
        cs = part_of(j, part)
        value = dot(wcat[h][0], ucat[h % 2, :width, cs])
        value = value[:LANES] + value[LANES:] + dot(wcat[h][1], ucat[h % 2, width:, cs])
        feat[h, :, cs] = value[:feats]

    def weight_product(h):
        value = dot_nt(xcat[h], ucat[h % 2, :width, :])
        low = dot_nt(xcat[h, :LANES, :], ucat[h % 2, width:, :])
        prod[h % 2] = value[:LANES] + value[LANES:] + low

    def shifts(h):
        shift = feature_shift(pay_ref, h)
        rows_scr[h, :devices, :] = shift
        rows_scr[h, devices:, :] = jnp.broadcast_to(real_nodes(pay_ref), shift.shape)
        own_shift = rows_scr[h, pl.ds(code_ref[0], 1), :]
        own_count = rows_scr[h, pl.ds(devices + code_ref[0], 1), :]
        shift_col[h] = as_column(own_shift)
        gram = gram_ref[h] + shift_col[h] * (own_shift * own_count)
        pack_ref[h ^ flip, at + HEAD_ROWS :, :] = gram[:HOP_ROWS]

    def pack(h):
        two = h % 2
        bias_sum = prod[two, feats : feats + 1, :]
        prod[two] = prod[two] + wide(shift_col[h], mid) * bias_sum
        prod[two, feats + 1 : feats + 2, :] = total_row(acc[two, 1])
        prod[two, feats + 2 : feats + 3, :] = 2.0 * total_row(acc[two, 0])
        for t in range(tiles):
            pack_ref[t ^ flip, h * HOP_ROWS : (h + 1) * HOP_ROWS, :] = prod[
                two, :HOP_ROWS, t * LANES : (t + 1) * LANES
            ]

    rows = 16
    weights(0)
    weave(
        [functools.partial(down_product, 0, part) for part in (0, 1)],
        [functools.partial(columns, 0)] + [functools.partial(shifts, h) for h in range(hops)],
    )
    for index, (h, j) in enumerate(stages):
        products = []
        z_in[h, j].wait()
        if j + 1 == count:
            x_in[h].wait()
            if h + 1 < hops:
                weights(h + 1)
                columns(h + 1)
        if index + 1 < len(stages):
            products += [functools.partial(down_product, index + 1, part) for part in (0, 1)]
        if index >= 1:
            before = [functools.partial(feature_product, index - 1, part) for part in (0, 1)]
            products = before + products
        if j == 1 and h >= 1:
            products.append(functools.partial(weight_product, h - 1))
        slabs = [functools.partial(slab, index, r, rows) for r in range(0, width, rows)]
        if j == 2 and h >= 1:
            copies.send(feat.at[h - 1], feat_hbm.at[h - 1])
            slabs.insert(len(slabs) // 2, functools.partial(pack, h - 1))
        weave(products, slabs)
    for part in (0, 1):
        feature_product(len(stages) - 1, part)
    copies.send(feat.at[hops - 1], feat_hbm.at[hops - 1])
    weight_product(hops - 1)
    pack(hops - 1)
    copies.finish()


def finish_kernel(
    code_ref, pay_ref, inv_ref, mine_ref, other_ref, w_ref, gain_ref, mask_ref, bg_ref, xcat_hbm,
    feat_hbm, fgrad_hbm, wgrad_hbm, gain_out, bias_out, slope1_out, slope2_out, mgain_out, mbias_out, mslope_out,
    owg_out, obg_out, loss_out,
    sum_ref, rows_scr, fgrad, wgrad, feat, xcat, sems,
):
    hops, feats, width = w_ref.shape
    tiles = mine_ref.shape[0] * 2
    half = tiles // 2
    flip = code_ref[1]
    copies = Copies(sems)
    ready = []
    for h in range(hops):
        ready.append((copies.start(feat_hbm.at[h], feat.at[h]), copies.start(xcat_hbm.at[h], xcat.at[h])))

    @pl.when(flip == 0)
    def _():
        for t in range(half):
            sum_ref[:, t * LANES : (t + 1) * LANES] = mine_ref[t]
            sum_ref[:, (half + t) * LANES : (half + t + 1) * LANES] = other_ref[t]

    @pl.when(flip != 0)
    def _():
        for t in range(half):
            sum_ref[:, t * LANES : (t + 1) * LANES] = other_ref[t]
            sum_ref[:, (half + t) * LANES : (half + t + 1) * LANES] = mine_ref[t]

    counts = real_nodes(pay_ref)
    total = jnp.sum(counts, axis=0, keepdims=True)
    keep = mask_ref[...].reshape(1, -1).astype(f32)
    at = hops * HOP_ROWS
    for h in range(hops):
        base = h * HOP_ROWS
        w = pad_rows(w_ref[h], LANES)
        inverse = inv_ref[h]
        scale = gain_ref[h] * inverse
        bias_sum = sum_ref[base + feats : base + feats + 1, :]
        slope1_out[h] = sum_ref[base + feats + 1 : base + feats + 2, :]
        slope2_out[h] = sum_ref[base + feats + 2 : base + feats + 3, :]
        products = sum_ref[base : base + feats, :]
        gain_sum = inverse * jnp.sum(w_ref[h] * products, axis=0, keepdims=True)
        bias_out[h] = bias_sum
        gain_out[h] = gain_sum
        gram = sum_ref[at + HEAD_ROWS : at + HEAD_ROWS + HOP_ROWS, h * LANES : (h + 1) * LANES]
        inner = dot(gram, w, exact)[:feats] * (inverse * gain_sum / total)
        wgrad[h] = scale * (products - inner)
        copies.send(wgrad.at[h], wgrad_hbm.at[:, h, :])
        shift = feature_shift(pay_ref, h)
        rows_scr[...] = shift
        own_shift = rows_scr[pl.ds(code_ref[0], 1), :]
        mix = dot_nt(w * (scale * inverse * gain_sum / total), w, exact)
        lane = lax.broadcasted_iota(jnp.int32, (1, LANES), 1)
        off = jnp.sum(w * (scale * bias_sum / total), axis=1, keepdims=True)
        off = off + jnp.sum(mix * jnp.where(lane < feats, own_shift, 0.0), axis=1, keepdims=True)
        high, low = split(mix)
        for copy in ready[h]:
            copy.wait()
        mixed = dot(jnp.concatenate([high, high], axis=1), xcat[h]) + dot(low, xcat[h, :LANES])
        fgrad[h] = keep * (feat[h] - (mixed + off)[:feats])
        copies.send(fgrad.at[h], fgrad_hbm.at[:, h, :])
    owg_out[...] = sum_ref[at : at + owg_out.shape[0], :]
    mslope_out[...] = sum_ref[at + CLASS_ROWS : at + CLASS_ROWS + 1, :]
    obg_out[...] = sum_ref[at + CLASS_ROWS + 1 : at + CLASS_ROWS + 2, : obg_out.shape[1]]
    loss_out[...] = sum_ref[at + CLASS_ROWS + 2 : at + CLASS_ROWS + 3, :1] / total
    mbias_out[...] = bg_ref[0:1, :]
    mgain_out[...] = bg_ref[1:2, :]
    copies.finish()


def place_kernel(pieces, code_ref, *refs):
    out_ref, sems = refs[-2:]
    copies = Copies(sems)
    for ref, (s, first, rows) in zip(refs, pieces):
        for i in range(ref.shape[0] // rows):
            block = s * 2 * PIECES + ((first + i) ^ code_ref[s])
            copies.send(ref.at[pl.ds(i * rows, rows)], out_ref.at[aligned(block, rows)])
    copies.finish()


def exchange(values, bit, devices):
    return lax.ppermute(values, axes, [(i, i ^ (1 << bit)) for i in range(devices)])


def exchange_two(a, bit_a, b, bit_b, devices):
    a, b = lax.optimization_barrier((a, b))
    return lax.optimization_barrier((exchange(a, bit_a, devices), exchange(b, bit_b, devices)))


def swap_halves(a, bit_a, b, bit_b, devices):
    size = a.shape[0] // 2
    ra, rb = exchange_two(a[size:], bit_a, b[size:], bit_b, devices)
    return a[:size] + ra, b[:size] + rb


def code_of(me, order):
    code = 0
    for bit in order:
        code = code * 2 + ((me >> bit) & 1)
    return code


def after(values, *others):
    return lax.optimization_barrier((values, *others))[0]


def on_device(
    devices,
    hop_features,
    branch_weight,
    branch_gain,
    branch_bias,
    first_slope,
    second_slope,
    mid_weight,
    mid_gain,
    mid_bias,
    mid_slope,
    out_weight,
    out_bias,
    labels,
    valid_mask,
):
    hops, feats, nodes = hop_features.shape
    width = branch_weight.shape[2]
    mid = mid_weight.shape[1]
    classes = out_weight.shape[1]
    tiles = mid // LANES
    bits = devices.bit_length() - 1
    me = lax.axis_index(axes).astype(jnp.int32)
    rest = tuple(range(5, bits))
    codes = jnp.stack([code_of(me, (0, 1, 2, 3, 4)), code_of(me, (0, 2, 1, 3, 4))])
    place_code = jnp.stack([me, me & 1])
    shape = jax.ShapeDtypeStruct
    by_hop = lambda v: v.reshape(hops, 1, width)
    gain, bias, slope1, slope2 = map(by_hop, (branch_gain, branch_bias, first_slope, second_slope))
    row = lambda v: v.reshape(1, -1)
    gather = functools.partial(
        lax.all_to_all, axis_name=axes, split_axis=0, concat_axis=0, tiled=True
    )
    dma = pltpu.SemaphoreType.DMA
    scratch = lambda dtype, *dims: pltpu.VMEM(dims, dtype)
    mask = valid_mask

    pay, gram, xcat, w = call(
        stats_kernel,
        60,
        in_specs=[anywhere, anywhere, vmem],
        out_specs=[vmem, vmem, anywhere, anywhere],
        out_shape=(
            shape((devices, hops, width + LANES), f32), shape((hops, LANES, LANES), f32),
            shape((hops, 2 * LANES, nodes), bf16), shape((hops, feats, width), f32),
        ),
        scratch_shapes=[
            scratch(f32, hops, feats, nodes), scratch(f32, hops, feats, width),
            scratch(bf16, hops, 2 * LANES, nodes), scratch(f32, hops, width + LANES), dma((4 * hops,)),
        ],
        cost_estimate=cost(1_000_000_000, 8_000_000),
        name="first_stats",
    )(jnp.transpose(hop_features, (1, 0, 2)), jnp.transpose(branch_weight, (1, 0, 2)), mask)
    pay = gather(after(pay, codes, place_code))

    pre, w2cat = call(
        prepare_kernel,
        60,
        in_specs=[anywhere, vmem, anywhere],
        out_specs=[anywhere] * 2,
        out_shape=(shape((hops * width, nodes), f32), shape((hops, mid, 2 * width), bf16)),
        scratch_shapes=[
            scratch(bf16, hops, 2 * LANES, nodes), scratch(f32, hops, width, mid),
            scratch(f32, hops, width, nodes), scratch(bf16, hops, mid, 2 * width), dma((4 * hops,)),
        ],
        cost_estimate=cost(4 * 2 * 4 * hops * LANES * width * nodes, 20_000_000),
        name="prepare",
    )(xcat, w, mid_weight)

    mid_pre, stat, first_inv, colpack, act = call(
        forward_kernel,
        45,
        in_specs=[smem] + [vmem] * 7 + [anywhere] * 2,
        out_specs=[vmem] * 4 + [anywhere],
        out_shape=(
            shape((mid, nodes), f32), shape((devices, 8, LANES), f32), shape((hops, 1, width), f32),
            shape((hops, width, LANES), f32), shape((2, hops * width, nodes), bf16),
        ),
        scratch_shapes=[
            scratch(f32, hops, width, nodes), scratch(bf16, hops, mid, 2 * width),
            scratch(bf16, hops, 2, width, nodes), scratch(f32, hops, devices, width),
            scratch(f32, 8, LANES), dma((4 * hops,)),
        ],
        cost_estimate=cost(3 * 2 * hops * width * mid * nodes, 20_000_000),
        name="forward",
    )(place_code, pay, w, gain, bias, slope1, slope2, mask, pre, w2cat)
    stat = gather(stat)

    logits, mid_inv, sums, misc, up, normed = call(
        head_kernel,
        40,
        in_specs=[vmem] * 10,
        out_specs=[vmem] * 6,
        out_shape=(
            shape((classes, nodes), f32), shape((1, mid), f32), shape((devices, 8, LANES), f32),
            shape((tiles, HEAD_ROWS, LANES), f32), shape((mid, nodes), f32), shape((mid, nodes), f32),
        ),
        scratch_shapes=[
            scratch(f32, LANES, mid), scratch(f32, 1, LANES), scratch(f32, 8, LANES),
            scratch(f32, mid, nodes), scratch(f32, mid, nodes), scratch(bf16, 2 * mid, nodes),
            scratch(f32, 6, mid, LANES), scratch(f32, mid, nodes), scratch(f32, 3, mid, LANES),
            scratch(f32, HEAD_ROWS, mid),
        ],
        cost_estimate=cost(2_000_000_000, 10_000_000),
        name="head",
    )(pay, stat, row(mid_gain), row(mid_bias), row(mid_slope), out_weight.T, row(out_bias), labels, mask, mid_pre)
    sums = gather(sums)

    product_cost = cost(2 * 3 * 2 * width * mid * nodes, 10_000_000)
    send, mid_bg, gcat = call(
        mid_grad_kernel,
        36,
        in_specs=[smem] + [vmem] * 7 + [anywhere],
        out_specs=[vmem] * 3,
        out_shape=(
            shape((2, width, mid), f32), shape((2, mid), f32), shape((2 * mid, nodes), bf16),
        ),
        scratch_shapes=[scratch(bf16, 2, 2, width, nodes), dma((8,))],
        cost_estimate=product_cost,
        name="mid_grad_send",
    )(codes, pay, sums, mid_inv, row(mid_gain), mask, up, normed, act)
    came = exchange(send, 0, devices)
    kept = call(
        mid_grad_rest_kernel,
        40,
        in_specs=[smem, vmem, anywhere],
        out_specs=vmem,
        out_shape=shape((2, width, mid), f32),
        scratch_shapes=[scratch(bf16, 2, 2, width, nodes), dma((8,))],
        cost_estimate=product_cost,
        name="mid_grad_keep",
    )(codes, gcat, act)

    pack_rows = hops * HOP_ROWS + HEAD_ROWS + HOP_ROWS

    def backward(gcat):
        return call(
            backward_kernel,
            42,
            in_specs=[smem] + [vmem] * 9 + [anywhere] * 2,
            out_specs=[vmem, anywhere],
            scratch_shapes=[
                scratch(f32, hops, width, nodes), scratch(bf16, hops, 2 * LANES, nodes),
                scratch(f32, hops, feats, nodes), scratch(f32, 2, 6, width, LANES),
                scratch(f32, 2, width, 2 * CHUNK), scratch(bf16, 2, 2 * width, nodes),
                scratch(f32, 2, 2, width, LANES), scratch(f32, 2, LANES, mid),
                scratch(f32, hops, 2 * devices, LANES), scratch(f32, hops, LANES, LANES),
                dma((3 * hops + (hops + 1) * nodes // CHUNK,)),
            ],
            out_shape=(shape((tiles, pack_rows, LANES), f32), shape((hops, feats, nodes), f32)),
            cost_estimate=cost(hops * 2 * 4 * width * mid * nodes, 24_000_000),
            name="backward",
        )(place_code, pay, first_inv, gain, colpack, w, gram, misc, gcat, mid_weight, pre, xcat)

    a, b = kept[0] + came[0], kept[1] + came[1]
    size = a.shape[0] // 2
    send_a, send_b = a[size:], b[size:]
    ra = exchange(send_a, 1, devices)
    rb = exchange(send_b, 2, devices)
    pack, feat = backward(after(gcat, send_a, send_b))
    a, b = a[:size] + after(ra, pack), b[:size] + after(rb, pack)

    half = tiles // 2
    groups = {}
    for i in range(devices):
        groups.setdefault(i & ~14, []).append(i)
    spread = functools.partial(
        lax.all_to_all, axis_name=axes, split_axis=0, concat_axis=0,
        axis_index_groups=list(groups.values()), tiled=True,
    )
    pack = after(pack, a, b)
    pack = pack[:half] + exchange(pack[half:], 0, devices)
    a, b, pack = lax.optimization_barrier((a, b, pack))
    a, b = swap_halves(a, 2, b, 1, devices)
    pack = spread(pack.reshape(8, -1, LANES))
    part = a.shape[0] // 4
    both = jnp.stack([a.reshape(4, part, mid), b.reshape(4, part, mid)], axis=1)
    both = both[:2] + exchange(both[2:], 3, devices)
    pack = pack.sum(axis=0)
    pack, both = lax.optimization_barrier((pack, both))
    came, pack_came = lax.optimization_barrier(
        (exchange(both[1:], 4, devices), exchange(pack, 4, devices))
    )
    both, pack = both[:1] + came, pack + pack_came
    for bit in rest:
        both, pack = both + exchange(both, bit, devices), pack + exchange(pack, bit, devices)
    pack = jnp.broadcast_to(pack[None], (8,) + pack.shape)
    pack, both = lax.optimization_barrier((pack, both))
    pack = spread(pack).reshape(half, pack_rows, LANES)
    both = jnp.concatenate([both, exchange(both, 4, devices)])
    both = jnp.concatenate([both, exchange(both, 3, devices)])
    a, b = both[:, 0].reshape(-1, mid), both[:, 1].reshape(-1, mid)
    ra, rb = exchange_two(a, 2, b, 1, devices)
    a, b = jnp.concatenate([a, ra]), jnp.concatenate([b, rb])
    a, b = lax.optimization_barrier((a, b))
    ra, rb = exchange(a, 1, devices), exchange(b, 2, devices)
    other_a, other_b = exchange(a, 0, devices), exchange(b, 0, devices)
    pack_other = exchange(pack, 0, devices)

    rows_out = [shape((hops, 1, width), f32)] * 4
    rows_mid = [shape((1, mid), f32)] * 3
    (
        feature_grad, branch_weight_grad, branch_gain_grad, branch_bias_grad, first_slope_grad,
        second_slope_grad, mid_gain_grad, mid_bias_grad, mid_slope_grad, out_weight_grad,
        out_bias_grad, mean_loss,
    ) = call(
        finish_kernel,
        60,
        in_specs=[smem] + [vmem] * 8 + [anywhere] * 2,
        out_specs=[anywhere, anywhere] + [vmem] * 10,
        scratch_shapes=[
            scratch(f32, pack_rows, mid), scratch(f32, devices, LANES), scratch(f32, hops, feats, nodes),
            scratch(f32, hops, feats, width), scratch(f32, hops, feats, nodes),
            scratch(bf16, hops, 2 * LANES, nodes), dma((4 * hops,)),
        ],
        out_shape=(
            shape((feats, hops, nodes), f32), shape((feats, hops, width), f32), *rows_out, *rows_mid,
            shape((classes, mid), f32), shape((1, classes), f32), shape((1, 1), f32),
        ),
        cost_estimate=cost(0, 20_000_000),
        name="finish",
    )(place_code, pay, first_inv, pack, pack_other, w, gain, mask, mid_bg, xcat, feat)

    rows = mid_weight.shape[0] // (4 * PIECES)
    eight = PIECES // 2

    def place(pieces, *base):
        values = [value for value, *_ in pieces]
        kinds = [(s, first, rows) for _, s, first in pieces]
        return call(
            functools.partial(place_kernel, kinds),
            16,
            in_specs=[smem] + [vmem] * len(values) + [anywhere] * len(base),
            out_specs=anywhere,
            scratch_shapes=[dma((len(values) * eight,))],
            out_shape=shape(mid_weight.shape, f32),
            input_output_aliases={1 + len(values): 0} if base else {},
            cost_estimate=cost(0, 4_000_000),
            name="place",
        )(codes, *values, *base)

    grad = place(
        [(a, 0, 0), (b, 1, 0), (other_a, 0, PIECES), (after(other_b, mid_bias_grad), 1, PIECES)]
    )
    ra, rb, grad = lax.optimization_barrier((ra, rb, grad))
    other_ra, other_rb = exchange(ra, 0, devices), exchange(rb, 0, devices)
    grad = place([(ra, 0, eight), (rb, 1, eight)], grad)
    mid_weight_grad = place(
        [(other_ra, 0, PIECES + eight), (after(other_rb, grad), 1, PIECES + eight)], grad
    )

    flat = lambda v: v.reshape(-1)
    return (
        logits,
        mean_loss.reshape(()),
        jnp.transpose(feature_grad, (1, 0, 2)),
        jnp.transpose(branch_weight_grad, (1, 0, 2)),
        flat(branch_gain_grad),
        flat(branch_bias_grad),
        flat(first_slope_grad),
        flat(second_slope_grad),
        mid_weight_grad,
        flat(mid_gain_grad),
        flat(mid_bias_grad),
        flat(mid_slope_grad),
        out_weight_grad.T,
        flat(out_bias_grad),
    )


def solution(mesh):
    devices = mesh.shape["dp"] * mesh.shape["rep"]

    def body(*arrays):
        return on_device(devices, *arrays)

    nodes = P(("dp", "rep"))
    return jax.shard_map(
        body,
        mesh=mesh,
        in_specs=(P(None, None, ("dp", "rep")),) + (P(),) * 11 + (nodes, nodes),
        out_specs=(P(None, ("dp", "rep")), P(), P(None, None, ("dp", "rep"))) + (P(),) * 11,
        check_vma=False,
    )
```

```python
import functools

import jax
import jax.numpy as jnp
from jax import lax
from jax.experimental import pallas as pl
from jax.experimental.pallas import tpu as pltpu
from jax.sharding import PartitionSpec as P

epsilon = 1e-05
axes = ("dp", "rep")
exact = lax.Precision.HIGHEST
f32 = jnp.float32
bf16 = jnp.bfloat16
LANES = 128
CHUNK = 256
PIECES = 16
HOP_ROWS = 104
HEAD_ROWS = 56
CLASS_ROWS = 48


def dot(left, right, precision=None):
    return lax.dot_general(
        left, right, (((1,), (0,)), ((), ())), precision=precision, preferred_element_type=f32
    )


def dot_nt(left, right, precision=None):
    return lax.dot_general(
        left, right, (((1,), (1,)), ((), ())), precision=precision, preferred_element_type=f32
    )


def split(values):
    high = values.astype(bf16)
    return high, (values - high.astype(f32)).astype(bf16)


def as_column(row):
    return jnp.broadcast_to(row, (LANES, row.shape[1])).T


def wide(column, width):
    return jnp.concatenate([column] * (width // LANES), axis=1)


def fold(values):
    total = values[:, :LANES]
    for start in range(LANES, values.shape[1], LANES):
        total = total + values[:, start : start + LANES]
    return total


def total_row(partial):
    return jnp.sum(partial.T, axis=0, keepdims=True)


def pad_rows(values, rows):
    return jnp.concatenate(
        [values, jnp.zeros((rows - values.shape[0], values.shape[1]), values.dtype)], axis=0
    )


def weave(products, slabs):
    done = 0
    for j, product in enumerate(products):
        until = (j + 1) * len(slabs) // len(products)
        for slab in slabs[done:until]:
            slab()
        done = until
        product()


def cost(flops=0, bytes_accessed=0):
    return pl.CostEstimate(flops=flops, bytes_accessed=bytes_accessed, transcendentals=0)


def call(kernel, mib, **options):
    return pl.pallas_call(
        kernel, compiler_params=pltpu.CompilerParams(vmem_limit_bytes=mib * 1024 * 1024), **options
    )


class Copies:
    def __init__(self, sems):
        self.sems = sems
        self.used = 0
        self.waiting = []

    def start(self, source, target):
        copy = pltpu.make_async_copy(source, target, self.sems.at[self.used])
        self.used += 1
        copy.start()
        return copy

    def send(self, source, target):
        self.waiting.append(self.start(source, target))

    def finish(self):
        for copy in self.waiting:
            copy.wait()


anywhere = pl.BlockSpec(memory_space=pl.ANY)
vmem = pl.BlockSpec(memory_space=pltpu.VMEM)
smem = pl.BlockSpec(memory_space=pltpu.SMEM)


def aligned(index, step):
    return pl.ds(pl.multiple_of(index * step, step), step)


def stats_kernel(
    x_hbm, w_hbm, mask_ref,
    pay_ref, gram_ref, xcat_hbm, w_out,
    x_scr, w_scr, xcat_ref, row_ref, sems,
):
    copies = Copies(sems)
    hops, feats, _ = x_scr.shape
    x_in, w_in = [], []
    for h in range(hops):
        x_in.append(copies.start(x_hbm.at[:, h, :], x_scr.at[h]))
        w_in.append(copies.start(w_hbm.at[:, h, :], w_scr.at[h]))
    keep = mask_ref[...].reshape(1, -1).astype(f32)
    count = jnp.sum(keep, axis=1, keepdims=True)
    safe = jnp.maximum(count, 1.0)
    row_ref[...] = jnp.zeros_like(row_ref)
    means, grams = [], []
    place = lax.broadcasted_iota(jnp.int32, (LANES, x_scr.shape[2]), 0)
    for h in range(hops):
        x_in[h].wait()
        x = x_scr[h]
        means.append(jnp.sum(x * keep, axis=1, keepdims=True) / safe)
        high, low = split(jnp.where(place == feats, 1.0, pad_rows(x - means[h], LANES)))
        xcat_ref[h, :LANES, :] = high
        xcat_ref[h, LANES:, :] = low
        copies.send(xcat_ref.at[h], xcat_hbm.at[h])
    for h in range(hops):
        real = xcat_ref[h] * keep.astype(bf16)
        gram = dot_nt(real, real)
        grams.append(
            (gram[:LANES, :LANES] + gram[LANES:, LANES:]) + (gram[:LANES, LANES:] + gram[LANES:, :LANES])
        )
        gram_ref[h] = grams[h]
    for h in range(hops):
        w_in[h].wait()
        copies.send(w_scr.at[h], w_out.at[h])
    for h in range(hops):
        w = pad_rows(w_scr[h], LANES)
        width = w.shape[1]
        row_ref[h : h + 1, :width] = jnp.sum(dot(grams[h], w, exact) * w, axis=0, keepdims=True)
        mean = pad_rows(jnp.broadcast_to(means[h], (feats, LANES)), LANES).T
        row_ref[h : h + 1, width:] = mean[:1]
        row_ref[h : h + 1, width + LANES - 1 :] = count
    pay_ref[...] = jnp.broadcast_to(row_ref[...][None], pay_ref.shape)
    copies.finish()


def real_nodes(pay_ref):
    return pay_ref[:, 0, pay_ref.shape[2] - 1 :]


def feature_shift(pay_ref, h):
    means = pay_ref[:, h, pay_ref.shape[2] - LANES :]
    counts = means[:, LANES - 1 :]
    total = jnp.sum(counts, axis=0, keepdims=True)
    return means - jnp.sum(counts * means, axis=0, keepdims=True) / total


def prepare_kernel(xcat_hbm, w_ref, w2_hbm, pre_hbm, w2cat_hbm, xcat, w2, pre, w2cat, sems):
    copies = Copies(sems)
    hops, _, width = w_ref.shape
    nodes = xcat.shape[2]
    step = 2 * CHUNK
    quarter = width // 4
    ready = []
    for h in range(hops):
        ready.append(copies.start(xcat_hbm.at[h], xcat.at[h]))
        ready.append(copies.start(w2_hbm.at[h * width : (h + 1) * width, :], w2.at[h]))
    for h in range(hops):
        high, low = split(pad_rows(w_ref[h], LANES).T)
        wcat = jnp.concatenate(
            [jnp.concatenate([high, high], axis=1), jnp.concatenate([low, low], axis=1)], axis=0
        )

        def product(start):
            cols = slice(start, start + step)
            value = dot(wcat, xcat[h, :, cols])
            pre[h, :, cols] = value[:width] + value[width:]

        def turn(i):
            at = i * quarter
            high, low = split(w2[h, at : at + quarter, :].T)
            w2cat[h, :, at : at + quarter] = high
            w2cat[h, :, width + at : width + at + quarter] = low

        ready[2 * h].wait()
        ready[2 * h + 1].wait()
        weave(
            [functools.partial(product, start) for start in range(0, nodes, step)],
            [functools.partial(turn, i) for i in range(4)],
        )
        copies.send(pre.at[h], pre_hbm.at[h * width : (h + 1) * width, :])
        copies.send(w2cat.at[h], w2cat_hbm.at[h])
    copies.finish()


def columns_of(pack):
    rows = pack.shape[0]
    return [jnp.broadcast_to(pack[:, i : i + 1], (rows, LANES)) for i in range(6)]


def forward_kernel(
    code_ref, pay_ref, w_ref, gain_ref, bias_ref, slope1_ref, slope2_ref, mask_ref, pre_hbm, w2cat_hbm,
    mid_ref, stat_ref, inv_ref, colpack_ref, act_hbm,
    pre, w2cat, act, shift_ref, row_ref, sems,
):
    copies = Copies(sems)
    hops, _, width = w_ref.shape
    nodes = mid_ref.shape[1]
    ready = []
    for h in range(hops):
        rows = slice(h * width, (h + 1) * width)
        ready.append((
            copies.start(pre_hbm.at[rows, :], pre.at[h]),
            copies.start(w2cat_hbm.at[h], w2cat.at[h]),
        ))
    counts = real_nodes(pay_ref)
    total = jnp.sum(counts, axis=0, keepdims=True)
    for h in range(hops):
        shift = dot(feature_shift(pay_ref, h), pad_rows(w_ref[h], LANES), exact)
        shift_ref[h] = shift
        squares = pay_ref[:, h, :width]
        square = jnp.sum(squares + counts * shift * shift, axis=0, keepdims=True)
        inverse = lax.rsqrt(square / total + epsilon)
        inv_ref[h] = inverse
        scale = 0.5 * gain_ref[h] * inverse
        rows = [
            scale,
            shift_ref[h, pl.ds(code_ref[0], 1), :] * scale + 0.5 * bias_ref[h],
            0.5 + 0.5 * slope1_ref[h],
            0.5 - 0.5 * slope1_ref[h],
            1.0 + slope2_ref[h],
            1.0 - slope2_ref[h],
        ]
        colpack_ref[h] = pad_rows(jnp.concatenate(rows, axis=0), LANES).T

    size = width // 2
    units = [(h, start) for h in range(hops) for start in (0, size)]

    def slabs(h, start):
        rows = 16

        def slab(r):
            rs = slice(r, r + rows)
            columns = columns_of(colpack_ref[h, rs, :])
            scale, shift, p1, q1, p2, q2 = (wide(c, nodes) for c in columns)
            half = pre[h, rs, :] * scale + shift
            half = half * (p1 + q1 * jnp.tanh(half))
            high, low = split(half * (p2 + q2 * jnp.tanh(half)))
            act[h, 0, rs, :] = high
            act[h, 1, rs, :] = low

        return [functools.partial(slab, r) for r in range(start, start + size, rows)]

    def products(h, start):
        own = slice(start, start + size)
        w2_high, w2_low = w2cat[h, :, own], w2cat[h, :, width + start : width + start + size]
        w2_parts = jnp.concatenate([w2_high, w2_high, w2_low], axis=1)

        def product(at):
            cols = slice(at, at + CHUNK)
            high, low = act[h, 0, own, cols], act[h, 1, own, cols]
            value = dot(w2_parts, jnp.concatenate([high, low, high], axis=0))
            mid_ref[:, cols] = value if (h, start) == units[0] else mid_ref[:, cols] + value

        return [functools.partial(product, at) for at in range(0, nodes, CHUNK)]

    for i in range(len(units) + 1):
        if i < len(units) and units[i][1] == 0:
            for copy in ready[units[i][0]]:
                copy.wait()
        weave(
            products(*units[i - 1]) if i else [lambda: None],
            slabs(*units[i]) if i < len(units) else [],
        )
        if i < len(units) and units[i][1] == size:
            h = units[i][0]
            rows = slice(h * width, (h + 1) * width)
            copies.send(act.at[h, 0], act_hbm.at[0, rows, :])
            copies.send(act.at[h, 1], act_hbm.at[1, rows, :])
    keep = mask_ref[...].reshape(1, -1).astype(f32)
    count = jnp.maximum(jnp.sum(keep, axis=1, keepdims=True), 1.0)
    mid = mid_ref[...]
    average = total_row(fold(mid * keep)) / count
    off = mid - wide(as_column(average), nodes)
    square = total_row(fold(off * off * keep))
    put_rows(row_ref, average, square)
    stat_ref[...] = jnp.broadcast_to(row_ref[...][None], stat_ref.shape)
    copies.finish()


def put_rows(row_ref, *rows):
    at = 0
    for row in rows:
        for start in range(0, row.shape[1], LANES):
            row_ref[at : at + 1, :] = row[:, start : start + LANES]
            at += 1


def rows_of(ref, first, count):
    return jnp.concatenate([ref[:, i, :] for i in range(first, first + count)], axis=1)


def head_kernel(
    pay_ref, stat_ref, gain_ref, bias_ref, slope_ref, ow_ref, ob_ref, label_ref, mask_ref, mid_ref,
    logit_ref, inv_ref, sums_ref, misc_ref, up_ref, norm_ref,
    ow_scr, ob_scr, row_ref, half_ref, tan_ref, acat_ref, col_ref, back_ref, acc_ref, misc_scr,
):
    width, nodes = mid_ref.shape
    classes = ow_ref.shape[0]
    tiles = width // LANES
    counts = real_nodes(pay_ref)
    total = jnp.sum(counts, axis=0, keepdims=True)
    means = rows_of(stat_ref, 0, tiles)
    average = jnp.sum(counts * means, axis=0, keepdims=True) / total
    off = means - average
    square = jnp.sum(rows_of(stat_ref, tiles, tiles) + counts * off * off, axis=0, keepdims=True)
    inverse = lax.rsqrt(square / total + epsilon)
    inv_ref[...] = inverse
    col_ref[0] = as_column(average)
    col_ref[1] = as_column(inverse)
    col_ref[2] = 0.5 * as_column(gain_ref[...])
    col_ref[3] = 0.5 * as_column(bias_ref[...])
    slope = as_column(slope_ref[...])
    col_ref[4] = 0.5 + 0.5 * slope
    col_ref[5] = 0.5 - 0.5 * slope
    ow_scr[...] = jnp.zeros_like(ow_scr)
    ow_scr[:classes, :] = ow_ref[...]
    ow_t = split(ow_scr[:CLASS_ROWS, :])
    ow = split(ow_scr[...].T)
    ob_scr[...] = jnp.zeros_like(ob_scr)
    ob_scr[:, :classes] = ob_ref[...]
    ob_col = wide(as_column(ob_scr[...])[:CLASS_ROWS], nodes)
    rows = 16
    for r in range(0, width, rows):
        rs = slice(r, r + rows)
        mean, inv, gain, bias, p, q = (wide(col_ref[i, rs], nodes) for i in range(6))
        normed = (mid_ref[rs, :] - mean) * inv
        norm_ref[rs, :] = normed
        half = normed * gain + bias
        tangent = jnp.tanh(half)
        half_ref[rs, :] = half
        tan_ref[rs, :] = tangent
        high, low = split(2.0 * half * (p + q * tangent))
        acat_ref[rs, :] = high
        acat_ref[slice(width + r, width + r + rows), :] = low
    high, low = acat_ref[:width, :], acat_ref[width:, :]
    logits = dot(jnp.concatenate([ow_t[0], ow_t[0]], axis=1), acat_ref[...]) + dot(ow_t[1], high)
    logits = logits + ob_col
    logit_ref[...] = logits[:classes]
    keep = mask_ref[...].reshape(1, -1).astype(f32)
    place = lax.broadcasted_iota(jnp.int32, (CLASS_ROWS, nodes), 0)
    logits = jnp.where(place < classes, logits, -3.0e38)
    shifted = logits - jnp.max(logits, axis=0, keepdims=True)
    weights = jnp.exp(shifted)
    norm = jnp.sum(weights, axis=0, keepdims=True)
    onehot = place == label_ref[...].reshape(1, -1)
    picked = jnp.sum(jnp.where(onehot, shifted, 0.0), axis=0, keepdims=True)
    loss = jnp.sum(fold(keep * (jnp.log(norm) - picked)), axis=1, keepdims=True)
    grad = keep * (weights * (1.0 / norm) - jnp.where(onehot, 1.0, 0.0))
    grad_sum = fold(grad)
    grad_high, grad_low = split(pad_rows(grad, LANES))
    gcat = jnp.concatenate([grad_high, grad_low, grad_high], axis=0)
    owcat = jnp.concatenate([ow[0], ow[0], ow[1]], axis=1)

    def back(start):
        back_ref[:, start : start + CHUNK] = dot(owcat, gcat[:, start : start + CHUNK])

    for start in range(0, nodes, CHUNK):
        back(start)
    both = jnp.concatenate([grad_high, grad_low], axis=0)

    def weight_grad():
        value = dot_nt(both, high)
        value = value[:CLASS_ROWS] + value[LANES : LANES + CLASS_ROWS]
        misc_scr[:CLASS_ROWS, :] = value + dot_nt(grad_high[:CLASS_ROWS], low)

    def slab(r):
        rs = slice(r, r + rows)
        p, q = wide(col_ref[4, rs], nodes), wide(col_ref[5, rs], nodes)
        half, tangent, act_grad = half_ref[rs, :], tan_ref[rs, :], back_ref[rs, :]
        away = half * (1.0 - tangent)
        acc_ref[0, rs] = fold(act_grad * away)
        up = act_grad * (p + q * (tangent + away * (1.0 + tangent)))
        up_ref[rs, :] = up
        acc_ref[1, rs] = fold(up)
        acc_ref[2, rs] = fold(up * norm_ref[rs, :])

    slabs = [functools.partial(slab, r) for r in range(0, width, rows)]
    weave([weight_grad, lambda: None], slabs)
    put_rows(row_ref, total_row(acc_ref[1]), total_row(acc_ref[2]))
    sums_ref[...] = jnp.broadcast_to(row_ref[...][None], sums_ref.shape)
    misc_scr[CLASS_ROWS:, :] = jnp.zeros((HEAD_ROWS - CLASS_ROWS, width), f32)
    misc_scr[CLASS_ROWS : CLASS_ROWS + 1, :] = total_row(acc_ref[0])
    misc_scr[CLASS_ROWS + 1 : CLASS_ROWS + 2, :LANES] = total_row(pad_rows(grad_sum, LANES))
    misc_scr[CLASS_ROWS + 2 : CLASS_ROWS + 3, :1] = loss
    for t in range(tiles):
        misc_ref[t] = misc_scr[:, t * LANES : (t + 1) * LANES]


def mid_grad_kernel(
    code_ref, pay_ref, sums_ref, inv_ref, gain_ref, mask_ref, up_ref, norm_ref, act_hbm,
    out_ref, bg_ref, gcat,
    act, sems,
):
    width, nodes = up_ref.shape
    ready = act_in(1, code_ref, Copies(sems), act_hbm, act)
    tiles = width // LANES
    total = jnp.sum(real_nodes(pay_ref), axis=0, keepdims=True)
    bias_sum = jnp.sum(rows_of(sums_ref, 0, tiles), axis=0, keepdims=True)
    gain_sum = jnp.sum(rows_of(sums_ref, tiles, tiles), axis=0, keepdims=True)
    bg_ref[0:1, :] = bias_sum
    bg_ref[1:2, :] = gain_sum
    scale = as_column(gain_ref[...] * inv_ref[...])
    bias_col = as_column(bias_sum / total)
    gain_col = as_column(gain_sum / total)
    keep = mask_ref[...].reshape(1, -1).astype(f32)
    rows = 16
    for r in range(0, width, rows):
        rs = slice(r, r + rows)
        bias, gain = wide(bias_col[rs], nodes), wide(gain_col[rs], nodes)
        grad = up_ref[rs, :] - bias - norm_ref[rs, :] * gain
        high, low = split(keep * (wide(scale[rs], nodes) * grad))
        gcat[rs, :] = high
        gcat[width + r : width + r + rows, :] = low
    mid_product(code_ref, ready, act, gcat, out_ref)


def act_in(half_sel, code_ref, copies, act_hbm, act):
    parts, _, width, _ = act.shape
    rows = width // 2
    ready = []
    for s in range(parts):
        for r in (0, 1):
            block = (s * 2 + (half_sel ^ (code_ref[s] >> 4))) * 2 + r
            ready.append([
                copies.start(act_hbm.at[i, aligned(block, rows)], act.at[s, i, r * rows : (r + 1) * rows])
                for i in (0, 1)
            ])
    return ready


def mid_product(code_ref, ready, act, gcat, out_ref):
    parts, width, mid = out_ref.shape
    rows = width // PIECES
    size = width // 2
    for s in range(parts):
        code = code_ref[s] & (PIECES - 1)
        for r in (0, 1):
            for copy in ready[s * 2 + r]:
                copy.wait()
            here = slice(r * size, (r + 1) * size)
            high, low = act[s, 0, here, :], act[s, 1, here, :]
            value = dot_nt(
                jnp.concatenate([high, high, low], axis=1),
                jnp.concatenate([gcat[:mid, :], gcat[mid:, :], gcat[:mid, :]], axis=1),
            )
            for i in range(size // rows):
                place = (r * (size // rows) + i) ^ code
                out_ref[s, aligned(place, rows), :] = value[i * rows : (i + 1) * rows]


def mid_grad_rest_kernel(code_ref, gcat, act_hbm, out_ref, act, sems):
    ready = act_in(0, code_ref, Copies(sems), act_hbm, act)
    mid_product(code_ref, ready, act, gcat, out_ref)


def backward_kernel(
    code_ref, pay_ref, inv_ref, gain_ref, colpack_ref, w_ref, gram_ref, misc_ref,
    g, w2, pre_hbm, xcat_hbm,
    pack_ref, feat_hbm,
    pre, xcat, feat, col, down, ucat, acc, prod, rows_scr, shift_col, sems,
):
    copies = Copies(sems)
    hops, feats, width = w_ref.shape
    mid, nodes = g.shape[0] // 2, g.shape[1]
    tiles = mid // LANES
    size = 2 * CHUNK
    chunks = [slice(start, start + size) for start in range(0, nodes, size)]
    count = len(chunks)
    stages = [(h, j) for h in range(hops) for j in range(count)]
    z_in, x_in = {}, {}
    for h in range(hops):
        own = slice(h * width, (h + 1) * width)
        for j, c in enumerate(chunks):
            z_in[h, j] = copies.start(pre_hbm.at[own, c], pre.at[h, :, c])
        x_in[h] = copies.start(xcat_hbm.at[h], xcat.at[h])
    devices = pay_ref.shape[0]
    flip = code_ref[1] * (tiles // 2)
    at = hops * HOP_ROWS
    for t in range(tiles):
        pack_ref[t ^ flip, at : at + HEAD_ROWS, :] = misc_ref[t]
    w2cat, wcat = {}, {}

    def columns(h):
        rows = 64
        for r in range(0, width, rows):
            for k, values in enumerate(columns_of(colpack_ref[h, r : r + rows, :])):
                col[h % 2, k, r : r + rows, :] = values

    def weights(h):
        high, low = split(pad_rows(w_ref[h], LANES) * (gain_ref[h] * inv_ref[h]))
        wcat[h] = (jnp.concatenate([high, low], axis=0), high)
        high, low = split(0.5 * w2[h * width : (h + 1) * width, :])
        w2cat[h] = jnp.concatenate([high, high, low], axis=1)

    def part_of(j, part):
        return slice(chunks[j].start + part * CHUNK, chunks[j].start + (part + 1) * CHUNK)

    def down_product(index, part):
        h, j = stages[index]
        cs = part_of(j, part)
        high, low = g[:mid, cs], g[mid:, cs]
        value = dot(w2cat[h], jnp.concatenate([high, low, high], axis=0))
        down[index % 2, :, part * CHUNK : (part + 1) * CHUNK] = value

    def slab(index, r, rows):
        h, j = stages[index]
        two = h % 2
        rs, cs = slice(r, r + rows), chunks[j]
        scale, shift, p1, q1, p2, q2 = (wide(col[two, k, rs], size) for k in range(6))
        half1 = pre[h, rs, cs] * scale + shift
        grad2 = down[index % 2, rs, :]
        tan1 = jnp.tanh(half1)
        half2 = half1 * (p1 + q1 * tan1)
        tan2 = jnp.tanh(half2)
        away2 = half2 * (1.0 - tan2)
        add(acc, two, 0, rs, j, fold(grad2 * away2))
        grad1 = grad2 * (p2 + q2 * (tan2 + away2 * (1.0 + tan2)))
        away1 = half1 * (1.0 - tan1)
        add(acc, two, 1, rs, j, fold(grad1 * away1))
        grad = grad1 * (p1 + q1 * (tan1 + away1 * (1.0 + tan1)))
        high, low = split(grad)
        ucat[two, rs, cs] = high
        ucat[two, width + r : width + r + rows, cs] = low

    def add(acc, two, k, rs, j, value):
        acc[two, k, rs] = value if j == 0 else acc[two, k, rs] + value

    def feature_product(index, part):
        h, j = stages[index]
        cs = part_of(j, part)
        value = dot(wcat[h][0], ucat[h % 2, :width, cs])
        value = value[:LANES] + value[LANES:] + dot(wcat[h][1], ucat[h % 2, width:, cs])
        feat[h, :, cs] = value[:feats]

    def weight_product(h):
        value = dot_nt(xcat[h], ucat[h % 2, :width, :])
        low = dot_nt(xcat[h, :LANES, :], ucat[h % 2, width:, :])
        prod[h % 2] = value[:LANES] + value[LANES:] + low

    def shifts(h):
        shift = feature_shift(pay_ref, h)
        rows_scr[h, :devices, :] = shift
        rows_scr[h, devices:, :] = jnp.broadcast_to(real_nodes(pay_ref), shift.shape)
        own_shift = rows_scr[h, pl.ds(code_ref[0], 1), :]
        own_count = rows_scr[h, pl.ds(devices + code_ref[0], 1), :]
        shift_col[h] = as_column(own_shift)
        gram = gram_ref[h] + shift_col[h] * (own_shift * own_count)
        pack_ref[h ^ flip, at + HEAD_ROWS :, :] = gram[:HOP_ROWS]

    def slope_sums(h):
        return total_row(acc[h % 2, 1]), 2.0 * total_row(acc[h % 2, 0])

    def pack(h, sums=None):
        two = h % 2
        slope1_sum, slope2_sum = sums or slope_sums(h)
        bias_sum = prod[two, feats : feats + 1, :]
        prod[two] = prod[two] + wide(shift_col[h], mid) * bias_sum
        prod[two, feats + 1 : feats + 2, :] = slope1_sum
        prod[two, feats + 2 : feats + 3, :] = slope2_sum
        for t in range(tiles):
            pack_ref[t ^ flip, h * HOP_ROWS : (h + 1) * HOP_ROWS, :] = prod[
                two, :HOP_ROWS, t * LANES : (t + 1) * LANES
            ]

    rows = 16
    weights(0)
    weave(
        [functools.partial(down_product, 0, part) for part in (0, 1)],
        [functools.partial(columns, 0)] + [functools.partial(shifts, h) for h in range(hops)],
    )
    for index, (h, j) in enumerate(stages):
        products = []
        z_in[h, j].wait()
        if j + 1 == count:
            x_in[h].wait()
            if h + 1 < hops:
                weights(h + 1)
                columns(h + 1)
        if index + 1 < len(stages):
            products += [functools.partial(down_product, index + 1, part) for part in (0, 1)]
        if index >= 1:
            before = [functools.partial(feature_product, index - 1, part) for part in (0, 1)]
            products = before + products
        if j == 1 and h >= 1:
            products.append(functools.partial(weight_product, h - 1))
        slabs = [functools.partial(slab, index, r, rows) for r in range(0, width, rows)]
        if j == 2 and h >= 1:
            copies.send(feat.at[h - 1], feat_hbm.at[h - 1])
            slabs.insert(len(slabs) // 2, functools.partial(pack, h - 1))
        weave(products, slabs)
    for part in (0, 1):
        feature_product(len(stages) - 1, part)
    copies.send(feat.at[hops - 1], feat_hbm.at[hops - 1])
    sums = slope_sums(hops - 1)
    weight_product(hops - 1)
    pack(hops - 1, sums)
    copies.finish()


def finish_kernel(
    code_ref, pay_ref, inv_ref, mine_ref, other_ref, w_ref, gain_ref, mask_ref, bg_ref, xcat_hbm,
    feat_hbm, fgrad_hbm, wgrad_hbm, gain_out, bias_out, slope1_out, slope2_out, mgain_out, mbias_out, mslope_out,
    owg_out, obg_out, loss_out,
    sum_ref, rows_scr, fgrad, wgrad, feat, xcat, sems,
):
    hops, feats, width = w_ref.shape
    tiles = mine_ref.shape[0] * 2
    half = tiles // 2
    flip = code_ref[1]
    copies = Copies(sems)
    ready = []
    for h in range(hops):
        ready.append((copies.start(feat_hbm.at[h], feat.at[h]), copies.start(xcat_hbm.at[h], xcat.at[h])))

    @pl.when(flip == 0)
    def _():
        for t in range(half):
            sum_ref[:, t * LANES : (t + 1) * LANES] = mine_ref[t]
            sum_ref[:, (half + t) * LANES : (half + t + 1) * LANES] = other_ref[t]

    @pl.when(flip != 0)
    def _():
        for t in range(half):
            sum_ref[:, t * LANES : (t + 1) * LANES] = other_ref[t]
            sum_ref[:, (half + t) * LANES : (half + t + 1) * LANES] = mine_ref[t]

    counts = real_nodes(pay_ref)
    total = jnp.sum(counts, axis=0, keepdims=True)
    keep = mask_ref[...].reshape(1, -1).astype(f32)
    at = hops * HOP_ROWS
    for h in range(hops):
        base = h * HOP_ROWS
        w = pad_rows(w_ref[h], LANES)
        inverse = inv_ref[h]
        scale = gain_ref[h] * inverse
        bias_sum = sum_ref[base + feats : base + feats + 1, :]
        slope1_out[h] = sum_ref[base + feats + 1 : base + feats + 2, :]
        slope2_out[h] = sum_ref[base + feats + 2 : base + feats + 3, :]
        products = sum_ref[base : base + feats, :]
        gain_sum = inverse * jnp.sum(w_ref[h] * products, axis=0, keepdims=True)
        bias_out[h] = bias_sum
        gain_out[h] = gain_sum
        gram = sum_ref[at + HEAD_ROWS : at + HEAD_ROWS + HOP_ROWS, h * LANES : (h + 1) * LANES]
        inner = dot(gram, w, exact)[:feats] * (inverse * gain_sum / total)
        wgrad[h] = scale * (products - inner)
        copies.send(wgrad.at[h], wgrad_hbm.at[:, h, :])
        shift = feature_shift(pay_ref, h)
        rows_scr[...] = shift
        own_shift = rows_scr[pl.ds(code_ref[0], 1), :]
        mix = dot_nt(w * (scale * inverse * gain_sum / total), w, exact)
        lane = lax.broadcasted_iota(jnp.int32, (1, LANES), 1)
        off = jnp.sum(w * (scale * bias_sum / total), axis=1, keepdims=True)
        off = off + jnp.sum(mix * jnp.where(lane < feats, own_shift, 0.0), axis=1, keepdims=True)
        high, low = split(mix)
        for copy in ready[h]:
            copy.wait()
        mixed = dot(jnp.concatenate([high, high], axis=1), xcat[h]) + dot(low, xcat[h, :LANES])
        fgrad[h] = keep * (feat[h] - (mixed + off)[:feats])
        copies.send(fgrad.at[h], fgrad_hbm.at[:, h, :])
    owg_out[...] = sum_ref[at : at + owg_out.shape[0], :]
    mslope_out[...] = sum_ref[at + CLASS_ROWS : at + CLASS_ROWS + 1, :]
    obg_out[...] = sum_ref[at + CLASS_ROWS + 1 : at + CLASS_ROWS + 2, : obg_out.shape[1]]
    loss_out[...] = sum_ref[at + CLASS_ROWS + 2 : at + CLASS_ROWS + 3, :1] / total
    mbias_out[...] = bg_ref[0:1, :]
    mgain_out[...] = bg_ref[1:2, :]
    copies.finish()


def place_kernel(pieces, code_ref, *refs):
    out_ref, sems = refs[-2:]
    copies = Copies(sems)
    for ref, (s, first, rows) in zip(refs, pieces):
        for i in range(ref.shape[0] // rows):
            block = s * 2 * PIECES + ((first + i) ^ code_ref[s])
            copies.send(ref.at[pl.ds(i * rows, rows)], out_ref.at[aligned(block, rows)])
    copies.finish()


def exchange(values, bit, devices):
    return lax.ppermute(values, axes, [(i, i ^ (1 << bit)) for i in range(devices)])


def exchange_two(a, bit_a, b, bit_b, devices):
    a, b = lax.optimization_barrier((a, b))
    return lax.optimization_barrier((exchange(a, bit_a, devices), exchange(b, bit_b, devices)))


def swap_halves(a, bit_a, b, bit_b, devices):
    size = a.shape[0] // 2
    ra, rb = exchange_two(a[size:], bit_a, b[size:], bit_b, devices)
    return a[:size] + ra, b[:size] + rb


def code_of(me, order):
    code = 0
    for bit in order:
        code = code * 2 + ((me >> bit) & 1)
    return code


def after(values, *others):
    return lax.optimization_barrier((values, *others))[0]


def on_device(
    devices,
    hop_features,
    branch_weight,
    branch_gain,
    branch_bias,
    first_slope,
    second_slope,
    mid_weight,
    mid_gain,
    mid_bias,
    mid_slope,
    out_weight,
    out_bias,
    labels,
    valid_mask,
):
    hops, feats, nodes = hop_features.shape
    width = branch_weight.shape[2]
    mid = mid_weight.shape[1]
    classes = out_weight.shape[1]
    tiles = mid // LANES
    bits = devices.bit_length() - 1
    me = lax.axis_index(axes).astype(jnp.int32)
    rest = tuple(range(5, bits))
    codes = jnp.stack([code_of(me, (0, 1, 2, 3, 4)), code_of(me, (0, 2, 1, 3, 4))])
    place_code = jnp.stack([me, me & 1])
    shape = jax.ShapeDtypeStruct
    by_hop = lambda v: v.reshape(hops, 1, width)
    gain, bias, slope1, slope2 = map(by_hop, (branch_gain, branch_bias, first_slope, second_slope))
    row = lambda v: v.reshape(1, -1)
    gather = functools.partial(
        lax.all_to_all, axis_name=axes, split_axis=0, concat_axis=0, tiled=True
    )
    dma = pltpu.SemaphoreType.DMA
    scratch = lambda dtype, *dims: pltpu.VMEM(dims, dtype)
    mask = valid_mask

    pay, gram, xcat, w = call(
        stats_kernel,
        60,
        in_specs=[anywhere, anywhere, vmem],
        out_specs=[vmem, vmem, anywhere, anywhere],
        out_shape=(
            shape((devices, hops, width + LANES), f32), shape((hops, LANES, LANES), f32),
            shape((hops, 2 * LANES, nodes), bf16), shape((hops, feats, width), f32),
        ),
        scratch_shapes=[
            scratch(f32, hops, feats, nodes), scratch(f32, hops, feats, width),
            scratch(bf16, hops, 2 * LANES, nodes), scratch(f32, hops, width + LANES), dma((4 * hops,)),
        ],
        cost_estimate=cost(1_000_000_000, 8_000_000),
        name="first_stats",
    )(jnp.transpose(hop_features, (1, 0, 2)), jnp.transpose(branch_weight, (1, 0, 2)), mask)
    pay = gather(after(pay, codes, place_code))

    pre, w2cat = call(
        prepare_kernel,
        60,
        in_specs=[anywhere, vmem, anywhere],
        out_specs=[anywhere] * 2,
        out_shape=(shape((hops * width, nodes), f32), shape((hops, mid, 2 * width), bf16)),
        scratch_shapes=[
            scratch(bf16, hops, 2 * LANES, nodes), scratch(f32, hops, width, mid),
            scratch(f32, hops, width, nodes), scratch(bf16, hops, mid, 2 * width), dma((4 * hops,)),
        ],
        cost_estimate=cost(4 * 2 * 4 * hops * LANES * width * nodes, 20_000_000),
        name="prepare",
    )(xcat, w, mid_weight)

    mid_pre, stat, first_inv, colpack, act = call(
        forward_kernel,
        45,
        in_specs=[smem] + [vmem] * 7 + [anywhere] * 2,
        out_specs=[vmem] * 4 + [anywhere],
        out_shape=(
            shape((mid, nodes), f32), shape((devices, 8, LANES), f32), shape((hops, 1, width), f32),
            shape((hops, width, LANES), f32), shape((2, hops * width, nodes), bf16),
        ),
        scratch_shapes=[
            scratch(f32, hops, width, nodes), scratch(bf16, hops, mid, 2 * width),
            scratch(bf16, hops, 2, width, nodes), scratch(f32, hops, devices, width),
            scratch(f32, 8, LANES), dma((4 * hops,)),
        ],
        cost_estimate=cost(3 * 2 * hops * width * mid * nodes, 20_000_000),
        name="forward",
    )(place_code, pay, w, gain, bias, slope1, slope2, mask, pre, w2cat)
    stat = gather(stat)

    logits, mid_inv, sums, misc, up, normed = call(
        head_kernel,
        40,
        in_specs=[vmem] * 10,
        out_specs=[vmem] * 6,
        out_shape=(
            shape((classes, nodes), f32), shape((1, mid), f32), shape((devices, 8, LANES), f32),
            shape((tiles, HEAD_ROWS, LANES), f32), shape((mid, nodes), f32), shape((mid, nodes), f32),
        ),
        scratch_shapes=[
            scratch(f32, LANES, mid), scratch(f32, 1, LANES), scratch(f32, 8, LANES),
            scratch(f32, mid, nodes), scratch(f32, mid, nodes), scratch(bf16, 2 * mid, nodes),
            scratch(f32, 6, mid, LANES), scratch(f32, mid, nodes), scratch(f32, 3, mid, LANES),
            scratch(f32, HEAD_ROWS, mid),
        ],
        cost_estimate=cost(2_000_000_000, 10_000_000),
        name="head",
    )(pay, stat, row(mid_gain), row(mid_bias), row(mid_slope), out_weight.T, row(out_bias), labels, mask, mid_pre)
    sums = gather(sums)

    product_cost = cost(2 * 3 * 2 * width * mid * nodes, 10_000_000)
    send, mid_bg, gcat = call(
        mid_grad_kernel,
        36,
        in_specs=[smem] + [vmem] * 7 + [anywhere],
        out_specs=[vmem] * 3,
        out_shape=(
            shape((2, width, mid), f32), shape((2, mid), f32), shape((2 * mid, nodes), bf16),
        ),
        scratch_shapes=[scratch(bf16, 2, 2, width, nodes), dma((8,))],
        cost_estimate=product_cost,
        name="mid_grad_send",
    )(codes, pay, sums, mid_inv, row(mid_gain), mask, up, normed, act)
    came = exchange(send, 0, devices)
    kept = call(
        mid_grad_rest_kernel,
        40,
        in_specs=[smem, vmem, anywhere],
        out_specs=vmem,
        out_shape=shape((2, width, mid), f32),
        scratch_shapes=[scratch(bf16, 2, 2, width, nodes), dma((8,))],
        cost_estimate=product_cost,
        name="mid_grad_keep",
    )(codes, gcat, act)

    pack_rows = hops * HOP_ROWS + HEAD_ROWS + HOP_ROWS

    def backward(gcat):
        return call(
            backward_kernel,
            42,
            in_specs=[smem] + [vmem] * 9 + [anywhere] * 2,
            out_specs=[vmem, anywhere],
            scratch_shapes=[
                scratch(f32, hops, width, nodes), scratch(bf16, hops, 2 * LANES, nodes),
                scratch(f32, hops, feats, nodes), scratch(f32, 2, 6, width, LANES),
                scratch(f32, 2, width, 2 * CHUNK), scratch(bf16, 2, 2 * width, nodes),
                scratch(f32, 2, 2, width, LANES), scratch(f32, 2, LANES, mid),
                scratch(f32, hops, 2 * devices, LANES), scratch(f32, hops, LANES, LANES),
                dma((3 * hops + (hops + 1) * nodes // CHUNK,)),
            ],
            out_shape=(shape((tiles, pack_rows, LANES), f32), shape((hops, feats, nodes), f32)),
            cost_estimate=cost(hops * 2 * 4 * width * mid * nodes, 24_000_000),
            name="backward",
        )(place_code, pay, first_inv, gain, colpack, w, gram, misc, gcat, mid_weight, pre, xcat)

    a, b = kept[0] + came[0], kept[1] + came[1]
    size = a.shape[0] // 2
    send_a, send_b = a[size:], b[size:]
    ra = exchange(send_a, 1, devices)
    rb = exchange(send_b, 2, devices)
    pack, feat = backward(after(gcat, send_a, send_b))
    a, b = a[:size] + after(ra, pack), b[:size] + after(rb, pack)

    half = tiles // 2
    groups = {}
    for i in range(devices):
        groups.setdefault(i & ~14, []).append(i)
    spread = functools.partial(
        lax.all_to_all, axis_name=axes, split_axis=0, concat_axis=0,
        axis_index_groups=list(groups.values()), tiled=True,
    )
    pack = after(pack, a, b)
    pack = pack[:half] + exchange(pack[half:], 0, devices)
    a, b, pack = lax.optimization_barrier((a, b, pack))
    a, b = swap_halves(a, 2, b, 1, devices)
    pack = spread(pack.reshape(8, -1, LANES))
    part = a.shape[0] // 4
    both = jnp.stack([a.reshape(4, part, mid), b.reshape(4, part, mid)], axis=1)
    both = both[:2] + exchange(both[2:], 3, devices)
    pack = pack.sum(axis=0)
    pack, both = lax.optimization_barrier((pack, both))
    came, pack_came = lax.optimization_barrier(
        (exchange(both[1:], 4, devices), exchange(pack, 4, devices))
    )
    both, pack = both[:1] + came, pack + pack_came
    for bit in rest:
        both, pack = both + exchange(both, bit, devices), pack + exchange(pack, bit, devices)
    pack = jnp.broadcast_to(pack[None], (8,) + pack.shape)
    pack, both = lax.optimization_barrier((pack, both))
    pack = spread(pack).reshape(half, pack_rows, LANES)
    both = jnp.concatenate([both, exchange(both, 4, devices)])
    both = jnp.concatenate([both, exchange(both, 3, devices)])
    a, b = both[:, 0].reshape(-1, mid), both[:, 1].reshape(-1, mid)
    ra, rb = exchange_two(a, 2, b, 1, devices)
    a, b = jnp.concatenate([a, ra]), jnp.concatenate([b, rb])
    a, b = lax.optimization_barrier((a, b))
    ra, rb = exchange(a, 1, devices), exchange(b, 2, devices)
    other_a, other_b = exchange(a, 0, devices), exchange(b, 0, devices)
    pack_other = exchange(pack, 0, devices)

    rows_out = [shape((hops, 1, width), f32)] * 4
    rows_mid = [shape((1, mid), f32)] * 3
    (
        feature_grad, branch_weight_grad, branch_gain_grad, branch_bias_grad, first_slope_grad,
        second_slope_grad, mid_gain_grad, mid_bias_grad, mid_slope_grad, out_weight_grad,
        out_bias_grad, mean_loss,
    ) = call(
        finish_kernel,
        60,
        in_specs=[smem] + [vmem] * 8 + [anywhere] * 2,
        out_specs=[anywhere, anywhere] + [vmem] * 10,
        scratch_shapes=[
            scratch(f32, pack_rows, mid), scratch(f32, devices, LANES), scratch(f32, hops, feats, nodes),
            scratch(f32, hops, feats, width), scratch(f32, hops, feats, nodes),
            scratch(bf16, hops, 2 * LANES, nodes), dma((4 * hops,)),
        ],
        out_shape=(
            shape((feats, hops, nodes), f32), shape((feats, hops, width), f32), *rows_out, *rows_mid,
            shape((classes, mid), f32), shape((1, classes), f32), shape((1, 1), f32),
        ),
        cost_estimate=cost(0, 20_000_000),
        name="finish",
    )(place_code, pay, first_inv, pack, pack_other, w, gain, mask, mid_bg, xcat, feat)

    rows = mid_weight.shape[0] // (4 * PIECES)
    eight = PIECES // 2

    def place(pieces, *base):
        values = [value for value, *_ in pieces]
        kinds = [(s, first, rows) for _, s, first in pieces]
        return call(
            functools.partial(place_kernel, kinds),
            16,
            in_specs=[smem] + [vmem] * len(values) + [anywhere] * len(base),
            out_specs=anywhere,
            scratch_shapes=[dma((len(values) * eight,))],
            out_shape=shape(mid_weight.shape, f32),
            input_output_aliases={1 + len(values): 0} if base else {},
            cost_estimate=cost(0, 4_000_000),
            name="place",
        )(codes, *values, *base)

    grad = place(
        [(a, 0, 0), (b, 1, 0), (other_a, 0, PIECES), (after(other_b, mid_bias_grad), 1, PIECES)]
    )
    ra, rb, grad = lax.optimization_barrier((ra, rb, grad))
    other_ra, other_rb = exchange(ra, 0, devices), exchange(rb, 0, devices)
    grad = place([(ra, 0, eight), (rb, 1, eight)], grad)
    mid_weight_grad = place(
        [(other_ra, 0, PIECES + eight), (after(other_rb, grad), 1, PIECES + eight)], grad
    )

    flat = lambda v: v.reshape(-1)
    return (
        logits,
        mean_loss.reshape(()),
        jnp.transpose(feature_grad, (1, 0, 2)),
        jnp.transpose(branch_weight_grad, (1, 0, 2)),
        flat(branch_gain_grad),
        flat(branch_bias_grad),
        flat(first_slope_grad),
        flat(second_slope_grad),
        mid_weight_grad,
        flat(mid_gain_grad),
        flat(mid_bias_grad),
        flat(mid_slope_grad),
        out_weight_grad.T,
        flat(out_bias_grad),
    )


def solution(mesh):
    devices = mesh.shape["dp"] * mesh.shape["rep"]

    def body(*arrays):
        return on_device(devices, *arrays)

    nodes = P(("dp", "rep"))
    return jax.shard_map(
        body,
        mesh=mesh,
        in_specs=(P(None, None, ("dp", "rep")),) + (P(),) * 11 + (nodes, nodes),
        out_specs=(P(None, ("dp", "rep")), P(), P(None, None, ("dp", "rep"))) + (P(),) * 11,
        check_vma=False,
    )
```
